32 devices in a mesh: dp: 8 (over y, x, core), tensor: 4 (over z).
Axes of the slice: x: 2, y: 2, z: 4, core: 2. Of those that a mesh axis runs over, the one named last changes fastest.
Arguments:
- block_input: bfloat16 [512, 50, 512], P(('dp', 'tensor')), may hold values from -6 to 6
- position_kernel: bfloat16 [3, 3, 512], replicated, may hold values from -2 to 2
- position_bias: bfloat16 [512], replicated, may hold values from -1.75 to 1.75
- early_gain: bfloat16 [512], replicated, may hold values from 0.5 to 1.5
- early_shift: bfloat16 [512], replicated, may hold values from -1.25 to 1.25
- joint_weight: bfloat16 [512, 1536], replicated, may hold values from -0.375 to 0.375
- joint_bias: bfloat16 [1024], replicated, may hold values from -1.75 to 1.75
- small_kernel: bfloat16 [3, 3, 128], replicated, may hold values from -2 to 2
- small_bias: bfloat16 [128], replicated, may hold values from -1.75 to 1.75
- middle_kernel: bfloat16 [5, 5, 192], replicated, may hold values from -1.25 to 1.25
- middle_bias: bfloat16 [192], replicated, may hold values from -1.75 to 1.75
- large_kernel: bfloat16 [7, 7, 192], replicated, may hold values from -0.875 to 0.875
- large_bias: bfloat16 [192], replicated, may hold values from -1.75 to 1.75
- output_weight: bfloat16 [512, 512], P('tensor'), may hold values from -0.25 to 0.25
- output_bias: bfloat16 [512], replicated, may hold values from -1.25 to 1.25
- late_gain: bfloat16 [512], replicated, may hold values from 0.5 to 1.5
- late_shift: bfloat16 [512], replicated, may hold values from -1.25 to 1.25
- expand_weight: bfloat16 [512, 2048], P(None, 'tensor'), may hold values from -0.25 to 0.25
- expand_bias: bfloat16 [2048], P('tensor'), may hold values from -1.75 to 1.75
- reduce_weight: bfloat16 [2048, 512], P('tensor'), may hold values from -0.125 to 0.125
- reduce_bias: bfloat16 [512], replicated, may hold values from -1.25 to 1.25
- cotangent: bfloat16 [512, 50, 512], P(('dp', 'tensor')), may hold values from -6 to 6
Outputs:
- block_output: bfloat16 [512, 50, 512], P(('dp', 'tensor'))
- input_grad: bfloat16 [512, 50, 512], P(('dp', 'tensor'))
- grad_position_kernel: float32 [3, 3, 512], replicated
- grad_position_bias: float32 [512], replicated
- grad_early_gain: float32 [512], replicated
- grad_early_shift: float32 [512], replicated
- grad_joint_weight: float32 [512, 1536], replicated
- grad_joint_bias: float32 [1024], replicated
- grad_small_kernel: float32 [3, 3, 128], replicated
- grad_small_bias: float32 [128], replicated
- grad_middle_kernel: float32 [5, 5, 192], replicated
- grad_middle_bias: float32 [192], replicated
- grad_large_kernel: float32 [7, 7, 192], replicated
- grad_large_bias: float32 [192], replicated
- grad_output_weight: float32 [512, 512], P('tensor')
- grad_output_bias: float32 [512], replicated
- grad_late_gain: float32 [512], replicated
- grad_late_shift: float32 [512], replicated
- grad_expand_weight: float32 [512, 2048], P(None, 'tensor')
- grad_expand_bias: float32 [2048], P('tensor')
- grad_reduce_weight: float32 [2048, 512], P('tensor')
- grad_reduce_bias: float32 [512], replicated
The draws below stay inside these ranges and needn't reach their ends.
All inputs are finite; a program needn't handle non-finite values.
Results may differ from the reference program's by a relative error of at most 0.019.
Values may be sent and summed in bfloat16 or wider, within the bound.
A program may use at most 256 MiB of HBM per device.

```python
import math
import jax
import jax.numpy as jnp
from jax import lax

D = 512
HEADS = 8
HEAD = 64
FF = 2048
TOK = 50
GRID = 7
IMAGES = 512


def levels(stream_key, dims, cuts, smallest, top_value):
    factor_of, own = 1.0, jax.random.fold_in(stream_key, 6)
    for axis_at, parts in cuts:
        steps = jnp.exp(jax.random.uniform(jax.random.fold_in(own, axis_at), (parts,), jnp.float32, smallest / len(cuts), top_value / len(cuts)))
        factor_of = factor_of * jnp.repeat(steps, dims[axis_at] // parts).reshape([-1 if axis == axis_at else 1 for axis in range(len(dims))])
    return factor_of


def gaussian(key, dims, deviation, most, pieces=(), kind=jnp.bfloat16):
    values = deviation * jax.random.normal(key, dims, jnp.float32)
    if pieces:
        values = values * levels(key, dims, pieces, -0.22, 0.18)
    return jnp.clip(values, -most, most).astype(kind)


def setup_inputs(seed: int = 0) -> dict:
    arg_keys = jax.random.split(jax.random.key(seed), 23)
    block_input = gaussian(arg_keys[0], (IMAGES, TOK, D), 1.0, 6.0, ((0, 32),))
    position_kernel = gaussian(arg_keys[1], (3, 3, D), 9 ** -0.5, 2.0)
    position_bias = gaussian(arg_keys[2], (D,), 0.3, 1.75)
    early_gain = jnp.clip(1.0 + 0.1 * jax.random.normal(arg_keys[3], (D,), jnp.float32), 0.5, 1.5).astype(jnp.bfloat16)
    early_shift = gaussian(arg_keys[4], (D,), 0.2, 1.25)
    joint_weight = gaussian(arg_keys[5], (D, 3 * D), (D // 2) ** -0.5, 0.375)
    joint_bias = gaussian(arg_keys[6], (2 * D,), 0.3, 1.75)
    small_kernel = gaussian(arg_keys[7], (3, 3, 2 * HEAD), 9 ** -0.5, 2.0)
    small_bias = gaussian(arg_keys[8], (2 * HEAD,), 0.3, 1.75)
    middle_kernel = gaussian(arg_keys[9], (5, 5, 3 * HEAD), 25 ** -0.5, 1.25)
    middle_bias = gaussian(arg_keys[10], (3 * HEAD,), 0.3, 1.75)
    large_kernel = gaussian(arg_keys[11], (7, 7, 3 * HEAD), 49 ** -0.5, 0.875)
    large_bias = gaussian(arg_keys[12], (3 * HEAD,), 0.3, 1.75)
    output_weight = gaussian(arg_keys[13], (D, D), D ** -0.5, 0.25, ((0, 4),))
    output_bias = gaussian(arg_keys[14], (D,), 0.2, 1.25)
    late_gain = jnp.clip(1.0 + 0.1 * jax.random.normal(arg_keys[15], (D,), jnp.float32), 0.5, 1.5).astype(jnp.bfloat16)
    late_shift = gaussian(arg_keys[16], (D,), 0.2, 1.25)
    expand_weight = gaussian(arg_keys[17], (D, FF), D ** -0.5, 0.25, ((1, 4),))
    expand_bias = gaussian(arg_keys[18], (FF,), 0.3, 1.75, ((0, 4),))
    reduce_weight = gaussian(arg_keys[19], (FF, D), FF ** -0.5, 0.125, ((0, 4),))
    reduce_bias = gaussian(arg_keys[20], (D,), 0.2, 1.25)
    cotangent = gaussian(arg_keys[21], (IMAGES, TOK, D), 1.0, 6.0, ((0, 32),))
    return dict(block_input=block_input, position_kernel=position_kernel, position_bias=position_bias, early_gain=early_gain, early_shift=early_shift, joint_weight=joint_weight, joint_bias=joint_bias, small_kernel=small_kernel, small_bias=small_bias, middle_kernel=middle_kernel, middle_bias=middle_bias, large_kernel=large_kernel, large_bias=large_bias, output_weight=output_weight, output_bias=output_bias, late_gain=late_gain, late_shift=late_shift, expand_weight=expand_weight, expand_bias=expand_bias, reduce_weight=reduce_weight, reduce_bias=reduce_bias, cotangent=cotangent)


@jax.custom_vjp
def low(v):
    return lax.optimization_barrier(v.astype(jnp.bfloat16)).astype(jnp.float32)

@jax.custom_vjp
def low_back(v):
    return v

def low_keep(v):
    return (low(v), None)

def low_pass(kept, grad):
    return (grad,)

def back_keep(v):
    return (v, None)

def back_low(kept, grad):
    return (low(grad),)
low.defvjp(low_keep, low_pass)
low_back.defvjp(back_keep, back_low)
norm_eps = 1e-06
highest = lax.Precision.HIGHEST

def layer_norm(values_in, norm_gain, norm_shift):
    centre = lax.optimization_barrier(jnp.mean(values_in, axis=-1, keepdims=True))
    centred = values_in - centre
    spread = lax.optimization_barrier(jnp.mean(centred * centred, axis=-1, keepdims=True))
    return centred * lax.rsqrt(spread + norm_eps) * norm_gain + norm_shift

def depthwise(field, kernel):
    extent = kernel.shape[0]
    margin = extent // 2
    side_len = field.shape[1]
    padded = jnp.pad(field, ((0, 0), (margin, margin), (margin, margin), (0, 0)))
    result = jnp.zeros_like(field)
    for row_tap in range(extent):
        for col_tap in range(extent):
            result = result + padded[:, row_tap:row_tap + side_len, col_tap:col_tap + side_len, :] * kernel[row_tap, col_tap]
    return result

def full_kernel(small_kernel, middle_kernel, large_kernel):
    small_pad = jnp.pad(small_kernel, ((2, 2), (2, 2), (0, 0)))
    middle_pad = jnp.pad(middle_kernel, ((1, 1), (1, 1), (0, 0)))
    return jnp.concatenate([small_pad, middle_pad, large_kernel], axis=2)

def forward(block_input, position_kernel, position_bias, early_gain, early_shift, joint_weight, joint_bias, small_kernel, small_bias, middle_kernel, middle_bias, large_kernel, large_bias, output_weight, output_bias, late_gain, late_shift, expand_weight, expand_bias, reduce_weight, reduce_bias):
    image_count = block_input.shape[0]
    grid_in = block_input[:, 1:].reshape(image_count, GRID, GRID, D)
    mixed_grid = grid_in + depthwise(grid_in, position_kernel) + position_bias
    first_sum = jnp.concatenate([block_input[:, :1], mixed_grid.reshape(image_count, GRID * GRID, D)], axis=1)
    normed_one = low(layer_norm(first_sum, early_gain, early_shift))
    projected = jnp.einsum('bnd,de->bne', normed_one, joint_weight, precision=highest)
    query = low_back(low(projected[..., :D] + joint_bias[:D]))
    keys = low_back(low(projected[..., D:2 * D]))
    values = low_back(low(projected[..., 2 * D:] + joint_bias[D:]))
    head_shape = (image_count, TOK, HEADS, HEAD)
    query_heads = query.reshape(head_shape)
    key_heads = keys.reshape(head_shape)
    value_heads = values.reshape(head_shape)
    key_soft = low(jax.nn.softmax(key_heads, axis=1))
    context = low_back(low(jnp.einsum('bnhk,bnhv->bhkv', key_soft, value_heads, precision=highest)))
    factor = jnp.einsum('bnhk,bhkv->bnhv', query_heads, context, precision=highest) * HEAD ** (-0.5)
    kernel_all = full_kernel(small_kernel, middle_kernel, large_kernel)
    bias_all = jnp.concatenate([small_bias, middle_bias, large_bias])
    value_grid = values[:, 1:].reshape(image_count, GRID, GRID, D)
    conv_grid = (depthwise(value_grid, kernel_all) + bias_all).reshape(image_count, GRID * GRID, D)
    relative = query[:, 1:] * conv_grid
    relative = jnp.concatenate([jnp.zeros((image_count, 1, D), query.dtype), relative], axis=1)
    attention = low_back(low(factor.reshape(image_count, TOK, D) + relative))
    branch_out = jnp.einsum('bnd,de->bne', attention, output_weight, precision=highest) + output_bias
    second_sum = first_sum + low_back(branch_out)
    normed_two = low(layer_norm(second_sum, late_gain, late_shift))
    pre_gelu = low_back(jnp.einsum('bnd,df->bnf', normed_two, expand_weight, precision=highest) + expand_bias)
    hidden = low(jax.nn.gelu(pre_gelu, approximate=False))
    return second_sum + jnp.einsum('bnf,fd->bnd', hidden, reduce_weight, precision=highest) + reduce_bias

def reference(block_input, position_kernel, position_bias, early_gain, early_shift, joint_weight, joint_bias, small_kernel, small_bias, middle_kernel, middle_bias, large_kernel, large_bias, output_weight, output_bias, late_gain, late_shift, expand_weight, expand_bias, reduce_weight, reduce_bias, cotangent):
    weights = tuple((weight.astype(jnp.float32) for weight in (position_kernel, position_bias, early_gain, early_shift, joint_weight, joint_bias, small_kernel, small_bias, middle_kernel, middle_bias, large_kernel, large_bias, output_weight, output_bias, late_gain, late_shift, expand_weight, expand_bias, reduce_weight, reduce_bias)))
    block_images = math.gcd(IMAGES, 64)
    block_count = IMAGES // block_images
    input_blocks = block_input.astype(jnp.float32).reshape(block_count, block_images, TOK, D)
    grad_blocks = cotangent.astype(jnp.float32).reshape(block_count, block_images, TOK, D)

    def one_block(totals, block_pair):
        inputs_here, grads_here = block_pair
        result, pullback = jax.vjp(forward, inputs_here, *weights)
        gradients = pullback(grads_here)
        totals = tuple((total + gradient for total, gradient in zip(totals, gradients[1:])))
        return (totals, (result.astype(jnp.bfloat16), gradients[0].astype(jnp.bfloat16)))
    starting = tuple((jnp.zeros_like(weight) for weight in weights))
    totals, (outputs, input_grads) = lax.scan(one_block, starting, (input_blocks, grad_blocks))
    full_shape = (IMAGES, TOK, D)
    return (outputs.reshape(full_shape), input_grads.reshape(full_shape), totals[0], totals[1], totals[2], totals[3], totals[4], totals[5], totals[6], totals[7], totals[8], totals[9], totals[10], totals[11], totals[12], totals[13], totals[14], totals[15], totals[16], totals[17], totals[18], totals[19])
```

```python
from functools import partial

import jax
import jax.numpy as jnp
from jax import lax
from jax.sharding import PartitionSpec as P

HEADS = 8
HEAD = 64
GRID = 7


norm_eps = 1e-06


def layer_norm(values_in, norm_gain, norm_shift):
    centre = jnp.mean(values_in, axis=-1, keepdims=True)
    centred = values_in - centre
    spread = jnp.mean(centred * centred, axis=-1, keepdims=True)
    return centred * lax.rsqrt(spread + norm_eps) * norm_gain + norm_shift


def depthwise(field, kernel):
    extent = kernel.shape[0]
    margin = extent // 2
    side_len = field.shape[1]
    padded = jnp.pad(field, ((0, 0), (margin, margin), (margin, margin), (0, 0)))
    result = jnp.zeros_like(field)
    for row_tap in range(extent):
        for col_tap in range(extent):
            result = (
                result
                + padded[:, row_tap : row_tap + side_len, col_tap : col_tap + side_len, :]
                * kernel[row_tap, col_tap]
            )
    return result


def full_kernel(small_kernel, middle_kernel, large_kernel):
    small_pad = jnp.pad(small_kernel, ((2, 2), (2, 2), (0, 0)))
    middle_pad = jnp.pad(middle_kernel, ((1, 1), (1, 1), (0, 0)))
    return jnp.concatenate([small_pad, middle_pad, large_kernel], axis=2)


def position_mix(field, kernel, bias_vec):
    return field + depthwise(field, kernel) + bias_vec


def per_device(
    block_input,
    position_kernel,
    position_bias,
    early_gain,
    early_shift,
    joint_weight,
    joint_bias,
    small_kernel,
    small_bias,
    middle_kernel,
    middle_bias,
    large_kernel,
    large_bias,
    output_weight,
    output_bias,
    late_gain,
    late_shift,
    expand_weight,
    expand_bias,
    reduce_weight,
    reduce_bias,
    cotangent,
):
    f32 = jnp.float32
    bf16 = jnp.bfloat16
    image_count, token_count, model_width = block_input.shape
    row_count = image_count * token_count
    part_count = 1
    head_width = model_width // part_count
    heads_here = HEADS // part_count
    first_chan = 0
    head_scale = HEAD ** (-0.5)
    grid_cells = GRID * GRID
    output_weight = lax.all_gather(output_weight, "tensor", axis=0, tiled=True)
    expand_weight = lax.all_gather(expand_weight, "tensor", axis=1, tiled=True)
    expand_bias = lax.all_gather(expand_bias, "tensor", axis=0, tiled=True)
    reduce_weight = lax.all_gather(reduce_weight, "tensor", axis=0, tiled=True)
    inputs_f = block_input.astype(f32)
    grid_in = inputs_f[:, 1:].reshape(image_count, GRID, GRID, model_width)
    mixed_grid, pull_position = jax.vjp(
        position_mix, grid_in, position_kernel.astype(f32), position_bias.astype(f32)
    )
    first_sum = jnp.concatenate(
        [inputs_f[:, :1], mixed_grid.reshape(image_count, grid_cells, model_width)], axis=1
    )
    first_sum = first_sum.reshape(row_count, model_width)
    normed_f, pull_early = jax.vjp(
        layer_norm, first_sum, early_gain.astype(f32), early_shift.astype(f32)
    )
    normed_one = normed_f.astype(bf16)
    projected = jnp.dot(normed_one, joint_weight, preferred_element_type=f32)
    joint_f = joint_bias.astype(f32)
    img_shape = (image_count, token_count, model_width)
    query_img = (projected[:, :model_width] + joint_f[:model_width]).astype(bf16).reshape(img_shape)
    key_img = projected[:, model_width : 2 * model_width].astype(bf16).reshape(img_shape)
    value_img = (
        (projected[:, 2 * model_width :] + joint_f[model_width:]).astype(bf16).reshape(img_shape)
    )
    query_loc, key_loc, value_loc = (
        query_img,
        key_img,
        value_img,
    )
    group_size = query_loc.shape[0]
    head_shape = (group_size, token_count, heads_here, HEAD)
    query_split = query_loc.reshape(head_shape)
    key_split = key_loc.reshape(head_shape)
    value_split = value_loc.reshape(head_shape)
    key_soft = jax.nn.softmax(key_split.astype(f32), axis=1)
    key_soft_low = key_soft.astype(bf16)
    context = jnp.einsum(
        "bnhk,bnhv->bhkv", key_soft_low, value_split, preferred_element_type=f32
    ).astype(bf16)
    factor = (
        jnp.einsum("bnhk,bhkv->bnhv", query_split, context, preferred_element_type=f32) * head_scale
    )

    def relative_term(
        query_grid, value_grid, small_w, small_b, middle_w, middle_b, large_w, large_b
    ):
        kernel_mine = lax.dynamic_slice_in_dim(
            full_kernel(small_w, middle_w, large_w), first_chan, head_width, 2
        )
        bias_mine = lax.dynamic_slice_in_dim(
            jnp.concatenate([small_b, middle_b, large_b]), first_chan, head_width, 0
        )
        conv_grid = depthwise(value_grid, kernel_mine) + bias_mine
        return query_grid * conv_grid.reshape(query_grid.shape)

    query_grid = query_loc[:, 1:].astype(f32)
    value_grid = value_loc[:, 1:].astype(f32).reshape(group_size, GRID, GRID, head_width)
    relative, pull_relative = jax.vjp(
        relative_term,
        query_grid,
        value_grid,
        small_kernel.astype(f32),
        small_bias.astype(f32),
        middle_kernel.astype(f32),
        middle_bias.astype(f32),
        large_kernel.astype(f32),
        large_bias.astype(f32),
    )
    zero_row = jnp.zeros((group_size, 1, head_width), f32)
    attention = (
        factor.reshape(group_size, token_count, head_width)
        + jnp.concatenate([zero_row, relative], axis=1)
    ).astype(bf16)
    attention_flat = attention.reshape(group_size * token_count, head_width)
    branch_out = jnp.dot(attention_flat, output_weight, preferred_element_type=f32)
    second_sum = first_sum + branch_out + output_bias.astype(f32)
    normed_two_f, pull_late = jax.vjp(
        layer_norm, second_sum, late_gain.astype(f32), late_shift.astype(f32)
    )
    normed_two = normed_two_f.astype(bf16)
    exact_gelu = partial(jax.nn.gelu, approximate=False)
    grad_flat = cotangent.reshape(row_count, model_width)
    normed_group = normed_two
    pre_gelu = jnp.dot(
        normed_group, expand_weight, preferred_element_type=f32
    ) + expand_bias.astype(f32)
    activated, pull_gelu = jax.vjp(exact_gelu, pre_gelu)
    hidden_low = activated.astype(bf16)
    feed_out = jnp.dot(
            hidden_low,
            reduce_weight,
            preferred_element_type=f32)
    block_output = (second_sum + feed_out + reduce_bias.astype(f32)).astype(bf16).reshape(img_shape)
    grad_out_f = grad_flat.astype(f32)
    grad_reduce_bias = jnp.sum(grad_out_f, axis=0)
    grad_group = grad_flat
    grad_reduce_weight = jnp.dot(hidden_low.T, grad_group, preferred_element_type=f32)
    grad_hidden = jnp.dot(grad_group, reduce_weight.T, preferred_element_type=f32)
    grad_pre = pull_gelu(grad_hidden)[0].astype(bf16)
    grad_expand_bias = jnp.sum(grad_pre.astype(f32), axis=0)
    grad_expand_weight = jnp.dot(normed_group.T, grad_pre, preferred_element_type=f32)
    grad_normed_two = jnp.dot(grad_pre, expand_weight.T, preferred_element_type=f32)
    grad_second_norm, grad_late_gain, grad_late_shift = pull_late(grad_normed_two)
    grad_second = grad_out_f + grad_second_norm
    grad_branch = grad_second.astype(bf16)
    grad_output_bias = jnp.sum(grad_branch.astype(f32), axis=0)
    branch_group = grad_branch
    grad_output_weight = jnp.dot(attention_flat.T, branch_group, preferred_element_type=f32)
    grad_attention = jnp.dot(branch_group, output_weight.T, preferred_element_type=f32).astype(bf16)
    grad_attention = grad_attention.reshape(group_size, token_count, head_width)
    grad_att_split = grad_attention.reshape(head_shape)
    grad_query_ctx = (
        jnp.einsum("bnhv,bhkv->bnhk", grad_att_split, context, preferred_element_type=f32)
        * head_scale
    )
    grad_context = (
        jnp.einsum("bnhk,bnhv->bhkv", query_split, grad_att_split, preferred_element_type=f32)
        * head_scale
    ).astype(bf16)
    grad_key_soft = jnp.einsum(
        "bnhv,bhkv->bnhk", value_split, grad_context, preferred_element_type=f32
    )
    grad_value_ctx = jnp.einsum(
        "bnhk,bhkv->bnhv", key_soft_low, grad_context, preferred_element_type=f32
    )
    grad_key_split = key_soft * (
        grad_key_soft - jnp.sum(grad_key_soft * key_soft, axis=1, keepdims=True)
    )
    (
        grad_query_grid,
        grad_value_grid,
        grad_small_kernel,
        grad_small_bias,
        grad_middle_kernel,
        grad_middle_bias,
        grad_large_kernel,
        grad_large_bias,
    ) = pull_relative(grad_attention[:, 1:].astype(f32))
    loc_shape = (group_size, token_count, head_width)
    grad_query_loc = (
        grad_query_ctx.reshape(loc_shape) + jnp.concatenate([zero_row, grad_query_grid], axis=1)
    ).astype(bf16)
    grad_key_loc = grad_key_split.reshape(loc_shape).astype(bf16)
    grad_value_loc = (
        grad_value_ctx.reshape(loc_shape)
        + jnp.concatenate(
            [zero_row, grad_value_grid.reshape(group_size, grid_cells, head_width)], axis=1
        )
    ).astype(bf16)
    grad_query_img, grad_key_img, grad_value_img = (
        grad_query_loc,
        grad_key_loc,
        grad_value_loc,
    )
    grad_projected = jnp.concatenate(
        [grad_query_img, grad_key_img, grad_value_img], axis=2
    ).reshape(row_count, 3 * model_width)
    grad_joint_weight = jnp.dot(normed_one.T, grad_projected, preferred_element_type=f32)
    grad_joint_bias = jnp.concatenate(
        [
            jnp.sum(grad_query_img.astype(f32), axis=(0, 1)),
            jnp.sum(grad_value_img.astype(f32), axis=(0, 1)),
        ]
    )
    grad_normed_one = jnp.dot(grad_projected, joint_weight.T, preferred_element_type=f32)
    grad_first_norm, grad_early_gain, grad_early_shift = pull_early(grad_normed_one)
    grad_first = (grad_second + grad_first_norm).reshape(img_shape)
    grad_grid, grad_position_kernel, grad_position_bias = pull_position(
        grad_first[:, 1:].reshape(image_count, GRID, GRID, model_width)
    )
    input_grad = jnp.concatenate(
        [grad_first[:, :1], grad_grid.reshape(image_count, grid_cells, model_width)], axis=1
    ).astype(bf16)
    (
        grad_position_kernel,
        grad_position_bias,
        grad_early_gain,
        grad_early_shift,
        grad_joint_weight,
        grad_joint_bias,
        grad_small_kernel,
        grad_small_bias,
        grad_middle_kernel,
        grad_middle_bias,
        grad_large_kernel,
        grad_large_bias,
        grad_output_bias,
        grad_late_gain,
        grad_late_shift,
        grad_reduce_bias,
    ) = lax.psum(
        (
            grad_position_kernel,
            grad_position_bias,
            grad_early_gain,
            grad_early_shift,
            grad_joint_weight,
            grad_joint_bias,
            grad_small_kernel,
            grad_small_bias,
            grad_middle_kernel,
            grad_middle_bias,
            grad_large_kernel,
            grad_large_bias,
            grad_output_bias,
            grad_late_gain,
            grad_late_shift,
            grad_reduce_bias,
        ),
        ("dp", "tensor"),
    )
    grad_output_weight, grad_expand_weight, grad_expand_bias, grad_reduce_weight = (
        lax.psum(
            lax.psum_scatter(part.astype(bf16), "tensor", scatter_dimension=axis, tiled=True), "dp"
        ).astype(f32)
        for part, axis in (
            (grad_output_weight, 0),
            (grad_expand_weight, 1),
            (grad_expand_bias, 0),
            (grad_reduce_weight, 0),
        )
    )
    return (
        block_output,
        input_grad,
        grad_position_kernel,
        grad_position_bias,
        grad_early_gain,
        grad_early_shift,
        grad_joint_weight,
        grad_joint_bias,
        grad_small_kernel,
        grad_small_bias,
        grad_middle_kernel,
        grad_middle_bias,
        grad_large_kernel,
        grad_large_bias,
        grad_output_weight,
        grad_output_bias,
        grad_late_gain,
        grad_late_shift,
        grad_expand_weight,
        grad_expand_bias,
        grad_reduce_weight,
        grad_reduce_bias,
    )


def solution(mesh):
    in_specs = (
        P(("dp", "tensor"), None, None),
        P(),
        P(),
        P(),
        P(),
        P(),
        P(),
        P(),
        P(),
        P(),
        P(),
        P(),
        P(),
        P("tensor", None),
        P(),
        P(),
        P(),
        P(None, "tensor"),
        P("tensor"),
        P("tensor", None),
        P(),
        P(("dp", "tensor"), None, None),
    )
    out_specs = (
        P(("dp", "tensor"), None, None),
        P(("dp", "tensor"), None, None),
        P(),
        P(),
        P(),
        P(),
        P(),
        P(),
        P(),
        P(),
        P(),
        P(),
        P(),
        P(),
        P("tensor", None),
        P(),
        P(),
        P(),
        P(None, "tensor"),
        P("tensor"),
        P("tensor", None),
        P(),
    )
    return jax.shard_map(
        per_device, mesh=mesh, in_specs=in_specs, out_specs=out_specs, check_vma=False
    )
```

```python
from functools import partial

import jax
import jax.numpy as jnp
from jax import lax
from jax.experimental import pallas as pl
from jax.experimental.pallas import tpu as pltpu
from jax.sharding import PartitionSpec as P

HEADS = 8
HEAD = 64
GRID = 7
CELLS = GRID * GRID
NORM_EPS = 1e-06
SCALE = HEAD**-0.5
LANES = 128
GROUP = 256
PAD_TOK = 64
VMEM_BYTES = 56 * 1024 * 1024

f32 = jnp.float32
bf16 = jnp.bfloat16

ROW_POS_BIAS, ROW_EARLY_GAIN, ROW_EARLY_SHIFT, ROW_BIAS_Q, ROW_BIAS_V = 0, 1, 2, 3, 4
ROW_BIAS_ALL, ROW_OUT_BIAS, ROW_LATE_GAIN, ROW_LATE_SHIFT, ROW_REDUCE_BIAS = 5, 6, 7, 8, 9
ROW_POS_KERNEL, ROW_KERNEL_ALL = 10, 19
PARAM_ROWS = 72

OUT_POS_KERNEL, OUT_KERNEL_ALL = 0, 9
OUT_POS_BIAS, OUT_EARLY_GAIN, OUT_EARLY_SHIFT, OUT_BIAS_Q, OUT_BIAS_V, OUT_BIAS_ALL = 58, 59, 60, 61, 62, 63
SMALL_ROWS = 64
LATE_GAIN, LATE_SHIFT, LATE_OUT_BIAS, LATE_REDUCE_BIAS, LATE_EXPAND_BIAS = 0, 1, 2, 3, 4


def lane(tile):
    if isinstance(tile, int):
        return slice(tile * LANES, (tile + 1) * LANES)
    return pl.ds(pl.multiple_of(tile * LANES, LANES), LANES)


def taps(extent):
    return range(extent)


def columns(shift):
    return range(max(0, -shift), min(GRID, GRID - shift))


def depthwise_rows(get_row, get_weight, extent, flip, emit):
    margin = extent // 2
    for i in range(GRID):
        total = [None] * GRID
        for a in range(extent):
            r = i + a - margin
            if not 0 <= r < GRID:
                continue
            row = get_row(r)
            for b in range(extent):
                weight = get_weight((extent - 1 - a, extent - 1 - b) if flip else (a, b))
                for j in columns(b - margin):
                    term = row[j + b - margin] * weight
                    total[j] = term if total[j] is None else total[j] + term
        emit(i, total)


def kernel_grads(get_left, get_right, extent, emit):
    margin = extent // 2
    for a in range(extent):
        total = [None] * extent
        for i in range(GRID):
            r = i + a - margin
            if not 0 <= r < GRID:
                continue
            left, right = get_left(i), get_right(r)
            for b in range(extent):
                for j in columns(b - margin):
                    term = left[j] * right[j + b - margin]
                    total[b] = term if total[b] is None else total[b] + term
        for b in range(extent):
            emit(a, b, total[b])


def cell_rows(images, cell, count=1):
    return slice((1 + cell) * images, (1 + cell + count) * images)


def grid_row(ref, tile, images, i):
    block = ref[tile, cell_rows(images, i * GRID, GRID), :]
    return [block[j * images : (j + 1) * images] for j in range(GRID)]


def full_tap(extent, a, b):
    extra = (GRID - extent) // 2
    return ROW_KERNEL_ALL + (a + extra) * GRID + b + extra


def tile_extents(body):
    body(0, 3)
    body(1, 5)

    def rest(tile, carry):
        body(tile, 7)
        return carry

    lax.fori_loop(2, 4, rest, 0)


def normalise(block, gain, shift):
    centre = jnp.mean(block, axis=-1, keepdims=True)
    centred = block - centre
    spread = jnp.mean(centred * centred, axis=-1, keepdims=True)
    scale = lax.rsqrt(spread + NORM_EPS)
    return centred * scale, scale


def normalise_back(grad, gain, unit, scale):
    scaled = grad * gain
    mean_one = jnp.mean(scaled, axis=-1, keepdims=True)
    mean_two = jnp.mean(scaled * unit, axis=-1, keepdims=True)
    return (scaled - mean_one - unit * mean_two) * scale


def fold_rows(block):
    return jnp.sum(block.reshape(block.shape[0] // 8, 8, block.shape[1]), axis=0)


def dot(left, right, left_dim=1, right_dim=0):
    return lax.dot_general(
        left, right, (((left_dim,), (right_dim,)), ((), ())), preferred_element_type=f32
    )


def head_of(rows, columns_):
    return lax.broadcasted_iota(jnp.int32, (rows, columns_), 1) // HEAD


def to_tokens(images, tokens, source, target):
    for tile in range(4):
        for b in range(images):
            target[tile, pl.ds(b, tokens, stride=images), :] = source(b, tile)


def compact_context(full):
    heads = head_of(HEAD, GROUP)
    total = jnp.zeros((HEAD, GROUP), f32)
    for h in range(GROUP // HEAD):
        total = jnp.where(heads == h, full[h * HEAD : (h + 1) * HEAD, :], total)
    return total.astype(bf16)


def spread_context(compact):
    heads = head_of(HEAD, GROUP)
    wide = compact.astype(f32)
    return jnp.concatenate(
        [jnp.where(heads == h, wide, 0.0).astype(bf16) for h in range(GROUP // HEAD)], axis=0
    )


def attention_forward(
    images, tokens, x_ref, prm_ref, wj_ref,
    xt_ref, x1_ref, h1_ref, q_ref, v_ref, ks_ref, conv_ref, qi_ref, ki_ref, vi_ref, ctx_ref, att_ref,
    fac_ref,
):
    rows = images * tokens
    prm = lambda row, tile: prm_ref[row : row + 1, lane(tile)]
    to_tokens(images, tokens, lambda b, t: x_ref[b, :, lane(t)].astype(f32), xt_ref)

    def position(tile, carry):
        x1_ref[0:images, lane(tile)] = xt_ref[tile, 0:images, :]
        bias = prm(ROW_POS_BIAS, tile)

        def emit(i, total):
            own = grid_row(xt_ref, tile, images, i)
            for j in range(GRID):
                x1_ref[cell_rows(images, i * GRID + j), lane(tile)] = own[j] + total[j] + bias

        depthwise_rows(
            lambda r: grid_row(xt_ref, tile, images, r),
            lambda ab: prm(ROW_POS_KERNEL + ab[0] * 3 + ab[1], tile),
            3, False, emit,
        )
        return carry

    lax.fori_loop(0, 4, position, 0)
    gain = prm_ref[ROW_EARLY_GAIN : ROW_EARLY_GAIN + 1, :]
    shift = prm_ref[ROW_EARLY_SHIFT : ROW_EARLY_SHIFT + 1, :]
    step = 80

    def norm(k, carry):
        at = pl.ds(pl.multiple_of(k * step, step), step)
        unit, _ = normalise(x1_ref[at, :], gain, shift)
        h1_ref[at, :] = (unit * gain + shift).astype(bf16)
        return carry

    lax.fori_loop(0, rows // step, norm, 0)

    width = 4 * LANES
    query = (dot(h1_ref[...], wj_ref[:, :width]) + prm_ref[ROW_BIAS_Q : ROW_BIAS_Q + 1, :]).astype(bf16).astype(f32)
    for tile in range(4):
        q_ref[tile] = query[:, lane(tile)]
    value = (dot(h1_ref[...], wj_ref[:, 2 * width :]) + prm_ref[ROW_BIAS_V : ROW_BIAS_V + 1, :]).astype(bf16).astype(f32)
    for tile in range(4):
        v_ref[tile] = value[:, lane(tile)]
    keys = dot(h1_ref[...], wj_ref[:, width : 2 * width]).astype(bf16).astype(f32)
    for tile in range(4):
        ks_ref[tile] = keys[:, lane(tile)]

    def soften(tile, carry):
        at = lambda n: slice(n * images, (n + 1) * images)
        top = ks_ref[tile, at(0), :]
        for n in range(1, tokens):
            top = jnp.maximum(top, ks_ref[tile, at(n), :])
        total = jnp.zeros_like(top)
        for n in range(tokens):
            e = jnp.exp(ks_ref[tile, at(n), :] - top)
            ks_ref[tile, at(n), :] = e
            total = total + e
        scale = 1.0 / total
        for n in range(tokens):
            ks_ref[tile, at(n), :] = ks_ref[tile, at(n), :] * scale
        return carry

    lax.fori_loop(0, 4, soften, 0)

    def relative(tile, extent):
        conv_ref[tile, 0:images, :] = jnp.zeros((images, LANES), f32)
        bias = prm(ROW_BIAS_ALL, tile)

        def emit(i, total):
            for j in range(GRID):
                conv_ref[tile, cell_rows(images, i * GRID + j), :] = total[j] + bias

        depthwise_rows(
            lambda r: grid_row(v_ref, tile, images, r),
            lambda ab: prm(full_tap(extent, *ab), tile),
            extent, False, emit,
        )

    tile_extents(relative)

    def image(b, carry):
        for source, target in ((q_ref, qi_ref), (ks_ref, ki_ref), (v_ref, vi_ref)):
            target[b, 48:PAD_TOK, :] = jnp.zeros((PAD_TOK - 48, width), bf16)
            for tile in range(4):
                target[b, 0:tokens, lane(tile)] = source[tile, pl.ds(b, tokens, stride=images), :].astype(bf16)
        for g in range(2):
            at = slice(g * GROUP, (g + 1) * GROUP)
            compact = compact_context(dot(ki_ref[b, :, at], vi_ref[b, :, at], 0, 0))
            ctx_ref[b, :, at] = compact
            out = dot(qi_ref[b, :, at], spread_context(compact)) * SCALE
            for t in range(2):
                fac_ref[2 * g + t, pl.ds(b, tokens, stride=images), :] = out[0:tokens, lane(t)]
        return carry

    lax.fori_loop(0, images, image, 0)

    def combine(tile, carry):
        att_ref[:, lane(tile)] = (fac_ref[tile] + q_ref[tile] * conv_ref[tile]).astype(bf16)
        return carry

    lax.fori_loop(0, 4, combine, 0)


def feed_forward(
    images, tokens, chunks, att_ref, x1_ref, prm_ref, eb_ref, wo_ref, we_ref, wr_ref, cot_ref,
    y_ref, dx2_ref, gwo_ref, gwe_ref, gwr_ref, late_ref, datt_ref,
    ct_ref, cb_ref, x2_ref, h2_ref, acc_ref, dh2_ref, hid_ref, dpre_ref,
):
    rows = images * tokens
    row = lambda r: prm_ref[r : r + 1, :]
    to_tokens(images, tokens, lambda b, t: cot_ref[b, :, lane(t)].astype(f32), ct_ref)
    for tile in range(4):
        cb_ref[:, lane(tile)] = ct_ref[tile].astype(bf16)
    step = 80
    gain, shift = row(ROW_LATE_GAIN), row(ROW_LATE_SHIFT)
    x2_ref[...] = x1_ref[...] + dot(att_ref[...], wo_ref[...]) + row(ROW_OUT_BIAS)

    def norm(k, carry):
        at = pl.ds(pl.multiple_of(k * step, step), step)
        unit, _ = normalise(x2_ref[at, :], gain, shift)
        h2_ref[at, :] = (unit * gain + shift).astype(bf16)
        return carry

    lax.fori_loop(0, rows // step, norm, 0)
    acc_ref[...] = jnp.zeros_like(acc_ref)
    dh2_ref[...] = jnp.zeros_like(dh2_ref)
    half = rows // 2
    cw = we_ref.shape[2]

    def chunk(c, carry):
        bias = eb_ref[c]
        folded = jnp.zeros((8, cw), f32)
        for k in range(2):
            at = slice(k * half, (k + 1) * half)
            pre = dot(h2_ref[at, :], we_ref[c]) + bias
            dh = dot(cb_ref[at, :], wr_ref[c], 1, 1)
            gauss = jnp.exp(pre * pre * -0.5)
            t = 1.0 / (1.0 + (0.3275911 * 0.7071067811865476) * jnp.abs(pre))
            poly = t * (0.127414796 + t * (-0.142248368 + t * (0.7107068705 + t * (-0.7265760135 + t * 0.5307027145))))
            tail = poly * gauss
            cdf = jnp.where(pre >= 0, 1.0 - tail, tail)
            hid_ref[at, :] = (pre * cdf).astype(bf16)
            dpre = ((cdf + pre * gauss * 0.3989422804014327) * dh).astype(bf16)
            dpre_ref[at, :] = dpre
            folded = folded + fold_rows(dpre.astype(f32))
        late_ref[c + LATE_EXPAND_BIAS, :, 0:cw] = folded
        acc_ref[...] += dot(hid_ref[...], wr_ref[c])
        gwr_ref[c] = dot(hid_ref[...], cb_ref[...], 0, 0).astype(bf16)
        gwe_ref[c] = dot(h2_ref[...], dpre_ref[...], 0, 0).astype(bf16)
        dh2_ref[...] += dot(dpre_ref[...], we_ref[c], 1, 1)
        return carry

    lax.fori_loop(0, chunks, chunk, 0)

    def finish(k, carry):
        at = pl.ds(pl.multiple_of(k * step, step), step)
        x2 = x2_ref[at, :]
        out = x2 + acc_ref[at, :] + row(ROW_REDUCE_BIAS)
        unit, scale = normalise(x2, gain, shift)
        grad = dh2_ref[at, :]
        dy = cb_ref[at, :].astype(f32)
        dx2 = dy + normalise_back(grad, gain, unit, scale)
        dx2_ref[at, :] = dx2
        low = dx2.astype(bf16)
        dh2_ref[at, :] = low.astype(f32)
        for tile in range(4):
            ct_ref[tile, at, :] = out[:, lane(tile)]
        late = carry
        return (
            late[0] + fold_rows(grad * unit),
            late[1] + fold_rows(grad),
            late[2] + fold_rows(low.astype(f32)),
            late[3] + fold_rows(dy),
        )

    zero = jnp.zeros((8, 4 * LANES), f32)
    sums = lax.fori_loop(0, rows // step, finish, (zero,) * 4)
    for r, total in enumerate(sums):
        late_ref[r] = total
    for b in range(images):
        for tile in range(4):
            y_ref[b, :, lane(tile)] = ct_ref[tile, pl.ds(b, tokens, stride=images), :].astype(bf16)
    branch = dh2_ref[...].astype(bf16)
    gwo_ref[...] = dot(att_ref[...], branch, 0, 0).astype(bf16)
    datt_ref[...] = dot(branch, wo_ref[...], 1, 1).astype(bf16)


def attention_backward(
    images, tokens, datt_ref, dx2_ref, x1_ref, h1_ref, xt_ref, q_ref, v_ref, ks_ref, conv_ref,
    qi_ref, ki_ref, vi_ref, ctx_ref, prm_ref, wj_ref,
    gwj_ref, small_ref, dx_ref,
    da_ref, dai_ref, dc_ref, dq_ref, dk_ref, dv_ref, raw_ref, dx1_ref,
):
    rows = images * tokens
    width = 4 * LANES
    prm = lambda r, tile: prm_ref[r : r + 1, lane(tile)]
    small_ref[...] = jnp.zeros_like(small_ref)
    for tile in range(4):
        da_ref[tile] = datt_ref[:, lane(tile)].astype(f32)

    def image(b, carry):
        dai_ref[b, 48:PAD_TOK, :] = jnp.zeros((PAD_TOK - 48, width), bf16)
        for tile in range(4):
            dai_ref[b, 0:tokens, lane(tile)] = da_ref[tile, pl.ds(b, tokens, stride=images), :].astype(bf16)
        for g in range(2):
            at = slice(g * GROUP, (g + 1) * GROUP)
            grad = dai_ref[b, :, at]
            ctx = spread_context(ctx_ref[b, :, at])
            dctx = spread_context(compact_context(dot(qi_ref[b, :, at], grad, 0, 0) * SCALE))
            dq = dot(grad, ctx, 1, 1) * SCALE
            dk = dot(vi_ref[b, :, at], dctx, 1, 1)
            dv = dot(ki_ref[b, :, at], dctx)
            for t in range(2):
                here = pl.ds(b, tokens, stride=images)
                dq_ref[2 * g + t, here, :] = dq[0:tokens, lane(t)]
                dk_ref[2 * g + t, here, :] = dk[0:tokens, lane(t)]
                dv_ref[2 * g + t, here, :] = dv[0:tokens, lane(t)]
        return carry

    lax.fori_loop(0, images, image, 0)

    def relative(tile, extent):
        at = lambda n: slice(n * images, (n + 1) * images)
        bias_q = jnp.zeros((images, LANES), f32)
        bias_all = jnp.zeros((images, LANES), f32)
        dot_sum = jnp.zeros((images, LANES), f32)
        for n in range(tokens):
            grad = da_ref[tile, at(n), :]
            dq = (dq_ref[tile, at(n), :] + grad * conv_ref[tile, at(n), :]).astype(bf16)
            raw_ref[at(n), lane(tile)] = dq
            bias_q = bias_q + dq.astype(f32)
            dc = grad * q_ref[tile, at(n), :]
            dc_ref[tile, at(n), :] = dc
            if n > 0:
                bias_all = bias_all + dc
            dot_sum = dot_sum + dk_ref[tile, at(n), :] * ks_ref[tile, at(n), :]
        for n in range(tokens):
            soft = ks_ref[tile, at(n), :]
            raw_ref[at(n), lane(tile + 4)] = (soft * (dk_ref[tile, at(n), :] - dot_sum)).astype(bf16)
        small_ref[OUT_BIAS_Q, :, lane(tile)] = fold_rows(bias_q)
        small_ref[OUT_BIAS_ALL, :, lane(tile)] = fold_rows(bias_all)
        first = dv_ref[tile, at(0), :].astype(bf16)
        raw_ref[at(0), lane(tile + 8)] = first
        sums = [first.astype(f32)]

        def emit(i, total):
            for j in range(GRID):
                here = cell_rows(images, i * GRID + j)
                dv = (dv_ref[tile, here, :] + total[j]).astype(bf16)
                raw_ref[here, lane(tile + 8)] = dv
                sums[0] = sums[0] + dv.astype(f32)

        depthwise_rows(
            lambda r: grid_row(dc_ref, tile, images, r),
            lambda ab: prm(full_tap(extent, *ab), tile),
            extent, True, emit,
        )
        small_ref[OUT_BIAS_V, :, lane(tile)] = fold_rows(sums[0])
        extra = (GRID - extent) // 2

        def emit_tap(a, b, total):
            small_ref[OUT_KERNEL_ALL + (a + extra) * GRID + b + extra, :, lane(tile)] = fold_rows(total)

        kernel_grads(
            lambda i: grid_row(dc_ref, tile, images, i),
            lambda r: grid_row(v_ref, tile, images, r),
            extent, emit_tap,
        )

    tile_extents(relative)

    for part in range(3):
        at = slice(part * width, (part + 1) * width)
        gwj_ref[:, at] = dot(h1_ref[...], raw_ref[:, at], 0, 0).astype(bf16)
    dx1_ref[...] = dot(raw_ref[...], wj_ref[...], 1, 1)
    gain = prm_ref[ROW_EARLY_GAIN : ROW_EARLY_GAIN + 1, :]
    shift = prm_ref[ROW_EARLY_SHIFT : ROW_EARLY_SHIFT + 1, :]
    step = 80

    def back(k, carry):
        at = pl.ds(pl.multiple_of(k * step, step), step)
        grad = dx1_ref[at, :]
        unit, scale = normalise(x1_ref[at, :], gain, shift)
        total = dx2_ref[at, :] + normalise_back(grad, gain, unit, scale)
        for tile in range(4):
            da_ref[tile, at, :] = total[:, lane(tile)]
        return carry[0] + fold_rows(grad * unit), carry[1] + fold_rows(grad)

    zero = jnp.zeros((8, width), f32)
    sums = lax.fori_loop(0, rows // step, back, (zero, zero))
    small_ref[OUT_EARLY_GAIN] = sums[0]
    small_ref[OUT_EARLY_SHIFT] = sums[1]

    def position(tile, carry):
        bias = [jnp.zeros((images, LANES), f32)]
        dc_ref[tile, 0:images, :] = da_ref[tile, 0:images, :]

        def emit(i, total):
            own = grid_row(da_ref, tile, images, i)
            for j in range(GRID):
                dc_ref[tile, cell_rows(images, i * GRID + j), :] = own[j] + total[j]
                bias[0] = bias[0] + own[j]

        depthwise_rows(
            lambda r: grid_row(da_ref, tile, images, r),
            lambda ab: prm(ROW_POS_KERNEL + ab[0] * 3 + ab[1], tile),
            3, True, emit,
        )
        small_ref[OUT_POS_BIAS, :, lane(tile)] = fold_rows(bias[0])

        def emit_tap(a, b, total):
            small_ref[OUT_POS_KERNEL + a * 3 + b, :, lane(tile)] = fold_rows(total)

        kernel_grads(
            lambda i: grid_row(da_ref, tile, images, i),
            lambda r: grid_row(xt_ref, tile, images, r),
            3, emit_tap,
        )
        return carry

    lax.fori_loop(0, 4, position, 0)
    for b in range(images):
        for tile in range(4):
            dx_ref[b, :, lane(tile)] = dc_ref[tile, pl.ds(b, tokens, stride=images), :].astype(bf16)


def call(kernel, outs, scratch):
    return pl.pallas_call(
        kernel,
        out_shape=[jax.ShapeDtypeStruct(shape, dtype) for shape, dtype in outs],
        scratch_shapes=[pltpu.VMEM(shape, dtype) for shape, dtype in scratch],
        compiler_params=pltpu.CompilerParams(vmem_limit_bytes=VMEM_BYTES),
    )


def pack_params(position_kernel, position_bias, early_gain, early_shift, joint_bias, small_kernel, small_bias,
                middle_kernel, middle_bias, large_kernel, large_bias, output_bias, late_gain, late_shift, reduce_bias):
    width = position_bias.shape[0]
    kernel_all = jnp.concatenate(
        [
            jnp.pad(small_kernel, ((2, 2), (2, 2), (0, 0))),
            jnp.pad(middle_kernel, ((1, 1), (1, 1), (0, 0))),
            large_kernel,
        ],
        axis=2,
    ).reshape(CELLS, width)
    return jnp.concatenate(
        [
            position_bias[None], early_gain[None], early_shift[None], joint_bias.reshape(2, width),
            jnp.concatenate([small_bias, middle_bias, large_bias])[None],
            output_bias[None], late_gain[None], late_shift[None], reduce_bias[None],
            position_kernel.reshape(9, width), kernel_all,
            jnp.zeros((PARAM_ROWS - ROW_KERNEL_ALL - CELLS, width), bf16),
        ],
        axis=0,
    ).astype(f32)


def block(block_input, params, joint_weight, output_weight, expand_weight, expand_bias, reduce_weight, cotangent):
    images, tokens, width = block_input.shape
    rows = images * tokens
    chunks, _, cw = expand_weight.shape
    tiled = ((4, rows, LANES), f32)
    flat = ((rows, width), f32)
    low = ((rows, width), bf16)
    per_image = ((images, PAD_TOK, width), bf16)
    xt, x1, h1, q, v, ks, conv, qi, ki, vi, ctx, att = call(
        partial(attention_forward, images, tokens),
        [tiled, flat, low, tiled, tiled, tiled, tiled, per_image, per_image, per_image,
         ((images, HEAD, width), bf16), low],
        [tiled],
    )(block_input, params, joint_weight)
    y, dx2, gwo, gwe, gwr, late, datt = call(
        partial(feed_forward, images, tokens, chunks),
        [((images, tokens, width), bf16), flat, ((width, width), bf16), ((chunks, width, cw), bf16),
         ((chunks, cw, width), bf16), ((LATE_EXPAND_BIAS + chunks, 8, width), f32), low],
        [tiled, low, flat, low, flat, flat, ((rows, cw), bf16), ((rows, cw), bf16)],
    )(att, x1, params, expand_bias, output_weight, expand_weight, reduce_weight, cotangent)
    gwj, small, dx = call(
        partial(attention_backward, images, tokens),
        [((width, 3 * width), bf16), ((SMALL_ROWS, 8, width), f32), ((images, tokens, width), bf16)],
        [tiled, per_image, tiled, tiled, tiled, tiled, ((rows, 3 * width), bf16), flat],
    )(datt, dx2, x1, h1, xt, q, v, ks, conv, qi, ki, vi, ctx, params, joint_weight)
    return y, dx, gwj, gwo, gwe, gwr, jnp.sum(small, axis=1), jnp.sum(late, axis=1)


def per_device(
    block_input, position_kernel, position_bias, early_gain, early_shift, joint_weight, joint_bias,
    small_kernel, small_bias, middle_kernel, middle_bias, large_kernel, large_bias,
    output_weight, output_bias, late_gain, late_shift, expand_weight, expand_bias,
    reduce_weight, reduce_bias, cotangent,
):
    width = block_input.shape[2]
    parts = lax.axis_size("tensor")
    params = pack_params(
        position_kernel, position_bias, early_gain, early_shift, joint_bias, small_kernel, small_bias,
        middle_kernel, middle_bias, large_kernel, large_bias, output_bias, late_gain, late_shift, reduce_bias,
    )
    whole_out = lax.all_gather(output_weight, "tensor", axis=0, tiled=True)
    whole_expand = lax.all_gather(expand_weight, "tensor")
    whole_bias = lax.all_gather(expand_bias, "tensor").astype(f32)[:, None, :]
    whole_reduce = lax.all_gather(reduce_weight, "tensor")
    y, dx, gwj, gwo, gwe, gwr, small, late = block(
        block_input, params, joint_weight, whole_out, whole_expand, whole_bias, whole_reduce, cotangent
    )
    gwo, gwe, gwr = (
        lax.psum(lax.psum_scatter(part, "tensor", scatter_dimension=0, tiled=True), "dp").astype(f32)
        for part in (gwo, gwe.reshape(-1, gwe.shape[2]), gwr.reshape(-1, width))
    )
    gwj, small, late = lax.psum((gwj.astype(f32), small, late), ("dp", "tensor"))
    g_bias = lax.dynamic_slice_in_dim(late, LATE_EXPAND_BIAS + lax.axis_index("tensor"), 1, 0)
    g_bias = g_bias[0, : expand_bias.shape[0]]
    return unpack(y, dx, gwj, gwo, gwe, gwr, small, late, g_bias, small_kernel, middle_kernel)


def unpack(y, dx, gwj, gwo, gwe, gwr, small, late, g_bias, small_kernel, middle_kernel):
    width = small.shape[1]
    kernel_all = small[OUT_KERNEL_ALL : OUT_KERNEL_ALL + CELLS].reshape(GRID, GRID, width)
    bias_all = small[OUT_BIAS_ALL]
    one = small_kernel.shape[2]
    two = one + middle_kernel.shape[2]
    return (
        y, dx, small[OUT_POS_KERNEL : OUT_POS_KERNEL + 9].reshape(3, 3, width),
        small[OUT_POS_BIAS], small[OUT_EARLY_GAIN], small[OUT_EARLY_SHIFT], gwj,
        small[OUT_BIAS_Q : OUT_BIAS_V + 1].reshape(-1),
        kernel_all[2:5, 2:5, :one], bias_all[:one], kernel_all[1:6, 1:6, one:two], bias_all[one:two],
        kernel_all[:, :, two:], bias_all[two:],
        gwo, late[LATE_OUT_BIAS], late[LATE_GAIN], late[LATE_SHIFT], gwe, g_bias, gwr, late[LATE_REDUCE_BIAS],
    )


def solution(mesh):
    images = P(("dp", "tensor"), None, None)
    in_specs = (images,) + (P(),) * 12 + (
        P("tensor", None), P(), P(), P(), P(None, "tensor"), P("tensor"), P("tensor", None), P(), images,
    )
    out_specs = (images, images) + (P(),) * 12 + (
        P("tensor", None), P(), P(), P(), P(None, "tensor"), P("tensor"), P("tensor", None), P(),
    )
    return jax.shard_map(per_device, mesh=mesh, in_specs=in_specs, out_specs=out_specs, check_vma=False)
```

```python
import math
from functools import partial

import jax
import jax.numpy as jnp
from jax import lax
from jax.experimental import pallas as pl
from jax.experimental.pallas import tpu as pltpu
from jax.sharding import PartitionSpec as P

HEADS = 8
HEAD = 64
GRID = 7
CELLS = GRID * GRID
NORM_EPS = 1e-06
SCALE = HEAD**-0.5
LANES = 128
GROUP = 256
PAD_TOK = 64
VMEM_BYTES = 62 * 1024 * 1024

f32 = jnp.float32
bf16 = jnp.bfloat16

ROW_POS_BIAS, ROW_EARLY_GAIN, ROW_EARLY_SHIFT, ROW_BIAS_Q, ROW_BIAS_V = 0, 1, 2, 3, 4
ROW_BIAS_ALL, ROW_OUT_BIAS, ROW_LATE_GAIN, ROW_LATE_SHIFT, ROW_REDUCE_BIAS = 5, 6, 7, 8, 9
ROW_POS_KERNEL, ROW_KERNEL_ALL = 10, 19
PARAM_ROWS = 72

OUT_POS_KERNEL, OUT_KERNEL_ALL = 0, 9
OUT_POS_BIAS, OUT_EARLY_GAIN, OUT_EARLY_SHIFT, OUT_BIAS_Q, OUT_BIAS_V, OUT_BIAS_ALL = 58, 59, 60, 61, 62, 63
OUT_LATE_GAIN, OUT_LATE_SHIFT, OUT_OUT_BIAS, OUT_REDUCE_BIAS, OUT_EXPAND_BIAS = 64, 65, 66, 67, 68
MESH = pl.DeviceIdType.MESH


def lane(tile):
    if isinstance(tile, int):
        return slice(tile * LANES, (tile + 1) * LANES)
    return pl.ds(pl.multiple_of(tile * LANES, LANES), LANES)


def taps(extent):
    return range(extent)


def columns(shift):
    return range(max(0, -shift), min(GRID, GRID - shift))


def depthwise_rows(get_row, get_weight, extent, flip, emit):
    margin = extent // 2
    for i in range(GRID):
        total = [None] * GRID
        for a in range(extent):
            r = i + a - margin
            if not 0 <= r < GRID:
                continue
            row = get_row(r)
            for b in range(extent):
                weight = get_weight((extent - 1 - a, extent - 1 - b) if flip else (a, b))
                for j in columns(b - margin):
                    term = row[j + b - margin] * weight
                    total[j] = term if total[j] is None else total[j] + term
        emit(i, total)


def kernel_grads(get_left, get_right, extent, emit):
    margin = extent // 2
    for a in range(extent):
        total = [None] * extent
        for i in range(GRID):
            r = i + a - margin
            if not 0 <= r < GRID:
                continue
            left, right = get_left(i), get_right(r)
            for b in range(extent):
                for j in columns(b - margin):
                    term = left[j] * right[j + b - margin]
                    total[b] = term if total[b] is None else total[b] + term
        for b in range(extent):
            emit(a, b, total[b])


def cell_rows(images, cell, count=1):
    return slice((1 + cell) * images, (1 + cell + count) * images)


def grid_row(ref, tile, images, i):
    block = ref[tile, cell_rows(images, i * GRID, GRID), :]
    return [block[j * images : (j + 1) * images] for j in range(GRID)]


def full_tap(extent, a, b):
    extra = (GRID - extent) // 2
    return ROW_KERNEL_ALL + (a + extra) * GRID + b + extra


def tile_extents(body):
    body(0, 3)
    body(1, 5)

    def rest(tile, carry):
        body(tile, 7)
        return carry

    lax.fori_loop(2, 4, rest, 0)


def normalise(block):
    centre = jnp.mean(block, axis=-1, keepdims=True)
    centred = block - centre
    spread = jnp.mean(centred * centred, axis=-1, keepdims=True)
    scale = lax.rsqrt(spread + NORM_EPS)
    return centred * scale, scale


def normalise_back(grad, gain, unit, scale):
    scaled = grad * gain
    mean_one = jnp.mean(scaled, axis=-1, keepdims=True)
    mean_two = jnp.mean(scaled * unit, axis=-1, keepdims=True)
    return (scaled - mean_one - unit * mean_two) * scale


def fold_rows(block):
    return jnp.sum(block.reshape(block.shape[0] // 8, 8, block.shape[1]), axis=0)


def dot(left, right, left_dim=1, right_dim=0):
    return lax.dot_general(
        left, right, (((left_dim,), (right_dim,)), ((), ())), preferred_element_type=f32
    )


def head_of(rows, columns_):
    return lax.broadcasted_iota(jnp.int32, (rows, columns_), 1) // HEAD


def compact_context(full):
    heads = head_of(HEAD, GROUP)
    total = jnp.zeros((HEAD, GROUP), f32)
    for h in range(GROUP // HEAD):
        total = jnp.where(heads == h, full[h * HEAD : (h + 1) * HEAD, :], total)
    return total.astype(bf16)


def spread_context(compact):
    heads = head_of(HEAD, GROUP)
    wide = compact.astype(f32)
    return jnp.concatenate(
        [jnp.where(heads == h, wide, 0.0).astype(bf16) for h in range(GROUP // HEAD)], axis=0
    )


def padded(count, unit):
    return -(-count // unit) * unit


class Ring:
    def __init__(self, pairs, depth, send_sems, recv_sems):
        self.dp = lax.axis_index("dp")
        self.me = lax.axis_index("tensor")
        self.planes, self.depth = pairs, depth
        group = 2 * pairs
        self.base = lax.div(self.dp, group) * group
        self.core = lax.rem(self.dp, 2)
        self.spot = lax.div(lax.rem(self.dp, group), 2)
        self.send_sems, self.recv_sems, self.used = send_sems, recv_sems, 0
        self.sent = []

    def twin(self):
        return {"dp": self.base + self.spot * 2 + (1 - self.core), "tensor": self.me}

    def plane(self, k):
        return {"dp": self.base + lax.rem(self.spot + k, self.planes) * 2 + self.core, "tensor": self.me}

    def plane_spot(self, k):
        return lax.rem(self.spot + k, self.planes)

    def stack(self, k):
        return {"dp": self.dp, "tensor": lax.rem(self.me + k, self.depth)}

    def everyone(self):
        return (
            [self.twin()]
            + [self.plane(k) for k in range(1, self.planes)]
            + [self.stack(k) for k in range(1, self.depth)]
        )

    def piece(self, rows, spot, core=None):
        each = rows // (2 * self.planes)
        core = self.core if core is None else core
        return pl.ds(pl.multiple_of((core * self.planes + spot) * each, each), each)

    def half(self, rows, core):
        return pl.ds(pl.multiple_of(core * (rows // 2), rows // 2), rows // 2)

    def send(self, source, target, device):
        at = self.used
        self.used += 1
        copy = pltpu.make_async_remote_copy(
            src_ref=source, dst_ref=target, send_sem=self.send_sems.at[at], recv_sem=self.recv_sems.at[at],
            device_id=device, device_id_type=MESH,
        )
        copy.start()
        self.sent.append(copy)
        return copy


def arrive(copies):
    for copy in copies:
        copy.wait_recv()


class Reduction:
    def __init__(self, ring, grads, twin_box, plane_box, stack_box, out, whole, relative):
        self.ring, self.grads, self.out, self.whole, self.relative = ring, grads, out, whole, relative
        self.twin_box, self.plane_box, self.stack_box = twin_box, plane_box, stack_box
        self.rows = grads.shape[1]
        self.depth = grads.shape[0]
        self.pairs, self.planes = {}, {}
        self.all = slice(0, self.depth)

    def slot(self, k):
        return k if self.relative else lax.rem(self.ring.me + k, self.depth)

    def pair(self, part):
        ring = self.ring
        away = ring.half(self.rows, 1 - ring.core)
        self.pairs[str(part)] = ring.send(self.grads.at[part, away], self.twin_box.at[part], ring.twin())

    def plane(self, part):
        ring = self.ring
        arrive([self.pairs[str(part)]])
        mine = ring.half(self.rows, ring.core)
        self.grads[part, mine] = (
            self.grads[part, mine].astype(f32) + self.twin_box[part].astype(f32)
        ).astype(bf16)
        self.planes[str(part)] = [
            ring.send(
                self.grads.at[part, ring.piece(self.rows, ring.plane_spot(k))],
                self.plane_box.at[k - 1, part], ring.plane(k),
            )
            for k in range(1, ring.planes)
        ]

    def gather_plane(self, part):
        ring = self.ring
        arrive(self.planes[str(part)])
        mine = ring.piece(self.rows, ring.spot)
        total = self.grads[part, mine].astype(f32)
        for k in range(1, ring.planes):
            total = total + self.plane_box[k - 1, part].astype(f32)
        self.grads[part, mine] = total.astype(bf16)

    def stack(self):
        ring = self.ring
        mine = ring.piece(self.rows, ring.spot)
        self.stacks = [
            ring.send(self.grads.at[self.slot(k), mine], self.stack_box.at[k - 1], ring.stack(k))
            for k in range(1, self.depth)
        ]

    def settle(self):
        ring = self.ring
        arrive(self.stacks)
        mine = ring.piece(self.rows, ring.spot)
        total = self.grads[self.slot(0), mine].astype(f32)
        for k in range(1, self.depth):
            total = total + self.stack_box[k - 1].astype(f32)
        done = total.astype(bf16)
        if self.whole:
            self.out[ring.me, mine] = done
            place = self.out.at[ring.me, mine]
            self.spread = [ring.send(place, place, ring.stack(k)) for k in range(1, self.depth)]
        else:
            self.out[mine] = done
            self.to_plane()

    def to_plane(self):
        ring = self.ring
        mine = ring.piece(self.rows, ring.spot)
        if self.whole:
            arrive(self.spread)
            place = self.out.at[:, mine]
        else:
            place = self.out.at[mine]
        self.back = [ring.send(place, place, ring.plane(k)) for k in range(1, ring.planes)]

    def to_twin(self):
        ring = self.ring
        arrive(self.back)
        mine = ring.half(self.rows, ring.core)
        place = self.out.at[:, mine] if self.whole else self.out.at[mine]
        self.last = ring.send(place, place, ring.twin())

    def finish(self):
        arrive([self.last])


class Gather:
    def __init__(self, ring, shard, box, relative):
        self.ring, self.box, self.relative = ring, box, relative
        self.depth, self.rows = box.shape[0], box.shape[1]
        mine = ring.piece(self.rows, ring.spot)
        self.first = [
            ring.send(
                shard.at[mine], box.at[(self.depth - k) if relative else ring.me, mine], ring.stack(k)
            )
            for k in range(1, self.depth)
        ]

    def places(self, rows):
        if self.relative:
            return [self.box.at[1 : self.depth, rows]]
        return [self.box.at[lax.rem(self.ring.me + k, self.depth), rows] for k in range(1, self.depth)]

    def plane(self):
        ring = self.ring
        arrive(self.first)
        mine = ring.piece(self.rows, ring.spot)
        self.second = [
            ring.send(place, place, ring.plane(k))
            for k in range(1, ring.planes) for place in self.places(mine)
        ]

    def pair(self):
        ring = self.ring
        arrive(self.second)
        self.third = [
            ring.send(place, place, ring.twin()) for place in self.places(ring.half(self.rows, ring.core))
        ]

    def finish(self):
        arrive(self.third)


def wide(ref, at):
    return jnp.concatenate([ref[tile, at, :] for tile in range(4)], axis=1)


def put_wide(ref, at, block):
    for tile in range(4):
        ref[tile, at, :] = block[:, lane(tile)]


def whole_block(
    images, tokens, planes, depth,
    x_ref, cot_ref, prm_ref, wj_ref, wo_shard, we_shard, wr_shard, eb_shard,
    y_ref, dx_ref, gwo_ref, gwe_ref, gwr_ref, gwj_ref, gsm_ref,
    x1_ref, x2_ref, q_ref, v_ref, ks_ref, conv_ref, fac_ref, dc_ref, one_ref, two_ref, three_ref,
    h1_ref, att_ref, h2_ref, raw_ref,
    qi_ref, ki_ref, vi_ref, dai_ref, ctx_ref, sums_ref,
    wo_ref, we_ref, wr_ref, eb_ref,
    go_ref, ge_ref, gr_ref, gj_ref, gs_ref,
    to_ref, te_ref, tr_ref, tj_ref, ts_ref,
    po_ref, pe_ref, pr_ref, pj_ref, ps_ref,
    so_ref, se_ref, sr_ref, sj_ref, ss_ref,
    send_sems, recv_sems, local_sems,
):
    ring = Ring(planes, depth, send_sems, recv_sems)
    barrier = pltpu.get_barrier_semaphore()
    for device in ring.everyone():
        pl.semaphore_signal(barrier, inc=1, device_id=device, device_id_type=MESH)
    pl.semaphore_wait(barrier, planes + depth - 1)

    rows = images * tokens
    width = 4 * LANES
    step = 5 * images
    steps = rows // step
    share = width // depth
    cw = we_ref.shape[2]
    prm = lambda row, tile: prm_ref[row : row + 1, lane(tile)]
    row = lambda r: prm_ref[r : r + 1, :]
    block_at = lambda k: pl.ds(pl.multiple_of(k * step, step), step)

    get_out = Gather(ring, wo_shard, wo_ref, False)
    get_expand = Gather(ring, we_shard, we_ref, True)
    get_reduce = Gather(ring, wr_shard, wr_ref, True)
    gathers = (get_out, get_expand, get_reduce)
    get_bias = [ring.send(eb_shard, eb_ref.at[depth - k], ring.stack(k)) for k in range(1, depth)]
    own = [
        pltpu.make_async_copy(source, target, local_sems.at[at])
        for at, (source, target) in enumerate(
            ((wo_shard, wo_ref.at[ring.me]), (we_shard, we_ref.at[0]), (wr_shard, wr_ref.at[0]), (eb_shard, eb_ref.at[0]))
        )
    ]
    for copy in own:
        copy.start()

    x_row = lambda tile, i: [
        x_ref[cell_rows(images, i * GRID + j), lane(tile)].astype(f32) for j in range(GRID)
    ]

    def position(tile, carry):
        x1_ref[tile, 0:images, :] = x_ref[0:images, lane(tile)].astype(f32)
        bias = prm(ROW_POS_BIAS, tile)

        def emit(i, total):
            here = x_row(tile, i)
            for j in range(GRID):
                x1_ref[tile, cell_rows(images, i * GRID + j), :] = here[j] + total[j] + bias

        depthwise_rows(
            partial(x_row, tile), lambda ab: prm(ROW_POS_KERNEL + ab[0] * 3 + ab[1], tile), 3, False, emit
        )
        return carry

    lax.fori_loop(0, 4, position, 0)

    def norm_of(source, target, gain, shift):
        def norm(k, carry):
            at = block_at(k)
            unit, _ = normalise(wide(source, at))
            target[at, :] = (unit * gain + shift).astype(bf16)
            return carry

        lax.fori_loop(0, steps, norm, 0)

    gain_one, shift_one = row(ROW_EARLY_GAIN), row(ROW_EARLY_SHIFT)
    norm_of(x1_ref, h1_ref, gain_one, shift_one)
    every = slice(0, rows)
    put_wide(v_ref, every, (dot(h1_ref[...], wj_ref[:, 2 * width :]) + row(ROW_BIAS_V)).astype(bf16).astype(f32))
    for gather in gathers:
        gather.plane()
    put_wide(ks_ref, every, dot(h1_ref[...], wj_ref[:, width : 2 * width]).astype(bf16).astype(f32))
    put_wide(q_ref, every, (dot(h1_ref[...], wj_ref[:, :width]) + row(ROW_BIAS_Q)).astype(bf16).astype(f32))

    token = lambda n: slice(n * images, (n + 1) * images)

    def soften(tile, carry):
        top = ks_ref[tile, token(0), :]
        for n in range(1, tokens):
            top = jnp.maximum(top, ks_ref[tile, token(n), :])
        total = jnp.zeros_like(top)
        for n in range(tokens):
            e = jnp.exp(ks_ref[tile, token(n), :] - top)
            ks_ref[tile, token(n), :] = e
            total = total + e
        scale = 1.0 / total
        for n in range(tokens):
            ks_ref[tile, token(n), :] = ks_ref[tile, token(n), :] * scale
        return carry

    lax.fori_loop(0, 4, soften, 0)

    def convolve(tile, extent):
        conv_ref[tile, 0:images, :] = jnp.zeros((images, LANES), f32)
        bias = prm(ROW_BIAS_ALL, tile)

        def emit(i, total):
            for j in range(GRID):
                conv_ref[tile, cell_rows(images, i * GRID + j), :] = total[j] + bias

        depthwise_rows(
            partial(grid_row, v_ref, tile, images), lambda ab: prm(full_tap(extent, *ab), tile),
            extent, False, emit,
        )

    tile_extents(convolve)
    for gather in gathers:
        gather.pair()

    def image(b, carry):
        for source, target in ((q_ref, qi_ref), (ks_ref, ki_ref), (v_ref, vi_ref)):
            target[b, 48:PAD_TOK, :] = jnp.zeros((PAD_TOK - 48, width), bf16)
            for tile in range(4):
                target[b, 0:tokens, lane(tile)] = source[tile, pl.ds(b, tokens, stride=images), :].astype(bf16)
        for g in range(2):
            at = slice(g * GROUP, (g + 1) * GROUP)
            compact = compact_context(dot(ki_ref[b, :, at], vi_ref[b, :, at], 0, 0))
            ctx_ref[b, :, at] = compact
            out = dot(qi_ref[b, :, at], spread_context(compact)) * SCALE
            for t in range(2):
                fac_ref[2 * g + t, pl.ds(b, tokens, stride=images), :] = out[0:tokens, lane(t)]
        return carry

    lax.fori_loop(0, images, image, 0)

    def combine(tile, carry):
        att_ref[:, lane(tile)] = (fac_ref[tile] + q_ref[tile] * conv_ref[tile]).astype(bf16)
        return carry

    lax.fori_loop(0, 4, combine, 0)

    for copy in own:
        copy.wait()
    arrive(get_bias)
    for gather in gathers:
        gather.finish()
    whole_out = jnp.concatenate([wo_ref[t, 0:share, :] for t in range(depth)], axis=0)
    branch = dot(att_ref[...], whole_out) + row(ROW_OUT_BIAS)
    for tile in range(4):
        x2_ref[tile] = x1_ref[tile] + branch[:, lane(tile)]
    gain_two, shift_two = row(ROW_LATE_GAIN), row(ROW_LATE_SHIFT)
    norm_of(x2_ref, h2_ref, gain_two, shift_two)

    send_expand = Reduction(ring, ge_ref, te_ref, pe_ref, se_ref, gwe_ref, False, True)
    send_reduce = Reduction(ring, gr_ref, tr_ref, pr_ref, sr_ref, gwr_ref, False, True)
    send_out = Reduction(ring, go_ref, to_ref, po_ref, so_ref, gwo_ref, False, False)
    send_joint = Reduction(ring, gj_ref, tj_ref, pj_ref, sj_ref, gwj_ref, True, False)
    send_small = Reduction(ring, gs_ref, ts_ref, ps_ref, ss_ref, gsm_ref, True, False)
    feed = (send_expand, send_reduce)
    acc_ref, dh2_ref = one_ref, two_ref
    hid_ref, dpre_ref = raw_ref.at[:, 0:cw], raw_ref.at[:, width : width + cw]
    datt_ref = raw_ref.at[:, 2 * width : 3 * width]
    half = rows // 2
    sums_ref[...] = jnp.zeros_like(sums_ref)
    for c in range(depth):
        bias = eb_ref[c, 0:1, :]
        folded = jnp.zeros((8, cw), f32)
        we, wr = we_ref[c], wr_ref[c, 0:cw, :]
        for k in range(2):
            at = slice(k * half, (k + 1) * half)
            pre = dot(h2_ref[at, :], we) + bias
            dh = dot(cot_ref[at, :], wr, 1, 1)
            gauss = jnp.exp(pre * pre * -0.5)
            t = 1.0 / (1.0 + (0.3275911 * 0.7071067811865476) * jnp.abs(pre))
            poly = t * (0.127414796 + t * (-0.142248368 + t * (0.7107068705 + t * (-0.7265760135 + t * 0.5307027145))))
            tail = poly * gauss
            cdf = jnp.where(pre >= 0, 1.0 - tail, tail)
            hid_ref[at, :] = (pre * cdf).astype(bf16)
            dpre = ((cdf + pre * gauss * 0.3989422804014327) * dh).astype(bf16)
            dpre_ref[at, :] = dpre
            folded = folded + fold_rows(dpre.astype(f32))
        sums_ref[OUT_EXPAND_BIAS + lax.rem(ring.me + c, depth), :, 0:cw] = folded
        ge_ref[c] = dot(h2_ref[...], dpre_ref[...], 0, 0).astype(bf16)
        gr_ref[c, 0:cw] = dot(hid_ref[...], cot_ref[...], 0, 0).astype(bf16)
        if gr_ref.shape[1] > cw:
            gr_ref[c, cw:] = jnp.zeros((gr_ref.shape[1] - cw, width), bf16)
        for part in feed:
            part.pair(c)
        out = dot(hid_ref[...], wr)
        back = dot(dpre_ref[...], we, 1, 1)
        for tile in range(4):
            if c == 0:
                acc_ref[tile] = out[:, lane(tile)]
                dh2_ref[tile] = back[:, lane(tile)]
            else:
                acc_ref[tile] += out[:, lane(tile)]
                dh2_ref[tile] += back[:, lane(tile)]
        if c >= 1:
            for part in feed:
                part.plane(c - 1)
        if c >= 2:
            for part in feed:
                part.gather_plane(c - 2)

    def finish(k, carry):
        at = block_at(k)
        x2 = wide(x2_ref, at)
        y_ref[at, :] = (x2 + wide(acc_ref, at) + row(ROW_REDUCE_BIAS)).astype(bf16)
        unit, scale = normalise(x2)
        grad = wide(dh2_ref, at)
        dy = cot_ref[at, :].astype(f32)
        dx2 = dy + normalise_back(grad, gain_two, unit, scale)
        put_wide(x2_ref, at, dx2)
        low = dx2.astype(bf16)
        datt_ref[at, :] = low
        return (
            carry[0] + fold_rows(grad * unit), carry[1] + fold_rows(grad),
            carry[2] + fold_rows(low.astype(f32)), carry[3] + fold_rows(dy),
        )

    zero = jnp.zeros((8, width), f32)
    sums = lax.fori_loop(0, steps, finish, (zero,) * 4)
    for r, total in zip((OUT_LATE_GAIN, OUT_LATE_SHIFT, OUT_OUT_BIAS, OUT_REDUCE_BIAS), sums):
        sums_ref[r] = total
    for part in feed:
        part.plane(depth - 1)
        if depth > 1:
            part.gather_plane(depth - 2)
    grad_out = dot(att_ref[...], datt_ref[...], 0, 0).astype(bf16)
    for t in range(depth):
        go_ref[t, 0:share, :] = grad_out[t * share : (t + 1) * share, :]
        if go_ref.shape[1] > share:
            go_ref[t, share:, :] = jnp.zeros((go_ref.shape[1] - share, width), bf16)
    send_out.pair(send_out.all)
    grad_att = dot(datt_ref[...], whole_out, 1, 1).astype(bf16).astype(f32)
    da_ref, dq_ref, dk_ref, dv_ref = fac_ref, one_ref, two_ref, three_ref
    put_wide(da_ref, every, grad_att)
    send_out.plane(send_out.all)

    def image_back(b, carry):
        dai_ref[b, 48:PAD_TOK, :] = jnp.zeros((PAD_TOK - 48, width), bf16)
        for tile in range(4):
            dai_ref[b, 0:tokens, lane(tile)] = da_ref[tile, pl.ds(b, tokens, stride=images), :].astype(bf16)
        for g in range(2):
            at = slice(g * GROUP, (g + 1) * GROUP)
            grad = dai_ref[b, :, at]
            ctx = spread_context(ctx_ref[b, :, at])
            dctx = spread_context(compact_context(dot(qi_ref[b, :, at], grad, 0, 0) * SCALE))
            dq = dot(grad, ctx, 1, 1) * SCALE
            dk = dot(vi_ref[b, :, at], dctx, 1, 1)
            dv = dot(ki_ref[b, :, at], dctx)
            for t in range(2):
                here = pl.ds(b, tokens, stride=images)
                dq_ref[2 * g + t, here, :] = dq[0:tokens, lane(t)]
                dk_ref[2 * g + t, here, :] = dk[0:tokens, lane(t)]
                dv_ref[2 * g + t, here, :] = dv[0:tokens, lane(t)]
        return carry

    lax.fori_loop(0, images, image_back, 0)
    for part in feed:
        part.gather_plane(depth - 1)
        part.stack()
    send_out.gather_plane(send_out.all)
    send_out.stack()

    def relative(tile, extent):
        bias_q = jnp.zeros((images, LANES), f32)
        bias_all = jnp.zeros((images, LANES), f32)
        dot_sum = jnp.zeros((images, LANES), f32)
        for n in range(tokens):
            grad = da_ref[tile, token(n), :]
            dq = (dq_ref[tile, token(n), :] + grad * conv_ref[tile, token(n), :]).astype(bf16)
            raw_ref[token(n), lane(tile)] = dq
            bias_q = bias_q + dq.astype(f32)
            dc = grad * q_ref[tile, token(n), :]
            dc_ref[tile, token(n), :] = dc
            if n > 0:
                bias_all = bias_all + dc
            dot_sum = dot_sum + dk_ref[tile, token(n), :] * ks_ref[tile, token(n), :]
        for n in range(tokens):
            soft = ks_ref[tile, token(n), :]
            raw_ref[token(n), lane(tile + 4)] = (soft * (dk_ref[tile, token(n), :] - dot_sum)).astype(bf16)
        sums_ref[OUT_BIAS_Q, :, lane(tile)] = fold_rows(bias_q)
        sums_ref[OUT_BIAS_ALL, :, lane(tile)] = fold_rows(bias_all)
        first = dv_ref[tile, token(0), :].astype(bf16)
        raw_ref[token(0), lane(tile + 8)] = first
        bias_v = [first.astype(f32)]

        def emit(i, total):
            for j in range(GRID):
                here = cell_rows(images, i * GRID + j)
                dv = (dv_ref[tile, here, :] + total[j]).astype(bf16)
                raw_ref[here, lane(tile + 8)] = dv
                bias_v[0] = bias_v[0] + dv.astype(f32)

        depthwise_rows(
            partial(grid_row, dc_ref, tile, images), lambda ab: prm(full_tap(extent, *ab), tile),
            extent, True, emit,
        )
        sums_ref[OUT_BIAS_V, :, lane(tile)] = fold_rows(bias_v[0])
        extra = (GRID - extent) // 2

        def emit_tap(a, b, total):
            sums_ref[OUT_KERNEL_ALL + (a + extra) * GRID + b + extra, :, lane(tile)] = fold_rows(total)

        kernel_grads(
            partial(grid_row, dc_ref, tile, images), partial(grid_row, v_ref, tile, images), extent, emit_tap
        )

    tile_extents(relative)
    for part in feed:
        part.settle()
    send_out.settle()

    for k in range(3):
        at = slice(k * width, (k + 1) * width)
        grad_joint = dot(h1_ref[...], raw_ref[:, at], 0, 0).astype(bf16)
        for t in range(depth):
            gj_ref[t, 0:share, at] = grad_joint[t * share : (t + 1) * share, :]
            if gj_ref.shape[1] > share:
                gj_ref[t, share:, at] = jnp.zeros((gj_ref.shape[1] - share, width), bf16)
    send_joint.pair(send_joint.all)
    dh1_ref = one_ref
    put_wide(dh1_ref, every, dot(raw_ref[...], wj_ref[...], 1, 1))
    send_joint.plane(send_joint.all)
    for part in feed:
        part.to_twin()
    send_out.to_twin()

    def back(k, carry):
        at = block_at(k)
        grad = wide(dh1_ref, at)
        unit, scale = normalise(wide(x1_ref, at))
        put_wide(da_ref, at, wide(x2_ref, at) + normalise_back(grad, gain_one, unit, scale))
        return carry[0] + fold_rows(grad * unit), carry[1] + fold_rows(grad)

    sums = lax.fori_loop(0, steps, back, (zero, zero))
    sums_ref[OUT_EARLY_GAIN] = sums[0]
    sums_ref[OUT_EARLY_SHIFT] = sums[1]

    def position_back(tile, carry):
        bias = [jnp.zeros((images, LANES), f32)]
        dx_ref[0:images, lane(tile)] = da_ref[tile, 0:images, :].astype(bf16)

        def emit(i, total):
            here = grid_row(da_ref, tile, images, i)
            for j in range(GRID):
                dx_ref[cell_rows(images, i * GRID + j), lane(tile)] = (here[j] + total[j]).astype(bf16)
                bias[0] = bias[0] + here[j]

        depthwise_rows(
            partial(grid_row, da_ref, tile, images),
            lambda ab: prm(ROW_POS_KERNEL + ab[0] * 3 + ab[1], tile),
            3, True, emit,
        )
        sums_ref[OUT_POS_BIAS, :, lane(tile)] = fold_rows(bias[0])

        def emit_tap(a, b, total):
            sums_ref[OUT_POS_KERNEL + a * 3 + b, :, lane(tile)] = fold_rows(total)

        kernel_grads(partial(grid_row, da_ref, tile, images), partial(x_row, tile), 3, emit_tap)
        return carry

    lax.fori_loop(0, 4, position_back, 0)
    send_joint.gather_plane(send_joint.all)
    send_joint.stack()

    small = jnp.sum(sums_ref[...], axis=1).astype(bf16)
    for t in range(depth):
        gs_ref[t] = jnp.zeros(gs_ref.shape[1:], bf16)
        gs_ref[t, 0 : small.shape[0], :] = small[:, t * share : (t + 1) * share]
    send_small.pair(send_small.all)
    send_small.plane(send_small.all)
    send_joint.settle()
    send_small.gather_plane(send_small.all)
    send_small.stack()
    send_joint.to_plane()
    send_small.settle()
    send_joint.to_twin()
    send_small.to_plane()
    send_small.to_twin()
    for part in (send_expand, send_reduce, send_out, send_joint, send_small):
        part.finish()
    for copy in ring.sent:
        copy.wait_send()


def pack_params(position_kernel, position_bias, early_gain, early_shift, joint_bias, small_kernel, small_bias,
                middle_kernel, middle_bias, large_kernel, large_bias, output_bias, late_gain, late_shift, reduce_bias):
    width = position_bias.shape[0]
    kernel_all = jnp.concatenate(
        [
            jnp.pad(small_kernel, ((2, 2), (2, 2), (0, 0))),
            jnp.pad(middle_kernel, ((1, 1), (1, 1), (0, 0))),
            large_kernel,
        ],
        axis=2,
    ).reshape(CELLS, width)
    return jnp.concatenate(
        [
            position_bias[None], early_gain[None], early_shift[None], joint_bias.reshape(2, width),
            jnp.concatenate([small_bias, middle_bias, large_bias])[None],
            output_bias[None], late_gain[None], late_shift[None], reduce_bias[None],
            position_kernel.reshape(9, width), kernel_all,
            jnp.zeros((PARAM_ROWS - ROW_KERNEL_ALL - CELLS, width), bf16),
        ],
        axis=0,
    ).astype(f32)


def per_device(
    block_input, position_kernel, position_bias, early_gain, early_shift, joint_weight, joint_bias,
    small_kernel, small_bias, middle_kernel, middle_bias, large_kernel, large_bias,
    output_weight, output_bias, late_gain, late_shift, expand_weight, expand_bias,
    reduce_weight, reduce_bias, cotangent,
):
    images, tokens, width = block_input.shape
    rows = images * tokens
    depth, copies_of = lax.axis_size("tensor"), lax.axis_size("dp")
    planes = math.gcd(copies_of // 2, 4)
    pieces = 2 * planes
    share, cw = width // depth, expand_weight.shape[1]
    params = pack_params(
        position_kernel, position_bias, early_gain, early_shift, joint_bias, small_kernel, small_bias,
        middle_kernel, middle_bias, large_kernel, large_bias, output_bias, late_gain, late_shift, reduce_bias,
    )
    unit = 16 * pieces
    sum_rows = padded(OUT_EXPAND_BIAS + depth, 16)
    shapes = [
        (padded(share, unit), width), (padded(width, unit), cw), (padded(cw, unit), width),
        (padded(share, unit), 3 * width), (padded(sum_rows, unit), share),
    ]
    near, far = planes - 1, depth - 1
    copies = 11 * far + (2 + far) * near + 2 + far + 2 * depth * (1 + near) + 3 * (1 + near) + 5 * near + 5
    fill = lambda array, count: jnp.pad(array, ((0, count - array.shape[0]), (0, 0)))
    tiled = pltpu.VMEM((4, rows, LANES), f32)
    low = pltpu.VMEM((rows, width), bf16)
    per_image = pltpu.VMEM((images, PAD_TOK, width), bf16)
    boxes = lambda lead: [pltpu.VMEM(lead + shape, bf16) for shape in shapes]
    halves = [pltpu.VMEM((depth, r // 2, w), bf16) for r, w in shapes]
    pieces_of = lambda lead: [pltpu.VMEM(lead + (r // pieces, w), bf16) for r, w in shapes]
    scratch = (
        [tiled] * 11
        + [low] * 3 + [pltpu.VMEM((rows, 3 * width), bf16)]
        + [per_image] * 4 + [pltpu.VMEM((images, HEAD, width), bf16)]
        + [pltpu.VMEM((sum_rows, 8, width), f32)]
        + [pltpu.VMEM((depth,) + shape, bf16) for shape in shapes[:3]] + [pltpu.VMEM((depth, 8, cw), f32)]
        + boxes((depth,)) + halves + pieces_of((planes - 1, depth)) + pieces_of((depth - 1,))
        + [pltpu.SemaphoreType.DMA((copies,))] * 2 + [pltpu.SemaphoreType.DMA((4,))]
    )
    flat = lambda array: array.transpose(1, 0, 2).reshape(rows, width)
    anywhere = pl.BlockSpec(memory_space=pl.ANY)
    inside = pl.BlockSpec(memory_space=pltpu.VMEM)
    outs = [
        ((rows, width), bf16), ((rows, width), bf16),
        (shapes[0], bf16), (shapes[1], bf16), (shapes[2], bf16),
        ((depth,) + shapes[3], bf16), ((depth,) + shapes[4], bf16),
    ]
    y, dx, gwo, gwe, gwr, gwj, small = pl.pallas_call(
        partial(whole_block, images, tokens, planes, depth),
        out_shape=[jax.ShapeDtypeStruct(shape, dtype) for shape, dtype in outs],
        in_specs=[inside] * 4 + [anywhere] * 4,
        out_specs=[inside] * len(outs),
        scratch_shapes=scratch,
        compiler_params=pltpu.CompilerParams(
            vmem_limit_bytes=VMEM_BYTES, collective_id=1, has_side_effects=True
        ),
    )(
        flat(block_input), flat(cotangent), params, joint_weight,
        fill(output_weight, shapes[0][0]), fill(expand_weight, shapes[1][0]), fill(reduce_weight, shapes[2][0]),
        jnp.broadcast_to(expand_bias.astype(f32)[None], (8, cw)),
    )
    if copies_of > pieces:
        groups = [list(range(first, copies_of, pieces)) for first in range(pieces)]
        gwo, gwe, gwr, gwj, small = lax.psum((gwo, gwe, gwr, gwj, small), "dp", axis_index_groups=groups)
    image_form = lambda array: array.reshape(tokens, images, width).transpose(1, 0, 2)
    small = small.astype(f32).transpose(1, 0, 2).reshape(-1, width)
    kernel_all = small[OUT_KERNEL_ALL : OUT_KERNEL_ALL + CELLS].reshape(GRID, GRID, width)
    bias_all = small[OUT_BIAS_ALL]
    one = small_kernel.shape[2]
    two = one + middle_kernel.shape[2]
    bias_row = lax.dynamic_slice_in_dim(small, OUT_EXPAND_BIAS + lax.axis_index("tensor"), 1, 0)
    return (
        image_form(y), image_form(dx), small[OUT_POS_KERNEL : OUT_POS_KERNEL + 9].reshape(3, 3, width),
        small[OUT_POS_BIAS], small[OUT_EARLY_GAIN], small[OUT_EARLY_SHIFT],
        gwj[:, :share].reshape(width, 3 * width).astype(f32),
        small[OUT_BIAS_Q : OUT_BIAS_V + 1].reshape(-1),
        kernel_all[2:5, 2:5, :one], bias_all[:one], kernel_all[1:6, 1:6, one:two], bias_all[one:two],
        kernel_all[:, :, two:], bias_all[two:],
        gwo[:share].astype(f32), small[OUT_OUT_BIAS], small[OUT_LATE_GAIN], small[OUT_LATE_SHIFT],
        gwe[:width].astype(f32), bias_row[0, :cw], gwr[:cw].astype(f32), small[OUT_REDUCE_BIAS],
    )


def solution(mesh):
    images = P(("dp", "tensor"), None, None)
    in_specs = (images,) + (P(),) * 12 + (
        P("tensor", None), P(), P(), P(), P(None, "tensor"), P("tensor"), P("tensor", None), P(), images,
    )
    out_specs = (images, images) + (P(),) * 12 + (
        P("tensor", None), P(), P(), P(), P(None, "tensor"), P("tensor"), P("tensor", None), P(),
    )
    return jax.shard_map(per_device, mesh=mesh, in_specs=in_specs, out_specs=out_specs, check_vma=False)
```

```python
import math
from functools import partial

import jax
import jax.numpy as jnp
from jax import lax
from jax.experimental import pallas as pl
from jax.experimental.pallas import tpu as pltpu
from jax.sharding import PartitionSpec as P

HEADS = 8
HEAD = 64
GRID = 7
CELLS = GRID * GRID
NORM_EPS = 1e-06
SCALE = HEAD**-0.5
LANES = 128
GROUP = 256
PAD_TOK = 64
VMEM_BYTES = 62 * 1024 * 1024

f32 = jnp.float32
bf16 = jnp.bfloat16

ROW_POS_BIAS, ROW_EARLY_GAIN, ROW_EARLY_SHIFT, ROW_BIAS_Q, ROW_BIAS_V = 0, 1, 2, 3, 4
ROW_BIAS_ALL, ROW_OUT_BIAS, ROW_LATE_GAIN, ROW_LATE_SHIFT, ROW_REDUCE_BIAS = 5, 6, 7, 8, 9
ROW_POS_KERNEL, ROW_KERNEL_ALL = 10, 19
PARAM_ROWS = 72

OUT_KERNEL_ALL, OUT_BIAS_Q, OUT_BIAS_V, OUT_BIAS_ALL = 0, 49, 50, 51
OUT_LATE_GAIN, OUT_LATE_SHIFT, OUT_OUT_BIAS, OUT_REDUCE_BIAS, OUT_EXPAND_BIAS = 52, 53, 54, 55, 56
TAIL_POS_KERNEL, TAIL_POS_BIAS, TAIL_EARLY_GAIN, TAIL_EARLY_SHIFT, TAIL_ROWS = 0, 9, 10, 11, 16
MESH = pl.DeviceIdType.MESH


def lane(tile):
    if isinstance(tile, int):
        return slice(tile * LANES, (tile + 1) * LANES)
    return pl.ds(pl.multiple_of(tile * LANES, LANES), LANES)


def taps(extent):
    return range(extent)


def columns(shift):
    return range(max(0, -shift), min(GRID, GRID - shift))


def depthwise_rows(get_row, get_weight, extent, flip, emit):
    margin = extent // 2
    for i in range(GRID):
        total = [None] * GRID
        for a in range(extent):
            r = i + a - margin
            if not 0 <= r < GRID:
                continue
            row = get_row(r)
            for b in range(extent):
                weight = get_weight((extent - 1 - a, extent - 1 - b) if flip else (a, b))
                for j in columns(b - margin):
                    term = row[j + b - margin] * weight
                    total[j] = term if total[j] is None else total[j] + term
        emit(i, total)


def kernel_grads(get_left, get_right, extent, emit):
    margin = extent // 2
    for a in range(extent):
        total = [None] * extent
        for i in range(GRID):
            r = i + a - margin
            if not 0 <= r < GRID:
                continue
            left, right = get_left(i), get_right(r)
            for b in range(extent):
                for j in columns(b - margin):
                    term = left[j] * right[j + b - margin]
                    total[b] = term if total[b] is None else total[b] + term
        for b in range(extent):
            emit(a, b, total[b])


def cell_rows(images, cell, count=1):
    return slice((1 + cell) * images, (1 + cell + count) * images)


def grid_row(ref, tile, images, i):
    block = ref[tile, cell_rows(images, i * GRID, GRID), :]
    return [block[j * images : (j + 1) * images] for j in range(GRID)]


def full_tap(extent, a, b):
    extra = (GRID - extent) // 2
    return ROW_KERNEL_ALL + (a + extra) * GRID + b + extra


def narrow_tiles(body):
    body(0, 3)
    body(1, 5)


def wide_tiles(body):
    def rest(tile, carry):
        body(tile, 7)
        return carry

    lax.fori_loop(2, 4, rest, 0)


def normalise(block):
    centre = jnp.mean(block, axis=-1, keepdims=True)
    centred = block - centre
    spread = jnp.mean(centred * centred, axis=-1, keepdims=True)
    scale = lax.rsqrt(spread + NORM_EPS)
    return centred * scale, scale


def normalise_back(grad, gain, unit, scale):
    scaled = grad * gain
    mean_one = jnp.mean(scaled, axis=-1, keepdims=True)
    mean_two = jnp.mean(scaled * unit, axis=-1, keepdims=True)
    return (scaled - mean_one - unit * mean_two) * scale


def fold_rows(block):
    return jnp.sum(block.reshape(block.shape[0] // 8, 8, block.shape[1]), axis=0)


def dot(left, right, left_dim=1, right_dim=0):
    return lax.dot_general(
        left, right, (((left_dim,), (right_dim,)), ((), ())), preferred_element_type=f32
    )


def padded(count, unit):
    return -(-count // unit) * unit


class Ring:
    def __init__(self, pairs, depth, send_sems, recv_sems):
        self.dp = lax.axis_index("dp")
        self.me = lax.axis_index("tensor")
        self.planes, self.depth = pairs, depth
        group = 2 * pairs
        self.base = lax.div(self.dp, group) * group
        self.core = lax.rem(self.dp, 2)
        self.spot = lax.div(lax.rem(self.dp, group), 2)
        self.send_sems, self.recv_sems, self.used = send_sems, recv_sems, 0
        self.sent = []

    def twin(self):
        return {"dp": self.base + self.spot * 2 + (1 - self.core), "tensor": self.me}

    def plane(self, k):
        return {"dp": self.base + lax.rem(self.spot + k, self.planes) * 2 + self.core, "tensor": self.me}

    def plane_spot(self, k):
        return lax.rem(self.spot + k, self.planes)

    def across(self, k):
        return {"dp": self.base + self.beside(k) * 2 + self.core, "tensor": self.me}

    def beside(self, k):
        low, high = lax.rem(self.spot, 2), lax.div(self.spot, 2)
        return high * 2 + 1 - low if k == 1 else (1 - high) * 2 + low

    def stack(self, k):
        return {"dp": self.dp, "tensor": lax.rem(self.me + k, self.depth)}

    def everyone(self):
        return (
            [self.twin()]
            + [self.plane(k) for k in range(1, self.planes)]
            + [self.stack(k) for k in range(1, self.depth)]
        )

    def piece(self, rows, spot, core=None):
        each = rows // (2 * self.planes)
        core = self.core if core is None else core
        return pl.ds(pl.multiple_of((core * self.planes + spot) * each, each), each)

    def band(self, rows, high):
        each = rows // (2 * self.planes)
        start = (self.core * self.planes + high * 2) * each
        return pl.ds(pl.multiple_of(start, 2 * each), 2 * each)

    def half(self, rows, core):
        return pl.ds(pl.multiple_of(core * (rows // 2), rows // 2), rows // 2)

    def send(self, source, target, device):
        at = self.used
        self.used += 1
        copy = pltpu.make_async_remote_copy(
            src_ref=source, dst_ref=target, send_sem=self.send_sems.at[at], recv_sem=self.recv_sems.at[at],
            device_id=device, device_id_type=MESH,
        )
        copy.start()
        self.sent.append(copy)
        return copy


def arrive(copies):
    for copy in copies:
        copy.wait_recv()


class Reduction:
    def __init__(self, ring, grads, twin_box, plane_box, stack_box, out, whole, relative):
        self.ring, self.grads, self.out, self.whole, self.relative = ring, grads, out, whole, relative
        self.twin_box, self.plane_box, self.stack_box = twin_box, plane_box, stack_box
        self.rows = grads.shape[1]
        self.depth = grads.shape[0]
        self.pairs, self.planes, self.stacks = {}, {}, {}
        self.all = slice(0, self.depth)

    def slot(self, k):
        return k if self.relative else lax.rem(self.ring.me + k, self.depth)

    def pair(self, part):
        ring = self.ring
        away = ring.half(self.rows, 1 - ring.core)
        self.pairs[str(part)] = ring.send(self.grads.at[part, away], self.twin_box.at[part], ring.twin())

    def plane(self, part):
        ring = self.ring
        arrive([self.pairs[str(part)]])
        mine = ring.half(self.rows, ring.core)
        self.grads[part, mine] = (
            self.grads[part, mine].astype(f32) + self.twin_box[part].astype(f32)
        ).astype(bf16)
        self.planes[str(part)] = [
            ring.send(
                self.grads.at[part, ring.piece(self.rows, ring.plane_spot(k))],
                self.plane_box.at[k - 1, part], ring.plane(k),
            )
            for k in range(1, ring.planes)
        ]

    def gather_plane(self, part):
        ring = self.ring
        arrive(self.planes[str(part)])
        mine = ring.piece(self.rows, ring.spot)
        total = self.grads[part, mine].astype(f32)
        for k in range(1, ring.planes):
            total = total + self.plane_box[k - 1, part].astype(f32)
        self.grads[part, mine] = total.astype(bf16)

    def stack(self, offsets=None):
        ring = self.ring
        mine = ring.piece(self.rows, ring.spot)
        for k in range(1, self.depth) if offsets is None else offsets:
            self.stacks[k] = ring.send(self.grads.at[self.slot(k), mine], self.stack_box.at[k - 1], ring.stack(k))

    def settle(self):
        ring = self.ring
        arrive(self.stacks.values())
        mine = ring.piece(self.rows, ring.spot)
        total = self.grads[self.slot(0), mine].astype(f32)
        for k in self.stacks:
            total = total + self.stack_box[k - 1].astype(f32)
        done = total.astype(bf16)
        if self.whole:
            self.out[ring.me, mine] = done
            place = self.out.at[ring.me, mine]
            self.spread = [ring.send(place, place, ring.stack(k)) for k in range(1, self.depth)]
        else:
            self.out[mine] = done
            self.to_plane()

    def to_plane(self):
        ring = self.ring
        mine = ring.piece(self.rows, ring.spot)
        if self.whole:
            arrive(self.spread)
            place = self.out.at[:, mine]
        else:
            place = self.out.at[mine]
        self.back = [ring.send(place, place, ring.plane(k)) for k in range(1, ring.planes)]

    def to_twin(self):
        ring = self.ring
        arrive(self.back)
        mine = ring.half(self.rows, ring.core)
        place = self.out.at[:, mine] if self.whole else self.out.at[mine]
        self.last = ring.send(place, place, ring.twin())

    def finish(self):
        arrive([self.last])


class Feed(Reduction):
    def __init__(self, ring, grads, twin_box, first_box, band_box, low_box, high_box, stack_box, slide_box, out):
        super().__init__(ring, grads, twin_box, None, stack_box, out, False, True)
        self.first_box, self.band_box, self.low_box, self.high_box = first_box, band_box, low_box, high_box
        self.slide_box = slide_box
        self.cut = grads.shape[2] // 2
        self.ones, self.twos = {}, {}

    def add(self, part, at, columns, box):
        self.grads[part, at, columns] = (self.grads[part, at, columns].astype(f32) + box.astype(f32)).astype(bf16)

    def meet(self, part):
        ring = self.ring
        arrive([self.pairs[str(part)]])
        mine = ring.half(self.rows, ring.core)
        self.grads[part, mine] = (
            self.grads[part, mine].astype(f32) + self.twin_box[part].astype(f32)
        ).astype(bf16)

    def slide(self):
        ring = self.ring
        self.meet(1)
        mine = ring.half(self.rows, ring.core)
        self.slid = ring.send(self.grads.at[1, mine], self.slide_box, ring.stack(1))

    def absorb(self):
        ring = self.ring
        arrive([self.slid])
        self.add(0, ring.half(self.rows, ring.core), slice(None), self.slide_box[...])

    def phase_one(self, part):
        ring = self.ring
        left, right = slice(0, self.cut), slice(self.cut, 2 * self.cut)
        low, high = lax.rem(ring.spot, 2), lax.div(ring.spot, 2)
        self.ones[part] = [
            ring.send(
                self.grads.at[part, ring.piece(self.rows, 2 * y + 1 - low), left],
                self.first_box.at[part, y], ring.across(1),
            )
            for y in range(2)
        ] + [
            ring.send(
                self.grads.at[part, ring.band(self.rows, 1 - high), right], self.band_box.at[part], ring.across(2)
            )
        ]

    def phase_two(self, part):
        ring = self.ring
        left, right = slice(0, self.cut), slice(self.cut, 2 * self.cut)
        low, high = lax.rem(ring.spot, 2), lax.div(ring.spot, 2)
        arrive(self.ones[part])
        for y in range(2):
            self.add(part, ring.piece(self.rows, 2 * y + low), left, self.first_box[part, y])
        self.add(part, ring.band(self.rows, high), right, self.band_box[part])
        self.twos[part] = [
            ring.send(
                self.grads.at[part, ring.piece(self.rows, ring.beside(2)), left], self.high_box.at[part], ring.across(2)
            ),
            ring.send(
                self.grads.at[part, ring.piece(self.rows, ring.beside(1)), right], self.low_box.at[part], ring.across(1)
            ),
        ]

    def gather_plane(self, part):
        ring = self.ring
        arrive(self.twos[part])
        mine = ring.piece(self.rows, ring.spot)
        self.add(part, mine, slice(0, self.cut), self.high_box[part])
        self.add(part, mine, slice(self.cut, 2 * self.cut), self.low_box[part])


class Gather:
    def __init__(self, ring, shard, box, relative):
        self.ring, self.shard, self.box, self.relative = ring, shard, box, relative
        self.depth, self.rows = box.shape[0], box.shape[1]
        self.first, self.between, self.second, self.third = {}, {}, {}, {}

    def slot(self, j):
        return j if self.relative else lax.rem(self.ring.me + j, self.depth)

    def start(self, j):
        ring = self.ring
        mine = ring.piece(self.rows, ring.spot)
        target = self.box.at[j if self.relative else ring.me, mine]
        self.first[j] = ring.send(self.shard.at[mine], target, ring.stack(self.depth - j))

    def plane(self, j):
        ring = self.ring
        arrive([self.first[j]])
        place = self.box.at[self.slot(j), ring.piece(self.rows, ring.spot)]
        self.second[j] = [ring.send(place, place, ring.plane(k)) for k in range(1, ring.planes)]

    def phase_one(self, j):
        ring = self.ring
        arrive([self.first[j]])
        cut = self.box.shape[2] // 2
        mine = ring.piece(self.rows, ring.spot)
        left = self.box.at[self.slot(j), mine, 0:cut]
        right = self.box.at[self.slot(j), mine, cut : 2 * cut]
        self.between[j] = [ring.send(left, left, ring.across(2)), ring.send(right, right, ring.across(1))]

    def phase_two(self, j):
        ring = self.ring
        arrive(self.between[j])
        cut = self.box.shape[2] // 2
        low, high = lax.rem(ring.spot, 2), lax.div(ring.spot, 2)
        places = [self.box.at[self.slot(j), ring.piece(self.rows, 2 * y + low), 0:cut] for y in range(2)]
        band = self.box.at[self.slot(j), ring.band(self.rows, high), cut : 2 * cut]
        self.second[j] = [ring.send(place, place, ring.across(1)) for place in places]
        self.second[j].append(ring.send(band, band, ring.across(2)))

    def pair(self, j):
        ring = self.ring
        arrive(self.second[j])
        place = self.box.at[self.slot(j), ring.half(self.rows, ring.core)]
        self.third[j] = ring.send(place, place, ring.twin())

    def finish(self, j):
        arrive([self.third[j]])


class Tail:
    def __init__(self, ring, mine, boxes):
        self.ring, self.mine, self.boxes = ring, mine, boxes

    def run(self):
        ring = self.ring
        partners = (
            [ring.twin()],
            [ring.plane(k) for k in range(1, ring.planes)],
            [ring.stack(k) for k in range(1, ring.depth)],
        )
        total = None
        for stage, devices in enumerate(partners):
            box = self.boxes[stage]
            copies = [ring.send(self.mine.at[stage], box.at[k], device) for k, device in enumerate(devices)]
            total = self.mine[stage].astype(f32)
            for k, copy in enumerate(copies):
                copy.wait_recv()
                total = total + box[k].astype(f32)
            if stage < 2:
                self.mine[stage + 1] = total.astype(bf16)
        return total


def wide(ref, at):
    return jnp.concatenate([ref[tile, at, :] for tile in range(4)], axis=1)


def put_wide(ref, at, block):
    for tile in range(4):
        ref[tile, at, :] = block[:, lane(tile)]


def whole_block(
    images, tokens, planes, depth,
    x_ref, cot_ref, wj_ref, pk_ref, pb_ref, eg_ref, es_ref, jb_ref, sk_ref, sb_ref, mk_ref, mb_ref, lk_ref, lb_ref,
    ob_ref, lg_ref, ls_ref, rb_ref, eb_shard, wo_shard, we_shard, wr_shard,
    y_ref, dx_ref, gwo_ref, gwe_ref, gwr_ref, gqk_ref, gv_ref, gsm_ref, gtail_ref,
    prm_ref, x1_ref, x2_ref, q_ref, v_ref, ks_ref, conv_ref, fac_ref, one_ref, two_ref, three_ref,
    h1_ref, att_ref, h2_ref, raw_ref,
    qi_ref, ki_ref, vi_ref, dai_ref, ctx_ref, sums_ref, last_ref,
    wo_ref, we_ref, wr_ref, eb_ref,
    go_ref, ge_ref, gr_ref, gj_ref, gk_ref, gs_ref,
    to_ref, te_ref, tr_ref, tj_ref, tk_ref, ts_ref,
    po_ref, pj_ref, pk2_ref, ps_ref,
    e_first, e_band, e_low, e_high, e_slide, r_first, r_band, r_low, r_high, r_slide,
    so_ref, se_ref, sr_ref, sj_ref, sk2_ref, ss_ref,
    tail_ref, tail_pair, tail_plane, tail_stack,
    send_sems, recv_sems, local_sems,
):
    ring = Ring(planes, depth, send_sems, recv_sems)
    barrier = pltpu.get_barrier_semaphore()
    for device in ring.everyone():
        pl.semaphore_signal(barrier, inc=1, device_id=device, device_id_type=MESH)

    rows = images * tokens
    width = 4 * LANES
    step = 5 * images
    steps = rows // step
    share = width // depth
    cw = we_ref.shape[2]
    get_out = Gather(ring, wo_shard, wo_ref, False)
    get_expand = Gather(ring, we_shard, we_ref, True)
    get_reduce = Gather(ring, wr_shard, wr_ref, True)
    feed_in = (get_expand, get_reduce)
    slots = range(1, depth)
    own = [
        pltpu.make_async_copy(source, target, local_sems.at[at])
        for at, (source, target) in enumerate(
            ((wo_shard, wo_ref.at[ring.me]), (we_shard, we_ref.at[0]), (wr_shard, wr_ref.at[0]))
        )
    ]
    for copy in own:
        copy.start()
    eb_ref[0] = jnp.broadcast_to(eb_shard[...].astype(f32).reshape(1, cw), (8, cw))

    for at, ref in (
        (ROW_POS_BIAS, pb_ref), (ROW_EARLY_GAIN, eg_ref), (ROW_EARLY_SHIFT, es_ref), (ROW_OUT_BIAS, ob_ref),
        (ROW_LATE_GAIN, lg_ref), (ROW_LATE_SHIFT, ls_ref), (ROW_REDUCE_BIAS, rb_ref),
    ):
        prm_ref[at : at + 1, :] = ref[...].astype(f32).reshape(1, width)
    prm_ref[ROW_BIAS_Q : ROW_BIAS_Q + 1, :] = jb_ref[0:width].astype(f32).reshape(1, width)
    prm_ref[ROW_BIAS_V : ROW_BIAS_V + 1, :] = jb_ref[width : 2 * width].astype(f32).reshape(1, width)
    prm_ref[ROW_KERNEL_ALL:PARAM_ROWS, :] = jnp.zeros((PARAM_ROWS - ROW_KERNEL_ALL, width), f32)
    first_lane = 0
    for kernel_ref, bias_ref in ((sk_ref, sb_ref), (mk_ref, mb_ref), (lk_ref, lb_ref)):
        extent, count = kernel_ref.shape[0], kernel_ref.shape[2]
        span = slice(first_lane, first_lane + count)
        prm_ref[ROW_BIAS_ALL : ROW_BIAS_ALL + 1, span] = bias_ref[...].astype(f32).reshape(1, count)
        for a in range(extent):
            at = full_tap(extent, a, 0)
            prm_ref[at : at + extent, span] = kernel_ref[a].astype(f32)
        first_lane += count
    for a in range(3):
        prm_ref[ROW_POS_KERNEL + 3 * a : ROW_POS_KERNEL + 3 * a + 3, :] = pk_ref[a].astype(f32)

    pl.semaphore_wait(barrier, planes + depth - 1)
    order = sorted(slots, key=lambda j: min(j, depth - j))
    get_bias = [ring.send(eb_ref.at[0], eb_ref.at[j], ring.stack(depth - j)) for j in slots]
    for j in slots:
        get_out.start(j)
    for part in feed_in:
        part.start(order[0])

    prm = lambda row, tile: prm_ref[row : row + 1, lane(tile)]
    row = lambda r: prm_ref[r : r + 1, :]
    block_at = lambda k: pl.ds(pl.multiple_of(k * step, step), step)

    x_row = lambda tile, i: [
        x_ref[cell_rows(images, i * GRID + j), lane(tile)].astype(f32) for j in range(GRID)
    ]

    def position(tile, carry):
        x1_ref[tile, 0:images, :] = x_ref[0:images, lane(tile)].astype(f32)
        bias = prm(ROW_POS_BIAS, tile)

        def emit(i, total):
            here = x_row(tile, i)
            for j in range(GRID):
                x1_ref[tile, cell_rows(images, i * GRID + j), :] = here[j] + total[j] + bias

        depthwise_rows(
            partial(x_row, tile), lambda ab: prm(ROW_POS_KERNEL + ab[0] * 3 + ab[1], tile), 3, False, emit
        )
        return carry

    lax.fori_loop(0, 4, position, 0)
    for j in order[1:2]:
        for part in feed_in:
            part.start(j)

    def norm_of(source, target, gain, shift):
        def norm(k, carry):
            at = block_at(k)
            unit, _ = normalise(wide(source, at))
            target[at, :] = (unit * gain + shift).astype(bf16)
            return carry

        lax.fori_loop(0, steps, norm, 0)

    gain_one, shift_one = row(ROW_EARLY_GAIN), row(ROW_EARLY_SHIFT)
    norm_of(x1_ref, h1_ref, gain_one, shift_one)
    every = slice(0, rows)
    put_wide(v_ref, every, (dot(h1_ref[...], wj_ref[:, 2 * width :]) + row(ROW_BIAS_V)).astype(bf16).astype(f32))
    put_wide(ks_ref, every, dot(h1_ref[...], wj_ref[:, width : 2 * width]).astype(bf16).astype(f32))
    for j in slots:
        get_out.plane(j)
    for j in order[2:]:
        for part in feed_in:
            part.start(j)
    put_wide(q_ref, every, (dot(h1_ref[...], wj_ref[:, :width]) + row(ROW_BIAS_Q)).astype(bf16).astype(f32))

    token = lambda n: slice(n * images, (n + 1) * images)

    def soften(tile, carry):
        top = ks_ref[tile, token(0), :]
        for n in range(1, tokens):
            top = jnp.maximum(top, ks_ref[tile, token(n), :])
        total = jnp.zeros_like(top)
        for n in range(tokens):
            e = jnp.exp(ks_ref[tile, token(n), :] - top)
            ks_ref[tile, token(n), :] = e
            total = total + e
        scale = 1.0 / total
        for n in range(tokens):
            ks_ref[tile, token(n), :] = ks_ref[tile, token(n), :] * scale
        return carry

    lax.fori_loop(0, 4, soften, 0)
    for part in feed_in:
        part.phase_one(order[0])

    def convolve(tile, extent):
        conv_ref[tile, 0:images, :] = jnp.zeros((images, LANES), f32)
        bias = prm(ROW_BIAS_ALL, tile)

        def emit(i, total):
            for j in range(GRID):
                conv_ref[tile, cell_rows(images, i * GRID + j), :] = total[j] + bias

        depthwise_rows(
            partial(grid_row, v_ref, tile, images), lambda ab: prm(full_tap(extent, *ab), tile),
            extent, False, emit,
        )

    narrow_tiles(convolve)
    for j in slots:
        get_out.pair(j)
    wide_tiles(convolve)
    for part in feed_in:
        part.phase_two(order[0])
    for j in order[1:2]:
        for part in feed_in:
            part.phase_one(j)

    some = images // 4
    lanes_of = lax.broadcasted_iota(jnp.int32, (LANES, LANES), 1) // HEAD
    rows_of = lax.broadcasted_iota(jnp.int32, (LANES, LANES), 0) // HEAD
    pair_mask = jnp.where(lanes_of == rows_of, 1.0, 0.0)
    here = lambda b: pl.ds(b, tokens, stride=images)

    def per_image(source, target, b):
        target[b, 48:PAD_TOK, :] = jnp.zeros((PAD_TOK - 48, width), bf16)
        for tile in range(4):
            target[b, 0:tokens, lane(tile)] = source[tile, here(b), :].astype(bf16)

    def image(g, carry):
        batch = [g * some + u for u in range(some)]
        for b in batch:
            for source, target in ((ks_ref, ki_ref), (v_ref, vi_ref), (q_ref, qi_ref)):
                per_image(source, target, b)
        for b in batch:
            for t in range(4):
                full = dot(ki_ref[b, :, lane(t)], vi_ref[b, :, lane(t)], 0, 0)
                ctx_ref[b, t] = (full * pair_mask).astype(bf16)
        for b in batch:
            for t in range(4):
                out = dot(qi_ref[b, :, lane(t)], ctx_ref[b, t]) * SCALE
                fac_ref[t, here(b), :] = out[0:tokens]
        return carry

    for g in range(4):
        lax.fori_loop(g, g + 1, image, 0)
        if g == 1:
            for j in order[1:2]:
                for part in feed_in:
                    part.phase_two(j)
        if g == 2:
            for part in feed_in:
                part.pair(order[0])
            for j in order[2:]:
                for part in feed_in:
                    part.phase_one(j)

    def combine(tile, carry):
        att_ref[:, lane(tile)] = (fac_ref[tile] + q_ref[tile] * conv_ref[tile]).astype(bf16)
        return carry

    lax.fori_loop(0, 4, combine, 0)

    for copy in own:
        copy.wait()
    for j in slots:
        get_out.finish(j)
    whole_out = jnp.concatenate([wo_ref[t, 0:share, :] for t in range(depth)], axis=0)
    branch = dot(att_ref[...], whole_out) + row(ROW_OUT_BIAS)
    for tile in range(4):
        x2_ref[tile] = x1_ref[tile] + branch[:, lane(tile)]
    for j in order[2:]:
        for part in feed_in:
            part.phase_two(j)
    gain_two, shift_two = row(ROW_LATE_GAIN), row(ROW_LATE_SHIFT)
    norm_of(x2_ref, h2_ref, gain_two, shift_two)

    send_expand = Feed(ring, ge_ref, te_ref, e_first, e_band, e_low, e_high, se_ref, e_slide, gwe_ref)
    send_reduce = Feed(ring, gr_ref, tr_ref, r_first, r_band, r_low, r_high, sr_ref, r_slide, gwr_ref)
    send_out = Reduction(ring, go_ref, to_ref, po_ref, so_ref, gwo_ref, False, False)
    send_qk = Reduction(ring, gj_ref, tj_ref, pj_ref, sj_ref, gqk_ref, True, False)
    send_v = Reduction(ring, gk_ref, tk_ref, pk2_ref, sk2_ref, gv_ref, True, False)
    send_small = Reduction(ring, gs_ref, ts_ref, ps_ref, ss_ref, gsm_ref, True, False)
    feed = (send_expand, send_reduce)

    def each(parts, step_name, *args):
        for part in parts:
            getattr(part, step_name)(*args)

    def feed_stack(c):
        for part in feed:
            part.gather_plane(c)
            part.stack([c])

    acc_ref, dh2_ref = one_ref, two_ref
    hid_ref, dpre_ref = raw_ref.at[:, 0:cw], raw_ref.at[:, width : width + cw]
    datt_ref = raw_ref.at[:, 2 * width : 3 * width]
    half = rows // 2
    sums_ref[...] = jnp.zeros_like(sums_ref)
    arrive(get_bias)
    each(feed_in, "pair", order[1])
    chunks = [0] + order
    for at_chunk, c in enumerate(chunks):
        if at_chunk >= 1:
            each(feed_in, "finish", c)
        if at_chunk == 1:
            for j in order[2:]:
                each(feed_in, "pair", j)
        bias = eb_ref[c, 0:1, :]
        folded = jnp.zeros((8, cw), f32)
        we, wr = we_ref[c], wr_ref[c, 0:cw, :]
        for k in range(2):
            at = slice(k * half, (k + 1) * half)
            pre = dot(h2_ref[at, :], we) + bias
            dh = dot(cot_ref[at, :], wr, 1, 1)
            gauss = jnp.exp(pre * pre * -0.5)
            t = 1.0 / (1.0 + (0.3275911 * 0.7071067811865476) * jnp.abs(pre))
            poly = t * (0.127414796 + t * (-0.142248368 + t * (0.7107068705 + t * (-0.7265760135 + t * 0.5307027145))))
            tail = poly * gauss
            cdf = jnp.where(pre >= 0, 1.0 - tail, tail)
            hid_ref[at, :] = (pre * cdf).astype(bf16)
            dpre = ((cdf + pre * gauss * 0.3989422804014327) * dh).astype(bf16)
            dpre_ref[at, :] = dpre
            folded = folded + fold_rows(dpre.astype(f32))
            if k == 0 and at_chunk == 1:
                each(feed, "meet", 0)
            if k == 0 and at_chunk == 2:
                each(feed, "slide")
            if k == 0 and at_chunk >= 3:
                each(feed, "meet", chunks[at_chunk - 1])
                each(feed, "phase_one", chunks[at_chunk - 1])
            if k == 1 and at_chunk >= 4:
                each(feed, "phase_two", chunks[at_chunk - 2])
            if k == 1 and at_chunk >= 5:
                feed_stack(chunks[at_chunk - 3])
        sums_ref[OUT_EXPAND_BIAS + lax.rem(ring.me + c, depth), :, 0:cw] = folded
        ge_ref[c] = dot(h2_ref[...], dpre_ref[...], 0, 0).astype(bf16)
        gr_ref[c, 0:cw] = dot(hid_ref[...], cot_ref[...], 0, 0).astype(bf16)
        if gr_ref.shape[1] > cw:
            gr_ref[c, cw:] = jnp.zeros((gr_ref.shape[1] - cw, width), bf16)
        for part in feed:
            part.pair(c)
        out = dot(hid_ref[...], wr)
        back = dot(dpre_ref[...], we, 1, 1)
        for tile in range(4):
            if at_chunk == 0:
                acc_ref[tile] = out[:, lane(tile)]
                dh2_ref[tile] = back[:, lane(tile)]
            else:
                acc_ref[tile] += out[:, lane(tile)]
                dh2_ref[tile] += back[:, lane(tile)]

    def finish(k, carry):
        at = block_at(k)
        x2 = wide(x2_ref, at)
        y_ref[at, :] = (x2 + wide(acc_ref, at) + row(ROW_REDUCE_BIAS)).astype(bf16)
        unit, scale = normalise(x2)
        grad = wide(dh2_ref, at)
        dy = cot_ref[at, :].astype(f32)
        dx2 = dy + normalise_back(grad, gain_two, unit, scale)
        put_wide(x2_ref, at, dx2)
        low = dx2.astype(bf16)
        datt_ref[at, :] = low
        return (
            carry[0] + fold_rows(grad * unit), carry[1] + fold_rows(grad),
            carry[2] + fold_rows(low.astype(f32)), carry[3] + fold_rows(dy),
        )

    zero = jnp.zeros((8, width), f32)
    sums = lax.fori_loop(0, steps, finish, (zero,) * 4)
    for r, total in zip((OUT_LATE_GAIN, OUT_LATE_SHIFT, OUT_OUT_BIAS, OUT_REDUCE_BIAS), sums):
        sums_ref[r] = total
    each(feed, "meet", chunks[-1])
    each(feed, "phase_one", chunks[-1])
    if depth > 3:
        each(feed, "phase_two", chunks[-2])
    if depth > 4:
        feed_stack(chunks[-3])
    grad_out = dot(att_ref[...], datt_ref[...], 0, 0).astype(bf16)
    for t in range(depth):
        go_ref[t, 0:share, :] = grad_out[t * share : (t + 1) * share, :]
        if go_ref.shape[1] > share:
            go_ref[t, share:, :] = jnp.zeros((go_ref.shape[1] - share, width), bf16)
    send_out.pair(send_out.all)
    grad_att = dot(datt_ref[...], whole_out, 1, 1).astype(bf16).astype(f32)
    da_ref, dq_ref, dk_ref, dv_ref = fac_ref, one_ref, two_ref, three_ref
    put_wide(da_ref, every, grad_att)

    def image_back(g, carry):
        batch = [g * some + u for u in range(some)]
        scaled = pair_mask * SCALE
        for b in batch:
            per_image(da_ref, dai_ref, b)
        for b in batch:
            for t in range(4):
                dq = dot(dai_ref[b, :, lane(t)], ctx_ref[b, t], 1, 1) * SCALE
                dq_ref[t, here(b), :] = dq[0:tokens]
        for b in batch:
            for t in range(4):
                full = dot(qi_ref[b, :, lane(t)], dai_ref[b, :, lane(t)], 0, 0)
                ctx_ref[b, t] = (full * scaled).astype(bf16)
        for b in batch:
            for t in range(4):
                dk = dot(vi_ref[b, :, lane(t)], ctx_ref[b, t], 1, 1)
                dk_ref[t, here(b), :] = dk[0:tokens]
                dv = dot(ki_ref[b, :, lane(t)], ctx_ref[b, t])
                dv_ref[t, here(b), :] = dv[0:tokens]
        return carry

    for g in range(4):
        lax.fori_loop(g, g + 1, image_back, 0)
        if g == 0:
            send_out.plane(send_out.all)
            each(feed, "phase_two", chunks[-1])
        if g == 1:
            if depth > 3:
                feed_stack(chunks[-2])
            each(feed, "absorb")
            each(feed, "phase_one", 0)
        if g == 2:
            feed_stack(chunks[-1])
            send_out.gather_plane(send_out.all)
            send_out.stack()
        if g == 3:
            each(feed, "phase_two", 0)

    def split(tile, carry):
        bias_q = jnp.zeros((images, LANES), f32)
        bias_all = jnp.zeros((images, LANES), f32)
        dot_sum = jnp.zeros((images, LANES), f32)
        for n in range(tokens):
            grad = da_ref[tile, token(n), :]
            dq = (dq_ref[tile, token(n), :] + grad * conv_ref[tile, token(n), :]).astype(bf16)
            raw_ref[token(n), lane(tile)] = dq
            bias_q = bias_q + dq.astype(f32)
            dc = grad * q_ref[tile, token(n), :]
            da_ref[tile, token(n), :] = dc
            if n > 0:
                bias_all = bias_all + dc
            dot_sum = dot_sum + dk_ref[tile, token(n), :] * ks_ref[tile, token(n), :]
        for n in range(tokens):
            soft = ks_ref[tile, token(n), :]
            raw_ref[token(n), lane(tile + 4)] = (soft * (dk_ref[tile, token(n), :] - dot_sum)).astype(bf16)
        sums_ref[OUT_BIAS_Q, :, lane(tile)] = fold_rows(bias_q)
        sums_ref[OUT_BIAS_ALL, :, lane(tile)] = fold_rows(bias_all)
        return carry

    lax.fori_loop(0, 4, split, 0)

    def grad_joint(target, part, at):
        grad = dot(h1_ref[...], raw_ref[:, part * width : (part + 1) * width], 0, 0).astype(bf16)
        for t in range(depth):
            target[t, 0:share, at] = grad[t * share : (t + 1) * share, :]
            if target.shape[1] > share:
                target[t, share:, at] = jnp.zeros((target.shape[1] - share, width), bf16)

    grad_joint(gj_ref, 0, slice(0, width))
    grad_joint(gj_ref, 1, slice(width, 2 * width))
    send_qk.pair(send_qk.all)

    def values_back(tile, extent):
        first = dv_ref[tile, token(0), :].astype(bf16)
        raw_ref[token(0), lane(tile + 8)] = first
        bias_v = [first.astype(f32)]

        def emit(i, total):
            for j in range(GRID):
                here = cell_rows(images, i * GRID + j)
                dv = (dv_ref[tile, here, :] + total[j]).astype(bf16)
                raw_ref[here, lane(tile + 8)] = dv
                bias_v[0] = bias_v[0] + dv.astype(f32)

        depthwise_rows(
            partial(grid_row, da_ref, tile, images), lambda ab: prm(full_tap(extent, *ab), tile),
            extent, True, emit,
        )
        sums_ref[OUT_BIAS_V, :, lane(tile)] = fold_rows(bias_v[0])

    narrow_tiles(values_back)
    send_qk.plane(send_qk.all)
    each(feed, "gather_plane", 0)
    each(feed, "settle")
    send_out.settle()
    wide_tiles(values_back)
    grad_joint(gk_ref, 2, slice(0, width))
    send_v.pair(send_v.all)

    def tap_grads(tile, extent):
        extra = (GRID - extent) // 2

        def emit_tap(a, b, total):
            sums_ref[OUT_KERNEL_ALL + (a + extra) * GRID + b + extra, :, lane(tile)] = fold_rows(total)

        kernel_grads(
            partial(grid_row, da_ref, tile, images), partial(grid_row, v_ref, tile, images), extent, emit_tap
        )

    narrow_tiles(tap_grads)
    send_v.plane(send_v.all)
    send_qk.gather_plane(send_qk.all)
    send_qk.stack()
    wide_tiles(tap_grads)
    send_out.to_twin()
    each(feed, "to_twin")
    small = jnp.sum(sums_ref[...], axis=1).astype(bf16)
    for t in range(depth):
        gs_ref[t] = jnp.zeros(gs_ref.shape[1:], bf16)
        gs_ref[t, 0 : small.shape[0], :] = small[:, t * share : (t + 1) * share]
    send_small.pair(send_small.all)

    dh1_ref = one_ref
    put_wide(dh1_ref, every, dot(raw_ref[...], wj_ref[...], 1, 1))
    send_v.gather_plane(send_v.all)
    send_v.stack()
    send_small.plane(send_small.all)
    send_qk.settle()

    def back(k, carry):
        at = block_at(k)
        grad = wide(dh1_ref, at)
        unit, scale = normalise(wide(x1_ref, at))
        put_wide(da_ref, at, wide(x2_ref, at) + normalise_back(grad, gain_one, unit, scale))
        return carry[0] + fold_rows(grad * unit), carry[1] + fold_rows(grad)

    sums = lax.fori_loop(0, steps, back, (zero, zero))
    send_small.gather_plane(send_small.all)
    send_small.stack()
    send_v.settle()
    send_qk.to_plane()
    last_ref[...] = jnp.zeros_like(last_ref)
    last_ref[TAIL_EARLY_GAIN] = sums[0]
    last_ref[TAIL_EARLY_SHIFT] = sums[1]

    def position_back(tile, carry):
        bias = [jnp.zeros((images, LANES), f32)]
        dx_ref[0:images, lane(tile)] = da_ref[tile, 0:images, :].astype(bf16)

        def emit(i, total):
            here = grid_row(da_ref, tile, images, i)
            for j in range(GRID):
                dx_ref[cell_rows(images, i * GRID + j), lane(tile)] = (here[j] + total[j]).astype(bf16)
                bias[0] = bias[0] + here[j]

        depthwise_rows(
            partial(grid_row, da_ref, tile, images),
            lambda ab: prm(ROW_POS_KERNEL + ab[0] * 3 + ab[1], tile),
            3, True, emit,
        )
        last_ref[TAIL_POS_BIAS, :, lane(tile)] = fold_rows(bias[0])

        def emit_tap(a, b, total):
            last_ref[TAIL_POS_KERNEL + a * 3 + b, :, lane(tile)] = fold_rows(total)

        kernel_grads(partial(grid_row, da_ref, tile, images), partial(x_row, tile), 3, emit_tap)
        return carry

    lax.fori_loop(0, 2, position_back, 0)
    send_v.to_plane()
    send_small.settle()
    lax.fori_loop(2, 4, position_back, 0)
    send_qk.to_twin()
    tail_ref[0] = jnp.sum(last_ref[...], axis=1).astype(bf16)
    send_small.to_plane()
    gtail_ref[...] = Tail(ring, tail_ref, (tail_pair, tail_plane, tail_stack)).run()
    send_v.to_twin()
    send_small.to_twin()
    for part in (send_expand, send_reduce, send_out, send_qk, send_v, send_small):
        part.finish()
    for copy in ring.sent:
        copy.wait_send()


def write_out(
    y_ref, dx_ref, gwo_ref, gwe_ref, gwr_ref, gqk_ref, gv_ref, gsm_ref, gtail_ref,
    y_out, dx_out, pk_out, pb_out, eg_out, es_out, jw_out, jb_out, sk_out, sb_out, mk_out, mb_out, lk_out, lb_out,
    ow_out, ob_out, lg_out, ls_out, ew_out, eb_out, rw_out, rb_out,
    small_ref, sems,
):
    copies = [pltpu.make_async_copy(y_ref, y_out, sems.at[0]), pltpu.make_async_copy(dx_ref, dx_out, sems.at[1])]
    for copy in copies:
        copy.start()
    depth = gqk_ref.shape[0]
    width = y_ref.shape[1]
    share = width // depth
    for t in range(depth):
        small_ref[:, t * share : (t + 1) * share] = gsm_ref[t].astype(f32)
        at = slice(t * share, (t + 1) * share)
        jw_out[at, 0 : 2 * width] = gqk_ref[t, 0:share, :].astype(f32)
        jw_out[at, 2 * width :] = gv_ref[t, 0:share, :].astype(f32)
    for ref, out in ((gwo_ref, ow_out), (gwe_ref, ew_out), (gwr_ref, rw_out)):
        out[...] = ref[0 : out.shape[0], :].astype(f32)
    for at, out in (
        (OUT_OUT_BIAS, ob_out), (OUT_LATE_GAIN, lg_out), (OUT_LATE_SHIFT, ls_out), (OUT_REDUCE_BIAS, rb_out),
    ):
        out[...] = small_ref[at, :]
    jb_out[0:width] = small_ref[OUT_BIAS_Q, :]
    jb_out[width:] = small_ref[OUT_BIAS_V, :]
    cw = eb_out.shape[0]
    mine = small_ref[pl.ds(OUT_EXPAND_BIAS + lax.axis_index("tensor"), 1), 0:cw]
    eb_out[...] = mine.reshape(cw)
    first_lane = 0
    for kernel_out, bias_out in ((sk_out, sb_out), (mk_out, mb_out), (lk_out, lb_out)):
        extent, count = kernel_out.shape[0], kernel_out.shape[2]
        span = slice(first_lane, first_lane + count)
        bias_out[...] = small_ref[OUT_BIAS_ALL, span]
        for a in range(extent):
            at = full_tap(extent, a, 0) - ROW_KERNEL_ALL + OUT_KERNEL_ALL
            kernel_out[a] = small_ref[at : at + extent, span]
        first_lane += count
    for a in range(3):
        at = TAIL_POS_KERNEL + 3 * a
        pk_out[a] = gtail_ref[at : at + 3, :]
    for at, out in ((TAIL_POS_BIAS, pb_out), (TAIL_EARLY_GAIN, eg_out), (TAIL_EARLY_SHIFT, es_out)):
        out[...] = gtail_ref[at, :]
    for copy in copies:
        copy.wait()


def per_device(
    block_input, position_kernel, position_bias, early_gain, early_shift, joint_weight, joint_bias,
    small_kernel, small_bias, middle_kernel, middle_bias, large_kernel, large_bias,
    output_weight, output_bias, late_gain, late_shift, expand_weight, expand_bias,
    reduce_weight, reduce_bias, cotangent,
):
    images, tokens, width = block_input.shape
    rows = images * tokens
    depth, copies_of = lax.axis_size("tensor"), lax.axis_size("dp")
    planes = math.gcd(copies_of // 2, 4)
    pieces = 2 * planes
    share, cw = width // depth, expand_weight.shape[1]
    unit = 16 * pieces
    sum_rows = padded(OUT_EXPAND_BIAS + depth, 16)
    shapes = [
        (padded(share, unit), width), (padded(width, unit), cw), (padded(cw, unit), width),
        (padded(share, unit), 2 * width), (padded(share, unit), width), (padded(sum_rows, unit), share),
    ]
    near, far = planes - 1, depth - 1
    copies = far + far * (2 + near) + 2 * far * 7 + 2 * depth * 6 + 2 + 4 * (1 + near) + 6 * far + 3 * far + 6 * near + 6
    copies += 1 + near + far
    fill = lambda array, count: jnp.pad(array, ((0, count - array.shape[0]), (0, 0)))
    vmem = lambda shape, dtype=bf16: pltpu.VMEM(shape, dtype)
    tail = (TAIL_ROWS, width)
    scratch = (
        [vmem((PARAM_ROWS, width), f32)]
        + [vmem((4, rows, LANES), f32)] * 10
        + [vmem((rows, width))] * 3 + [vmem((rows, 3 * width))]
        + [vmem((images, PAD_TOK, width))] * 4 + [vmem((images, 4, LANES, LANES))]
        + [vmem((sum_rows, 8, width), f32), vmem((TAIL_ROWS, 8, width), f32)]
        + [vmem((depth,) + shape) for shape in shapes[:3]] + [vmem((depth, 8, cw), f32)]
        + [vmem((depth,) + shape) for shape in shapes]
        + [vmem((depth, r // 2, w)) for r, w in shapes]
        + [vmem((near, depth, r // pieces, w)) for r, w in shapes[:1] + shapes[3:]]
        + [
            vmem(shape)
            for r, w in shapes[1:3]
            for shape in (
                (depth, 2, r // pieces, w // 2), (depth, 2 * r // pieces, w // 2),
                (depth, r // pieces, w // 2), (depth, r // pieces, w // 2), (r // 2, w),
            )
        ]
        + [vmem((far, r // pieces, w)) for r, w in shapes]
        + [vmem((3,) + tail), vmem((1,) + tail), vmem((near,) + tail), vmem((far,) + tail)]
        + [pltpu.SemaphoreType.DMA((copies,))] * 2 + [pltpu.SemaphoreType.DMA((3,))]
    )
    flat = lambda array: array.transpose(1, 0, 2).reshape(rows, width)
    anywhere = pl.BlockSpec(memory_space=pl.ANY)
    inside = pl.BlockSpec(memory_space=pltpu.VMEM)
    outs = [
        ((rows, width), bf16), ((rows, width), bf16),
        (shapes[0], bf16), (shapes[1], bf16), (shapes[2], bf16),
        ((depth,) + shapes[3], bf16), ((depth,) + shapes[4], bf16), ((depth,) + shapes[5], bf16), (tail, f32),
    ]
    made = pl.pallas_call(
        partial(whole_block, images, tokens, planes, depth),
        out_shape=[jax.ShapeDtypeStruct(shape, dtype) for shape, dtype in outs],
        in_specs=[inside] * 19 + [anywhere] * 3,
        out_specs=[inside] * len(outs),
        scratch_shapes=scratch,
        compiler_params=pltpu.CompilerParams(
            vmem_limit_bytes=VMEM_BYTES, collective_id=1, has_side_effects=True
        ),
    )(
        flat(block_input), flat(cotangent), joint_weight, position_kernel, position_bias, early_gain, early_shift,
        joint_bias, small_kernel, small_bias, middle_kernel, middle_bias, large_kernel, large_bias, output_bias,
        late_gain, late_shift, reduce_bias, expand_bias,
        fill(output_weight, shapes[0][0]), fill(expand_weight, shapes[1][0]), fill(reduce_weight, shapes[2][0]),
    )
    if copies_of > pieces:
        groups = [list(range(first, copies_of, pieces)) for first in range(pieces)]
        made = list(made[:2]) + list(lax.psum(tuple(made[2:]), "dp", axis_index_groups=groups))
    like = lambda array: jax.ShapeDtypeStruct(array.shape, f32)
    results = pl.pallas_call(
        write_out,
        out_shape=[jax.ShapeDtypeStruct((rows, width), bf16)] * 2 + [
            like(array) for array in (
                position_kernel, position_bias, early_gain, early_shift, joint_weight, joint_bias,
                small_kernel, small_bias, middle_kernel, middle_bias, large_kernel, large_bias,
                output_weight, output_bias, late_gain, late_shift, expand_weight, expand_bias,
                reduce_weight, reduce_bias,
            )
        ],
        in_specs=[inside] * 9,
        out_specs=[anywhere] * 2 + [inside] * 20,
        scratch_shapes=[pltpu.VMEM((shapes[5][0], width), f32), pltpu.SemaphoreType.DMA((2,))],
        compiler_params=pltpu.CompilerParams(vmem_limit_bytes=VMEM_BYTES),
    )(*made)
    image_form = lambda array: array.reshape(tokens, images, width).transpose(1, 0, 2)
    return (image_form(results[0]), image_form(results[1])) + tuple(results[2:])


def solution(mesh):
    images = P(("dp", "tensor"), None, None)
    in_specs = (images,) + (P(),) * 12 + (
        P("tensor", None), P(), P(), P(), P(None, "tensor"), P("tensor"), P("tensor", None), P(), images,
    )
    out_specs = (images, images) + (P(),) * 12 + (
        P("tensor", None), P(), P(), P(), P(None, "tensor"), P("tensor"), P("tensor", None), P(),
    )
    return jax.shard_map(per_device, mesh=mesh, in_specs=in_specs, out_specs=out_specs, check_vma=False)
```

```python
import math
from functools import partial

import jax
import jax.numpy as jnp
from jax import lax
from jax.experimental import pallas as pl
from jax.experimental.pallas import tpu as pltpu
from jax.sharding import PartitionSpec as P

HEADS = 8
HEAD = 64
GRID = 7
CELLS = GRID * GRID
NORM_EPS = 1e-06
SCALE = HEAD**-0.5
LANES = 128
GROUP = 256
PAD_TOK = 64
VMEM_BYTES = 62 * 1024 * 1024

f32 = jnp.float32
bf16 = jnp.bfloat16

ROW_POS_BIAS, ROW_EARLY_GAIN, ROW_EARLY_SHIFT, ROW_BIAS_Q, ROW_BIAS_V = 0, 1, 2, 3, 4
ROW_BIAS_ALL, ROW_OUT_BIAS, ROW_LATE_GAIN, ROW_LATE_SHIFT, ROW_REDUCE_BIAS = 5, 6, 7, 8, 9
ROW_POS_KERNEL, ROW_KERNEL_ALL = 10, 19
PARAM_ROWS = 72

OUT_KERNEL_ALL, OUT_BIAS_Q, OUT_BIAS_V, OUT_BIAS_ALL = 0, 49, 50, 51
OUT_LATE_GAIN, OUT_LATE_SHIFT, OUT_OUT_BIAS, OUT_REDUCE_BIAS, OUT_EXPAND_BIAS = 52, 53, 54, 55, 56
TAIL_POS_KERNEL, TAIL_POS_BIAS, TAIL_EARLY_GAIN, TAIL_EARLY_SHIFT, TAIL_ROWS = 0, 9, 10, 11, 16
MESH = pl.DeviceIdType.MESH


def lane(tile):
    if isinstance(tile, int):
        return slice(tile * LANES, (tile + 1) * LANES)
    return pl.ds(pl.multiple_of(tile * LANES, LANES), LANES)


def taps(extent):
    return range(extent)


def columns(shift):
    return range(max(0, -shift), min(GRID, GRID - shift))


def depthwise_rows(get_row, get_weight, extent, flip, emit):
    margin = extent // 2
    for i in range(GRID):
        total = [None] * GRID
        for a in range(extent):
            r = i + a - margin
            if not 0 <= r < GRID:
                continue
            row = get_row(r)
            for b in range(extent):
                weight = get_weight((extent - 1 - a, extent - 1 - b) if flip else (a, b))
                for j in columns(b - margin):
                    term = row[j + b - margin] * weight
                    total[j] = term if total[j] is None else total[j] + term
        emit(i, total)


def kernel_grads(get_left, get_right, extent, emit):
    margin = extent // 2
    for a in range(extent):
        total = [None] * extent
        for i in range(GRID):
            r = i + a - margin
            if not 0 <= r < GRID:
                continue
            left, right = get_left(i), get_right(r)
            for b in range(extent):
                for j in columns(b - margin):
                    term = left[j] * right[j + b - margin]
                    total[b] = term if total[b] is None else total[b] + term
        for b in range(extent):
            emit(a, b, total[b])


def cell_rows(images, cell, count=1):
    return slice((1 + cell) * images, (1 + cell + count) * images)


def grid_row(ref, tile, images, i):
    block = ref[tile, cell_rows(images, i * GRID, GRID), :]
    return [block[j * images : (j + 1) * images] for j in range(GRID)]


def full_tap(extent, a, b):
    extra = (GRID - extent) // 2
    return ROW_KERNEL_ALL + (a + extra) * GRID + b + extra


def narrow_tiles(body):
    body(0, 3)
    body(1, 5)


def wide_tiles(body):
    def rest(tile, carry):
        body(tile, 7)
        return carry

    lax.fori_loop(2, 4, rest, 0)


def normalise(block):
    centre = jnp.mean(block, axis=-1, keepdims=True)
    centred = block - centre
    spread = jnp.mean(centred * centred, axis=-1, keepdims=True)
    scale = lax.rsqrt(spread + NORM_EPS)
    return centred * scale, scale


def normalise_back(grad, gain, unit, scale):
    scaled = grad * gain
    mean_one = jnp.mean(scaled, axis=-1, keepdims=True)
    mean_two = jnp.mean(scaled * unit, axis=-1, keepdims=True)
    return (scaled - mean_one - unit * mean_two) * scale


def fold_rows(block):
    return jnp.sum(block.reshape(block.shape[0] // 8, 8, block.shape[1]), axis=0)


def dot(left, right, left_dim=1, right_dim=0):
    return lax.dot_general(
        left, right, (((left_dim,), (right_dim,)), ((), ())), preferred_element_type=f32
    )


def padded(count, unit):
    return -(-count // unit) * unit


class Ring:
    def __init__(self, pairs, depth, send_sems, recv_sems):
        self.dp = lax.axis_index("dp")
        self.me = lax.axis_index("tensor")
        self.planes, self.depth = pairs, depth
        group = 2 * pairs
        self.base = lax.div(self.dp, group) * group
        self.core = lax.rem(self.dp, 2)
        self.spot = lax.div(lax.rem(self.dp, group), 2)
        self.send_sems, self.recv_sems, self.used = send_sems, recv_sems, 0
        self.sent = []

    def twin(self):
        return {"dp": self.base + self.spot * 2 + (1 - self.core), "tensor": self.me}

    def plane(self, k):
        return {"dp": self.base + lax.rem(self.spot + k, self.planes) * 2 + self.core, "tensor": self.me}

    def plane_spot(self, k):
        return lax.rem(self.spot + k, self.planes)

    def across(self, k):
        return {"dp": self.base + self.beside(k) * 2 + self.core, "tensor": self.me}

    def beside(self, k):
        low, high = lax.rem(self.spot, 2), lax.div(self.spot, 2)
        return high * 2 + 1 - low if k == 1 else (1 - high) * 2 + low

    def stack(self, k):
        return {"dp": self.dp, "tensor": lax.rem(self.me + k, self.depth)}

    def everyone(self):
        return (
            [self.twin()]
            + [self.plane(k) for k in range(1, self.planes)]
            + [self.stack(k) for k in range(1, self.depth)]
        )

    def piece(self, rows, spot, core=None):
        each = rows // (2 * self.planes)
        core = self.core if core is None else core
        return pl.ds(pl.multiple_of((core * self.planes + spot) * each, each), each)

    def band(self, rows, high):
        each = rows // (2 * self.planes)
        start = (self.core * self.planes + high * 2) * each
        return pl.ds(pl.multiple_of(start, 2 * each), 2 * each)

    def half(self, rows, core):
        return pl.ds(pl.multiple_of(core * (rows // 2), rows // 2), rows // 2)

    def send(self, source, target, device):
        at = self.used
        self.used += 1
        copy = pltpu.make_async_remote_copy(
            src_ref=source, dst_ref=target, send_sem=self.send_sems.at[at], recv_sem=self.recv_sems.at[at],
            device_id=device, device_id_type=MESH,
        )
        copy.start()
        self.sent.append(copy)
        return copy


def arrive(copies):
    for copy in copies:
        copy.wait_recv()


class Reduction:
    def __init__(self, ring, grads, twin_box, plane_box, stack_box, out, whole, relative):
        self.ring, self.grads, self.out, self.whole, self.relative = ring, grads, out, whole, relative
        self.twin_box, self.plane_box, self.stack_box = twin_box, plane_box, stack_box
        self.rows = grads.shape[1]
        self.depth = grads.shape[0]
        self.pairs, self.planes, self.stacks = {}, {}, {}
        self.all = slice(0, self.depth)

    def slot(self, k):
        return k if self.relative else lax.rem(self.ring.me + k, self.depth)

    def pair(self, part):
        ring = self.ring
        away = ring.half(self.rows, 1 - ring.core)
        self.pairs[str(part)] = ring.send(self.grads.at[part, away], self.twin_box.at[part], ring.twin())

    def meet(self, part):
        ring = self.ring
        arrive([self.pairs[str(part)]])
        mine = ring.half(self.rows, ring.core)
        self.grads[part, mine] = (
            self.grads[part, mine].astype(f32) + self.twin_box[part].astype(f32)
        ).astype(bf16)

    def plane(self, part):
        ring = self.ring
        self.meet(part)
        self.planes[str(part)] = [
            ring.send(
                self.grads.at[part, ring.piece(self.rows, ring.plane_spot(k))],
                self.plane_box.at[k - 1, part], ring.plane(k),
            )
            for k in range(1, ring.planes)
        ]

    def gather_plane(self, part):
        ring = self.ring
        arrive(self.planes[str(part)])
        mine = ring.piece(self.rows, ring.spot)
        total = self.grads[part, mine].astype(f32)
        for k in range(1, ring.planes):
            total = total + self.plane_box[k - 1, part].astype(f32)
        self.grads[part, mine] = total.astype(bf16)

    def stack(self, offsets=None):
        ring = self.ring
        mine = ring.piece(self.rows, ring.spot)
        for k in range(1, self.depth) if offsets is None else offsets:
            self.stacks[k] = ring.send(self.grads.at[self.slot(k), mine], self.stack_box.at[k - 1], ring.stack(k))

    def settle(self):
        ring = self.ring
        arrive(self.stacks.values())
        mine = ring.piece(self.rows, ring.spot)
        total = self.grads[self.slot(0), mine].astype(f32)
        for k in self.stacks:
            total = total + self.stack_box[k - 1].astype(f32)
        done = total.astype(bf16)
        if self.whole:
            self.out[ring.me, mine] = done
            place = self.out.at[ring.me, mine]
            self.spread = [ring.send(place, place, ring.stack(k)) for k in range(1, self.depth)]
        else:
            self.out[mine] = done
            self.to_plane()

    def to_plane(self):
        ring = self.ring
        mine = ring.piece(self.rows, ring.spot)
        if self.whole:
            arrive(self.spread)
            place = self.out.at[:, mine]
        else:
            place = self.out.at[mine]
        self.back = [ring.send(place, place, ring.plane(k)) for k in range(1, ring.planes)]

    def to_twin(self):
        ring = self.ring
        arrive(self.back)
        mine = ring.half(self.rows, ring.core)
        place = self.out.at[:, mine] if self.whole else self.out.at[mine]
        self.last = ring.send(place, place, ring.twin())

    def finish(self):
        arrive([self.last])


class TwoPhase(Reduction):
    def __init__(self, ring, grads, twin_box, plane_boxes, stack_box, out, whole, relative):
        super().__init__(ring, grads, twin_box, None, stack_box, out, whole, relative)
        self.first_box, self.band_box, self.low_box, self.high_box = plane_boxes
        self.cut = grads.shape[2] // 2
        self.ones, self.twos = {}, {}

    def add(self, part, at, columns, box):
        self.grads[part, at, columns] = (self.grads[part, at, columns].astype(f32) + box.astype(f32)).astype(bf16)

    def phase_one(self, part):
        ring = self.ring
        self.meet(part)
        left, right = slice(0, self.cut), slice(self.cut, 2 * self.cut)
        low, high = lax.rem(ring.spot, 2), lax.div(ring.spot, 2)
        self.ones[str(part)] = [
            ring.send(
                self.grads.at[part, ring.piece(self.rows, 2 * y + 1 - low), left],
                self.first_box.at[part, y], ring.across(1),
            )
            for y in range(2)
        ] + [
            ring.send(
                self.grads.at[part, ring.band(self.rows, 1 - high), right], self.band_box.at[part], ring.across(2)
            )
        ]

    def phase_two(self, part):
        ring = self.ring
        left, right = slice(0, self.cut), slice(self.cut, 2 * self.cut)
        low, high = lax.rem(ring.spot, 2), lax.div(ring.spot, 2)
        arrive(self.ones[str(part)])
        for y in range(2):
            self.add(part, ring.piece(self.rows, 2 * y + low), left, self.first_box[part, y])
        self.add(part, ring.band(self.rows, high), right, self.band_box[part])
        self.twos[str(part)] = [
            ring.send(
                self.grads.at[part, ring.piece(self.rows, ring.beside(2)), left], self.high_box.at[part], ring.across(2)
            ),
            ring.send(
                self.grads.at[part, ring.piece(self.rows, ring.beside(1)), right], self.low_box.at[part], ring.across(1)
            ),
        ]

    def to_plane(self):
        if self.whole:
            super().to_plane()
            return
        ring = self.ring
        mine = ring.piece(self.rows, ring.spot)
        left, right = self.out.at[mine, 0 : self.cut], self.out.at[mine, self.cut : 2 * self.cut]
        self.ahead = [ring.send(left, left, ring.across(2)), ring.send(right, right, ring.across(1))]

    def to_plane_two(self):
        ring = self.ring
        arrive(self.ahead)
        low, high = lax.rem(ring.spot, 2), lax.div(ring.spot, 2)
        places = [self.out.at[ring.piece(self.rows, 2 * y + low), 0 : self.cut] for y in range(2)]
        band = self.out.at[ring.band(self.rows, high), self.cut : 2 * self.cut]
        self.back = [ring.send(place, place, ring.across(1)) for place in places]
        self.back.append(ring.send(band, band, ring.across(2)))

    def gather_plane(self, part):
        ring = self.ring
        arrive(self.twos[str(part)])
        mine = ring.piece(self.rows, ring.spot)
        self.add(part, mine, slice(0, self.cut), self.high_box[part])
        self.add(part, mine, slice(self.cut, 2 * self.cut), self.low_box[part])


class StackFirst(Reduction):
    def __init__(self, ring, grads, twin_box, near_box, half_box, out):
        super().__init__(ring, grads, twin_box, near_box, None, out, True, False)
        self.half_box = half_box

    def climb(self):
        ring = self.ring
        self.meet(self.all)
        mine = ring.half(self.rows, ring.core)
        self.climbs = [
            ring.send(self.grads.at[self.slot(k), mine], self.half_box.at[k - 1], ring.stack(k))
            for k in range(1, self.depth)
        ]

    def across(self):
        ring = self.ring
        arrive(self.climbs)
        mine = ring.half(self.rows, ring.core)
        total = self.grads[ring.me, mine].astype(f32)
        for k in range(1, self.depth):
            total = total + self.half_box[k - 1].astype(f32)
        self.grads[ring.me, mine] = total.astype(bf16)
        self.over = [
            ring.send(
                self.grads.at[ring.me, ring.piece(self.rows, ring.plane_spot(k))], self.plane_box.at[k - 1], ring.plane(k)
            )
            for k in range(1, ring.planes)
        ]

    def settle(self):
        ring = self.ring
        arrive(self.over)
        mine = ring.piece(self.rows, ring.spot)
        total = self.grads[ring.me, mine].astype(f32)
        for k in range(1, ring.planes):
            total = total + self.plane_box[k - 1].astype(f32)
        self.out[ring.me, mine] = total.astype(bf16)
        place = self.out.at[ring.me, mine]
        self.spread = [ring.send(place, place, ring.plane(k)) for k in range(1, ring.planes)]

    def descend(self):
        ring = self.ring
        arrive(self.spread)
        place = self.out.at[ring.me, ring.half(self.rows, ring.core)]
        self.back = [ring.send(place, place, ring.stack(k)) for k in range(1, self.depth)]


class Gather:
    def __init__(self, ring, shard, box, relative):
        self.ring, self.shard, self.box, self.relative = ring, shard, box, relative
        self.depth, self.rows = box.shape[0], box.shape[1]
        self.first, self.second, self.third = {}, {}, {}

    def slot(self, j):
        return j if self.relative else lax.rem(self.ring.me + j, self.depth)

    def start(self, j):
        ring = self.ring
        mine = ring.piece(self.rows, ring.spot)
        target = self.box.at[j if self.relative else ring.me, mine]
        self.first[j] = ring.send(self.shard.at[mine], target, ring.stack(self.depth - j))

    def plane(self, j):
        ring = self.ring
        arrive([self.first[j]])
        place = self.box.at[self.slot(j), ring.piece(self.rows, ring.spot)]
        self.second[j] = [ring.send(place, place, ring.plane(k)) for k in range(1, ring.planes)]

    def pair(self, j):
        ring = self.ring
        arrive(self.second[j])
        place = self.box.at[self.slot(j), ring.half(self.rows, ring.core)]
        self.third[j] = ring.send(place, place, ring.twin())

    def finish(self, j):
        arrive([self.third[j]])


class Tail:
    def __init__(self, ring, mine, boxes):
        self.ring, self.mine, self.boxes = ring, mine, boxes

    def start(self, stage):
        ring = self.ring
        devices = (
            [ring.twin()],
            [ring.plane(k) for k in range(1, ring.planes)],
            [ring.stack(k) for k in range(1, ring.depth)],
        )[stage]
        self.copies = [
            ring.send(self.mine.at[stage], self.boxes[stage].at[k], device) for k, device in enumerate(devices)
        ]

    def collect(self, stage):
        total = self.mine[stage].astype(f32)
        for k, copy in enumerate(self.copies):
            copy.wait_recv()
            total = total + self.boxes[stage][k].astype(f32)
        if stage < 2:
            self.mine[stage + 1] = total.astype(bf16)
            self.start(stage + 1)
        return total


def each(parts, step_name, *args):
    for part in parts:
        getattr(part, step_name)(*args)


def wide(ref, at):
    return jnp.concatenate([ref[tile, at, :] for tile in range(4)], axis=1)


def put_wide(ref, at, block):
    for tile in range(4):
        ref[tile, at, :] = block[:, lane(tile)]


def whole_block(
    images, tokens, planes, depth, *refs,
):
    given, refs = refs[:22], refs[22:]
    results, refs = refs[:10], refs[10:]
    held, refs = refs[:19], refs[19:]
    boxes, refs = refs[:10], refs[10:]
    (
        x_ref, cot_ref, wj_ref, pk_ref, pb_ref, eg_ref, es_ref, jb_ref, sk_ref, sb_ref, mk_ref, mb_ref,
        lk_ref, lb_ref, ob_ref, lg_ref, ls_ref, rb_ref, eb_shard,
    ) = held
    wo_shard, we_shard, wr_shard = given[19:]
    y_ref, dx_ref, gwo_ref, gwe_ref, gwr_ref, gwq_ref, gwk_ref, gwv_ref, gsm_ref, gtail_ref = boxes
    (
        prm_ref, x1_ref, x2_ref, q_ref, v_ref, ks_ref, conv_ref, fac_ref, one_ref, two_ref, three_ref,
        h1_ref, att_ref, h2_ref, raw_ref,
        qi_ref, ki_ref, vi_ref, dai_ref, ctx_ref, sums_ref, last_ref,
        wo_ref, we_ref, wr_ref, eb_ref,
        go_ref, ge_ref, gr_ref, gq_ref, gk_ref, gv_ref, gs_ref,
        to_ref, te_ref, tr_ref, tq_ref, tk_ref, tv_ref, ts_ref,
        po_ref, pk2_ref, pv_ref, ps_ref,
        e_first, e_band, e_low, e_high, r_first, r_band, r_low, r_high,
        q_near, q_half,
        so_ref, se_ref, sr_ref, sq_ref, sk2_ref, sv_ref, ss_ref,
        tail_ref, tail_pair, tail_plane, tail_stack,
        send_sems, recv_sems, local_sems,
    ) = refs
    ring = Ring(planes, depth, send_sems, recv_sems)
    barrier = pltpu.get_barrier_semaphore()
    for device in ring.everyone():
        pl.semaphore_signal(barrier, inc=1, device_id=device, device_id_type=MESH)

    rows = images * tokens
    width = 4 * LANES
    step = 5 * images
    steps = rows // step
    share = width // depth
    cw = we_ref.shape[2]
    get_out = Gather(ring, wo_shard, wo_ref, False)
    get_expand = Gather(ring, we_shard, we_ref, True)
    get_reduce = Gather(ring, wr_shard, wr_ref, True)
    feed_in = (get_expand, get_reduce)
    slots = range(1, depth)
    used = []

    def local(source, target):
        copy = pltpu.make_async_copy(source, target, local_sems.at[len(used)])
        copy.start()
        used.append(copy)
        return copy

    loads = [local(source, target) for source, target in zip(given, held)]
    pl.semaphore_wait(barrier, planes + depth - 1)
    order = list(slots)
    for j in slots:
        get_out.start(j)
    for part in feed_in:
        part.start(order[0])
    own = [
        local(source, target)
        for source, target in ((wo_shard, wo_ref.at[ring.me]), (we_shard, we_ref.at[0]), (wr_shard, wr_ref.at[0]))
    ]
    for copy in [loads[0]] + loads[3:]:
        copy.wait()
    eb_ref[0] = jnp.broadcast_to(eb_shard[...].astype(f32).reshape(1, cw), (8, cw))

    get_bias = [ring.send(eb_ref.at[0], eb_ref.at[j], ring.stack(depth - j)) for j in slots]

    for at, ref in (
        (ROW_POS_BIAS, pb_ref), (ROW_EARLY_GAIN, eg_ref), (ROW_EARLY_SHIFT, es_ref), (ROW_OUT_BIAS, ob_ref),
        (ROW_LATE_GAIN, lg_ref), (ROW_LATE_SHIFT, ls_ref), (ROW_REDUCE_BIAS, rb_ref),
    ):
        prm_ref[at : at + 1, :] = ref[...].astype(f32).reshape(1, width)
    prm_ref[ROW_BIAS_Q : ROW_BIAS_Q + 1, :] = jb_ref[0:width].astype(f32).reshape(1, width)
    prm_ref[ROW_BIAS_V : ROW_BIAS_V + 1, :] = jb_ref[width : 2 * width].astype(f32).reshape(1, width)
    prm_ref[ROW_KERNEL_ALL:PARAM_ROWS, :] = jnp.zeros((PARAM_ROWS - ROW_KERNEL_ALL, width), f32)
    first_lane = 0
    for kernel_ref, bias_ref in ((sk_ref, sb_ref), (mk_ref, mb_ref), (lk_ref, lb_ref)):
        extent, count = kernel_ref.shape[0], kernel_ref.shape[2]
        span = slice(first_lane, first_lane + count)
        prm_ref[ROW_BIAS_ALL : ROW_BIAS_ALL + 1, span] = bias_ref[...].astype(f32).reshape(1, count)
        for a in range(extent):
            at = full_tap(extent, a, 0)
            prm_ref[at : at + extent, span] = kernel_ref[a].astype(f32)
        first_lane += count
    for a in range(3):
        prm_ref[ROW_POS_KERNEL + 3 * a : ROW_POS_KERNEL + 3 * a + 3, :] = pk_ref[a].astype(f32)

    prm = lambda row, tile: prm_ref[row : row + 1, lane(tile)]
    row = lambda r: prm_ref[r : r + 1, :]
    block_at = lambda k: pl.ds(pl.multiple_of(k * step, step), step)

    x_row = lambda tile, i: [
        x_ref[cell_rows(images, i * GRID + j), lane(tile)].astype(f32) for j in range(GRID)
    ]

    def position(tile, carry):
        x1_ref[tile, 0:images, :] = x_ref[0:images, lane(tile)].astype(f32)
        bias = prm(ROW_POS_BIAS, tile)

        def emit(i, total):
            here = x_row(tile, i)
            for j in range(GRID):
                x1_ref[tile, cell_rows(images, i * GRID + j), :] = here[j] + total[j] + bias

        depthwise_rows(
            partial(x_row, tile), lambda ab: prm(ROW_POS_KERNEL + ab[0] * 3 + ab[1], tile), 3, False, emit
        )
        return carry

    lax.fori_loop(0, 4, position, 0)
    for j in order[1:2]:
        each(feed_in, "start", j)

    def norm_of(source, target, gain, shift):
        def norm(k, carry):
            at = block_at(k)
            unit, _ = normalise(wide(source, at))
            target[at, :] = (unit * gain + shift).astype(bf16)
            return carry

        lax.fori_loop(0, steps, norm, 0)

    gain_one, shift_one = row(ROW_EARLY_GAIN), row(ROW_EARLY_SHIFT)
    norm_of(x1_ref, h1_ref, gain_one, shift_one)
    every = slice(0, rows)
    loads[2].wait()
    put_wide(v_ref, every, (dot(h1_ref[...], wj_ref[:, 2 * width :]) + row(ROW_BIAS_V)).astype(bf16).astype(f32))
    put_wide(ks_ref, every, dot(h1_ref[...], wj_ref[:, width : 2 * width]).astype(bf16).astype(f32))
    put_wide(q_ref, every, (dot(h1_ref[...], wj_ref[:, :width]) + row(ROW_BIAS_Q)).astype(bf16).astype(f32))
    for j in slots:
        get_out.plane(j)
    for j in order[2:]:
        each(feed_in, "start", j)

    token = lambda n: slice(n * images, (n + 1) * images)

    def soften(tile, carry):
        top = ks_ref[tile, token(0), :]
        for n in range(1, tokens):
            top = jnp.maximum(top, ks_ref[tile, token(n), :])
        total = jnp.zeros_like(top)
        for n in range(tokens):
            e = jnp.exp(ks_ref[tile, token(n), :] - top)
            ks_ref[tile, token(n), :] = e
            total = total + e
        scale = 1.0 / total
        for n in range(tokens):
            ks_ref[tile, token(n), :] = ks_ref[tile, token(n), :] * scale
        return carry

    lax.fori_loop(0, 4, soften, 0)
    each(feed_in, "plane", order[0])

    def convolve(tile, extent):
        conv_ref[tile, 0:images, :] = jnp.zeros((images, LANES), f32)
        bias = prm(ROW_BIAS_ALL, tile)

        def emit(i, total):
            for j in range(GRID):
                conv_ref[tile, cell_rows(images, i * GRID + j), :] = total[j] + bias

        depthwise_rows(
            partial(grid_row, v_ref, tile, images), lambda ab: prm(full_tap(extent, *ab), tile),
            extent, False, emit,
        )

    narrow_tiles(convolve)
    wide_tiles(convolve)
    for j in slots:
        get_out.pair(j)

    some = images // 4
    lanes_of = lax.broadcasted_iota(jnp.int32, (LANES, LANES), 1) // HEAD
    rows_of = lax.broadcasted_iota(jnp.int32, (LANES, LANES), 0) // HEAD
    pair_mask = jnp.where(lanes_of == rows_of, 1.0, 0.0)
    here = lambda b: pl.ds(b, tokens, stride=images)

    def per_image(source, target, b):
        target[b, 48:PAD_TOK, :] = jnp.zeros((PAD_TOK - 48, width), bf16)
        for tile in range(4):
            target[b, 0:tokens, lane(tile)] = source[tile, here(b), :].astype(bf16)

    def image(g, carry):
        batch = [g * some + u for u in range(some)]
        for b in batch:
            for source, target in ((ks_ref, ki_ref), (v_ref, vi_ref), (q_ref, qi_ref)):
                per_image(source, target, b)
        for b in batch:
            for t in range(4):
                full = dot(ki_ref[b, :, lane(t)], vi_ref[b, :, lane(t)], 0, 0)
                ctx_ref[b, t] = (full * pair_mask).astype(bf16)
        for b in batch:
            for t in range(4):
                out = dot(qi_ref[b, :, lane(t)], ctx_ref[b, t]) * SCALE
                fac_ref[t, here(b), :] = out[0:tokens]
        return carry

    for g in range(4):
        lax.fori_loop(g, g + 1, image, 0)

    def combine(tile, carry):
        att_ref[:, lane(tile)] = (fac_ref[tile] + q_ref[tile] * conv_ref[tile]).astype(bf16)
        return carry

    lax.fori_loop(0, 4, combine, 0)

    loads[1].wait()
    for copy in own:
        copy.wait()
    for j in slots:
        get_out.finish(j)
    whole_out = jnp.concatenate([wo_ref[t, 0:share, :] for t in range(depth)], axis=0)
    branch = dot(att_ref[...], whole_out) + row(ROW_OUT_BIAS)
    for tile in range(4):
        x2_ref[tile] = x1_ref[tile] + branch[:, lane(tile)]
    gain_two, shift_two = row(ROW_LATE_GAIN), row(ROW_LATE_SHIFT)
    norm_of(x2_ref, h2_ref, gain_two, shift_two)
    for j in order[1:2]:
        each(feed_in, "plane", j)

    e_boxes, r_boxes = (e_first, e_band, e_low, e_high), (r_first, r_band, r_low, r_high)
    send_expand = TwoPhase(ring, ge_ref, te_ref, e_boxes, se_ref, gwe_ref, False, True)
    send_reduce = TwoPhase(ring, gr_ref, tr_ref, r_boxes, sr_ref, gwr_ref, False, True)
    send_out = Reduction(ring, go_ref, to_ref, po_ref, so_ref, gwo_ref, False, False)
    send_q = StackFirst(ring, gq_ref, tq_ref, q_near, q_half, gwq_ref)
    send_k = Reduction(ring, gk_ref, tk_ref, pk2_ref, sk2_ref, gwk_ref, True, False)
    send_v = Reduction(ring, gv_ref, tv_ref, pv_ref, sv_ref, gwv_ref, True, False)
    send_small = Reduction(ring, gs_ref, ts_ref, ps_ref, ss_ref, gsm_ref, True, False)
    feed = (send_expand, send_reduce)

    def feed_stack(c):
        for part in feed:
            part.gather_plane(c)
            if c >= 1:
                part.stack([c])

    acc_ref, dh2_ref = one_ref, two_ref
    hid_ref, dpre_ref = raw_ref.at[:, 0:cw], raw_ref.at[:, width : width + cw]
    datt_ref = raw_ref.at[:, 2 * width : 3 * width]
    half = rows // 2
    sums_ref[...] = jnp.zeros_like(sums_ref)
    arrive(get_bias)
    chunks = [0] + order
    for at_chunk, c in enumerate(chunks):
        if at_chunk >= 1:
            each(feed_in, "finish", c)
        bias = eb_ref[c, 0:1, :]
        folded = jnp.zeros((8, cw), f32)
        we, wr = we_ref[c], wr_ref[c, 0:cw, :]
        for k in range(2):
            at = slice(k * half, (k + 1) * half)
            pre = dot(h2_ref[at, :], we) + bias
            dh = dot(cot_ref[at, :], wr, 1, 1)
            gauss = jnp.exp(pre * pre * -0.5)
            t = 1.0 / (1.0 + (0.3275911 * 0.7071067811865476) * jnp.abs(pre))
            poly = t * (0.127414796 + t * (-0.142248368 + t * (0.7107068705 + t * (-0.7265760135 + t * 0.5307027145))))
            tail = poly * gauss
            cdf = jnp.where(pre >= 0, 1.0 - tail, tail)
            hid_ref[at, :] = (pre * cdf).astype(bf16)
            dpre = ((cdf + pre * gauss * 0.3989422804014327) * dh).astype(bf16)
            dpre_ref[at, :] = dpre
            folded = folded + fold_rows(dpre.astype(f32))
            if at_chunk == 0 and k == 0:
                each(feed_in, "pair", order[0])
                for j in order[2:]:
                    each(feed_in, "plane", j)
            if at_chunk == 1 and k == 1:
                for j in order[1:2]:
                    each(feed_in, "pair", j)
            if at_chunk == 2 and k == 1:
                for j in order[2:]:
                    each(feed_in, "pair", j)
            if k == 0 and at_chunk >= 1:
                each(feed, "phase_one", chunks[at_chunk - 1])
            if k == 0 and at_chunk >= 2:
                each(feed, "phase_two", chunks[at_chunk - 2])
            if k == 1 and at_chunk >= 3:
                feed_stack(chunks[at_chunk - 3])
        sums_ref[OUT_EXPAND_BIAS + lax.rem(ring.me + c, depth), :, 0:cw] = folded
        ge_ref[c] = dot(h2_ref[...], dpre_ref[...], 0, 0).astype(bf16)
        gr_ref[c, 0:cw] = dot(hid_ref[...], cot_ref[...], 0, 0).astype(bf16)
        if gr_ref.shape[1] > cw:
            gr_ref[c, cw:] = jnp.zeros((gr_ref.shape[1] - cw, width), bf16)
        for part in feed:
            part.pair(c)
        out = dot(hid_ref[...], wr)
        back = dot(dpre_ref[...], we, 1, 1)
        for tile in range(4):
            if at_chunk == 0:
                acc_ref[tile] = out[:, lane(tile)]
                dh2_ref[tile] = back[:, lane(tile)]
            else:
                acc_ref[tile] += out[:, lane(tile)]
                dh2_ref[tile] += back[:, lane(tile)]

    def finish(k, carry):
        at = block_at(k)
        x2 = wide(x2_ref, at)
        y_ref[at, :] = (x2 + wide(acc_ref, at) + row(ROW_REDUCE_BIAS)).astype(bf16)
        unit, scale = normalise(x2)
        grad = wide(dh2_ref, at)
        dy = cot_ref[at, :].astype(f32)
        dx2 = dy + normalise_back(grad, gain_two, unit, scale)
        put_wide(x2_ref, at, dx2)
        low = dx2.astype(bf16)
        datt_ref[at, :] = low
        return (
            carry[0] + fold_rows(grad * unit), carry[1] + fold_rows(grad),
            carry[2] + fold_rows(low.astype(f32)), carry[3] + fold_rows(dy),
        )

    zero = jnp.zeros((8, width), f32)
    sums = lax.fori_loop(0, steps, finish, (zero,) * 4)
    written = [local(y_ref, results[0])]
    for r, total in zip((OUT_LATE_GAIN, OUT_LATE_SHIFT, OUT_OUT_BIAS, OUT_REDUCE_BIAS), sums):
        sums_ref[r] = total
    each(feed, "phase_one", chunks[-1])
    if depth > 1:
        each(feed, "phase_two", chunks[-2])
    if depth > 2:
        feed_stack(chunks[-3])
    grad_out = dot(att_ref[...], datt_ref[...], 0, 0).astype(bf16)
    for t in range(depth):
        go_ref[t, 0:share, :] = grad_out[t * share : (t + 1) * share, :]
        if go_ref.shape[1] > share:
            go_ref[t, share:, :] = jnp.zeros((go_ref.shape[1] - share, width), bf16)
    send_out.pair(send_out.all)
    grad_att = dot(datt_ref[...], whole_out, 1, 1).astype(bf16).astype(f32)
    da_ref, dq_ref, dk_ref, dv_ref = fac_ref, one_ref, two_ref, three_ref
    put_wide(da_ref, every, grad_att)

    def image_back(g, carry):
        batch = [g * some + u for u in range(some)]
        scaled = pair_mask * SCALE
        for b in batch:
            per_image(da_ref, dai_ref, b)
        for b in batch:
            for t in range(4):
                dq = dot(dai_ref[b, :, lane(t)], ctx_ref[b, t], 1, 1) * SCALE
                dq_ref[t, here(b), :] = dq[0:tokens]
        for b in batch:
            for t in range(4):
                full = dot(qi_ref[b, :, lane(t)], dai_ref[b, :, lane(t)], 0, 0)
                ctx_ref[b, t] = (full * scaled).astype(bf16)
        for b in batch:
            for t in range(4):
                dk = dot(vi_ref[b, :, lane(t)], ctx_ref[b, t], 1, 1)
                dk_ref[t, here(b), :] = dk[0:tokens]
                dv = dot(ki_ref[b, :, lane(t)], ctx_ref[b, t])
                dv_ref[t, here(b), :] = dv[0:tokens]
        return carry

    for g in range(4):
        lax.fori_loop(g, g + 1, image_back, 0)
        if g == 2:
            send_out.plane(send_out.all)
        if g == 3:
            each(feed, "phase_two", chunks[-1])
            if depth > 1:
                feed_stack(chunks[-2])

    def split(tile, carry):
        bias_q = jnp.zeros((images, LANES), f32)
        bias_all = jnp.zeros((images, LANES), f32)
        dot_sum = jnp.zeros((images, LANES), f32)
        for n in range(tokens):
            grad = da_ref[tile, token(n), :]
            dq = (dq_ref[tile, token(n), :] + grad * conv_ref[tile, token(n), :]).astype(bf16)
            raw_ref[token(n), lane(tile)] = dq
            bias_q = bias_q + dq.astype(f32)
            dc = grad * q_ref[tile, token(n), :]
            da_ref[tile, token(n), :] = dc
            if n > 0:
                bias_all = bias_all + dc
            dot_sum = dot_sum + dk_ref[tile, token(n), :] * ks_ref[tile, token(n), :]
        for n in range(tokens):
            soft = ks_ref[tile, token(n), :]
            raw_ref[token(n), lane(tile + 4)] = (soft * (dk_ref[tile, token(n), :] - dot_sum)).astype(bf16)
        sums_ref[OUT_BIAS_Q, :, lane(tile)] = fold_rows(bias_q)
        sums_ref[OUT_BIAS_ALL, :, lane(tile)] = fold_rows(bias_all)
        return carry

    lax.fori_loop(0, 4, split, 0)

    def grad_joint(target, part):
        grad = dot(h1_ref[...], raw_ref[:, part * width : (part + 1) * width], 0, 0).astype(bf16)
        for t in range(depth):
            target[t, 0:share, :] = grad[t * share : (t + 1) * share, :]
            if target.shape[1] > share:
                target[t, share:, :] = jnp.zeros((target.shape[1] - share, width), bf16)

    grad_joint(gq_ref, 0)
    send_q.pair(send_q.all)
    grad_joint(gk_ref, 1)
    send_k.pair(send_k.all)
    def values_back(tile, extent):
        first = dv_ref[tile, token(0), :].astype(bf16)
        raw_ref[token(0), lane(tile + 8)] = first
        bias_v = [first.astype(f32)]

        def emit(i, total):
            for j in range(GRID):
                here = cell_rows(images, i * GRID + j)
                dv = (dv_ref[tile, here, :] + total[j]).astype(bf16)
                raw_ref[here, lane(tile + 8)] = dv
                bias_v[0] = bias_v[0] + dv.astype(f32)

        depthwise_rows(
            partial(grid_row, da_ref, tile, images), lambda ab: prm(full_tap(extent, *ab), tile),
            extent, True, emit,
        )
        sums_ref[OUT_BIAS_V, :, lane(tile)] = fold_rows(bias_v[0])

    narrow_tiles(values_back)
    send_q.climb()
    wide_tiles(values_back)
    send_k.plane(send_k.all)
    feed_stack(chunks[-1])
    send_out.gather_plane(send_out.all)
    send_out.stack()
    grad_joint(gv_ref, 2)
    send_v.pair(send_v.all)

    def tap_grads(tile, extent):
        extra = (GRID - extent) // 2

        def emit_tap(a, b, total):
            sums_ref[OUT_KERNEL_ALL + (a + extra) * GRID + b + extra, :, lane(tile)] = fold_rows(total)

        kernel_grads(
            partial(grid_row, da_ref, tile, images), partial(grid_row, v_ref, tile, images), extent, emit_tap
        )

    narrow_tiles(tap_grads)
    wide_tiles(tap_grads)
    send_v.plane(send_v.all)
    small = jnp.sum(sums_ref[...], axis=1).astype(bf16)
    for t in range(depth):
        gs_ref[t] = jnp.zeros(gs_ref.shape[1:], bf16)
        gs_ref[t, 0 : small.shape[0], :] = small[:, t * share : (t + 1) * share]
    send_small.pair(send_small.all)

    dh1_ref = one_ref
    put_wide(dh1_ref, every, dot(raw_ref[...], wj_ref[...], 1, 1))
    send_k.gather_plane(send_k.all)
    send_k.stack()
    send_small.plane(send_small.all)

    def back(k, carry):
        at = block_at(k)
        grad = wide(dh1_ref, at)
        unit, scale = normalise(wide(x1_ref, at))
        put_wide(da_ref, at, wide(x2_ref, at) + normalise_back(grad, gain_one, unit, scale))
        return carry[0] + fold_rows(grad * unit), carry[1] + fold_rows(grad)

    sums = lax.fori_loop(0, steps, back, (zero, zero))
    send_v.gather_plane(send_v.all)
    send_v.stack()
    send_out.settle()
    each(feed, "settle")
    last_ref[...] = jnp.zeros_like(last_ref)
    last_ref[TAIL_EARLY_GAIN] = sums[0]
    last_ref[TAIL_EARLY_SHIFT] = sums[1]

    def position_back(tile, carry):
        bias = [jnp.zeros((images, LANES), f32)]
        dx_ref[0:images, lane(tile)] = da_ref[tile, 0:images, :].astype(bf16)

        def emit(i, total):
            here = grid_row(da_ref, tile, images, i)
            for j in range(GRID):
                dx_ref[cell_rows(images, i * GRID + j), lane(tile)] = (here[j] + total[j]).astype(bf16)
                bias[0] = bias[0] + here[j]

        depthwise_rows(
            partial(grid_row, da_ref, tile, images),
            lambda ab: prm(ROW_POS_KERNEL + ab[0] * 3 + ab[1], tile),
            3, True, emit,
        )
        last_ref[TAIL_POS_BIAS, :, lane(tile)] = fold_rows(bias[0])

        def emit_tap(a, b, total):
            last_ref[TAIL_POS_KERNEL + a * 3 + b, :, lane(tile)] = fold_rows(total)

        kernel_grads(partial(grid_row, da_ref, tile, images), partial(x_row, tile), 3, emit_tap)
        return carry

    lax.fori_loop(0, 2, position_back, 0)
    send_q.across()
    lax.fori_loop(2, 4, position_back, 0)
    written.append(local(dx_ref, results[1]))
    tail_ref[0] = jnp.sum(last_ref[...], axis=1).astype(bf16)
    tail = Tail(ring, tail_ref, (tail_pair, tail_plane, tail_stack))
    tail.start(0)
    send_k.settle()
    send_small.gather_plane(send_small.all)
    send_small.stack()
    tail.collect(0)
    send_q.settle()
    each(feed, "to_plane_two")
    send_v.settle()
    send_k.to_plane()
    tail.collect(1)
    send_q.descend()
    send_small.settle()
    send_v.to_plane()
    send_out.to_twin()
    each(feed, "to_twin")
    send_small.to_plane()
    send_k.to_twin()
    send_q.to_twin()
    gtail_ref[...] = tail.collect(2)
    for part, at in ((send_out, 2), (send_expand, 3), (send_reduce, 4), (send_q, 5), (send_k, 6)):
        part.finish()
        written.append(local(boxes[at], results[at]))
    written.append(local(gtail_ref, results[9]))
    send_v.to_twin()
    send_small.to_twin()
    for part, at in ((send_v, 7), (send_small, 8)):
        part.finish()
        written.append(local(boxes[at], results[at]))
    for copy in written:
        copy.wait()
    for copy in ring.sent:
        copy.wait_send()


def write_out(
    y_ref, dx_ref, gwo_ref, gwe_ref, gwr_ref, gwq_ref, gwk_ref, gwv_ref, gsm_ref, gtail_ref,
    y_out, dx_out, pk_out, pb_out, eg_out, es_out, jw_out, jb_out, sk_out, sb_out, mk_out, mb_out, lk_out, lb_out,
    ow_out, ob_out, lg_out, ls_out, ew_out, eb_out, rw_out, rb_out,
    y_box, dx_box, q_box, k_box, v_box, o_box, e_box, r_box, jw_box, ow_box, ew_box, rw_box,
    small_ref, in_sems, out_sems,
):
    depth, share = gsm_ref.shape[0], gsm_ref.shape[2]
    width = y_ref.shape[1]
    joint = [
        (ref, box, jw_box.at[:, part * width : (part + 1) * width], jw_out.at[:, part * width : (part + 1) * width])
        for part, (ref, box) in enumerate(((gwq_ref, q_box), (gwk_ref, k_box), (gwv_ref, v_box)))
    ]
    flat = [
        (gwe_ref, e_box, ew_box, ew_out), (gwr_ref, r_box, rw_box, rw_out), (gwo_ref, o_box, ow_box, ow_out),
    ]
    plain = [(y_ref, y_box, y_out), (dx_ref, dx_box, dx_out)]
    sources = [(ref, box) for ref, box, _, _ in flat + joint] + [(ref, box) for ref, box, _ in plain]
    loads = [pltpu.make_async_copy(ref, box, in_sems.at[at]) for at, (ref, box) in enumerate(sources)]
    for load in loads:
        load.start()
    stores = []

    def store(box, out):
        stores.append(pltpu.make_async_copy(box, out, out_sems.at[len(stores)]))
        stores[-1].start()

    for at, (_, box, wide_box, out) in enumerate(flat):
        loads[at].wait()
        wide_box[...] = box[0 : wide_box.shape[0], :].astype(f32)
        store(wide_box, out)
    for at, (_, box, wide_box, out) in enumerate(joint):
        loads[3 + at].wait()
        for t in range(depth):
            wide_box[t * share : (t + 1) * share, :] = box[t, 0:share, :].astype(f32)
        store(wide_box, out)
    for at, (_, box, out) in enumerate(plain):
        loads[6 + at].wait()
        store(box, out)
    for t in range(depth):
        small_ref[:, t * share : (t + 1) * share] = gsm_ref[t].astype(f32)
    for at, out in (
        (OUT_OUT_BIAS, ob_out), (OUT_LATE_GAIN, lg_out), (OUT_LATE_SHIFT, ls_out), (OUT_REDUCE_BIAS, rb_out),
    ):
        out[...] = small_ref[at, :]
    jb_out[0:width] = small_ref[OUT_BIAS_Q, :]
    jb_out[width:] = small_ref[OUT_BIAS_V, :]
    cw = eb_out.shape[0]
    mine = small_ref[pl.ds(OUT_EXPAND_BIAS + lax.axis_index("tensor"), 1), 0:cw]
    eb_out[...] = mine.reshape(cw)
    first_lane = 0
    for kernel_out, bias_out in ((sk_out, sb_out), (mk_out, mb_out), (lk_out, lb_out)):
        extent, count = kernel_out.shape[0], kernel_out.shape[2]
        span = slice(first_lane, first_lane + count)
        bias_out[...] = small_ref[OUT_BIAS_ALL, span]
        for a in range(extent):
            at = full_tap(extent, a, 0) - ROW_KERNEL_ALL + OUT_KERNEL_ALL
            kernel_out[a] = small_ref[at : at + extent, span]
        first_lane += count
    for a in range(3):
        at = TAIL_POS_KERNEL + 3 * a
        pk_out[a] = gtail_ref[at : at + 3, :]
    for at, out in ((TAIL_POS_BIAS, pb_out), (TAIL_EARLY_GAIN, eg_out), (TAIL_EARLY_SHIFT, es_out)):
        out[...] = gtail_ref[at, :]
    for copy in stores:
        copy.wait()


def per_device(
    block_input, position_kernel, position_bias, early_gain, early_shift, joint_weight, joint_bias,
    small_kernel, small_bias, middle_kernel, middle_bias, large_kernel, large_bias,
    output_weight, output_bias, late_gain, late_shift, expand_weight, expand_bias,
    reduce_weight, reduce_bias, cotangent,
):
    images, tokens, width = block_input.shape
    rows = images * tokens
    depth, copies_of = lax.axis_size("tensor"), lax.axis_size("dp")
    planes = math.gcd(copies_of // 2, 4)
    pieces = 2 * planes
    share, cw = width // depth, expand_weight.shape[1]
    unit = 16 * pieces
    sum_rows = padded(OUT_EXPAND_BIAS + depth, 16)
    shapes = [
        (padded(share, unit), width), (padded(width, unit), cw), (padded(cw, unit), width),
        (padded(share, unit), width), (padded(share, unit), width), (padded(share, unit), width),
        (padded(sum_rows, unit), share),
    ]
    near, far = planes - 1, depth - 1
    copies = far + 3 * far * (2 + near) + 2 * depth * 6 + 4 * (1 + near) + 1 + 2 * (near + far)
    copies += 6 * far + 3 * far + 4 * near + 2 * 5 + 7
    copies += 1 + near + far
    fill = lambda array, count: jnp.pad(array, ((0, count - array.shape[0]), (0, 0)))
    vmem = lambda shape, dtype=bf16: pltpu.VMEM(shape, dtype)
    tail = (TAIL_ROWS, width)
    flat = lambda array: array.transpose(1, 0, 2).reshape(rows, width)
    given = (
        flat(block_input), flat(cotangent), joint_weight, position_kernel, position_bias, early_gain, early_shift,
        joint_bias, small_kernel, small_bias, middle_kernel, middle_bias, large_kernel, large_bias, output_bias,
        late_gain, late_shift, reduce_bias, expand_bias,
        fill(output_weight, shapes[0][0]), fill(expand_weight, shapes[1][0]), fill(reduce_weight, shapes[2][0]),
    )
    outs = [
        ((rows, width), bf16), ((rows, width), bf16),
        (shapes[0], bf16), (shapes[1], bf16), (shapes[2], bf16),
        ((depth,) + shapes[3], bf16), ((depth,) + shapes[4], bf16), ((depth,) + shapes[5], bf16),
        ((depth,) + shapes[6], bf16), (tail, f32),
    ]
    scratch = (
        [vmem(array.shape) for array in given[:19]] + [vmem(shape, dtype) for shape, dtype in outs] +
        [vmem((PARAM_ROWS, width), f32)]
        + [vmem((4, rows, LANES), f32)] * 10
        + [vmem((rows, width))] * 3 + [vmem((rows, 3 * width))]
        + [vmem((images, PAD_TOK, width))] * 4 + [vmem((images, 4, LANES, LANES))]
        + [vmem((sum_rows, 8, width), f32), vmem((TAIL_ROWS, 8, width), f32)]
        + [vmem((depth,) + shape) for shape in shapes[:3]] + [vmem((depth, 8, cw), f32)]
        + [vmem((depth,) + shape) for shape in shapes]
        + [vmem((depth, r // 2, w)) for r, w in shapes]
        + [vmem((near, depth, r // pieces, w)) for r, w in shapes[:1] + shapes[4:]]
        + [
            vmem(shape)
            for r, w in shapes[1:3]
            for shape in (
                (depth, 2, r // pieces, w // 2), (depth, 2 * r // pieces, w // 2),
                (depth, r // pieces, w // 2), (depth, r // pieces, w // 2),
            )
        ]
        + [vmem((near, shapes[3][0] // pieces, width)), vmem((far, shapes[3][0] // 2, width))]
        + [vmem((far, r // pieces, w)) for r, w in shapes]
        + [vmem((3,) + tail), vmem((1,) + tail), vmem((near,) + tail), vmem((far,) + tail)]
        + [pltpu.SemaphoreType.DMA((copies,))] * 2 + [pltpu.SemaphoreType.DMA((32,))]
    )
    anywhere = pl.BlockSpec(memory_space=pl.ANY)
    inside = pl.BlockSpec(memory_space=pltpu.VMEM)
    made = pl.pallas_call(
        partial(whole_block, images, tokens, planes, depth),
        out_shape=[jax.ShapeDtypeStruct(shape, dtype) for shape, dtype in outs],
        in_specs=[anywhere] * 22,
        out_specs=[anywhere] * len(outs),
        scratch_shapes=scratch,
        compiler_params=pltpu.CompilerParams(
            vmem_limit_bytes=VMEM_BYTES, collective_id=1, has_side_effects=True
        ),
    )(*given)
    if copies_of > pieces:
        groups = [list(range(first, copies_of, pieces)) for first in range(pieces)]
        made = list(made[:2]) + list(lax.psum(tuple(made[2:]), "dp", axis_index_groups=groups))
    like = lambda array: jax.ShapeDtypeStruct(array.shape, f32)
    results = pl.pallas_call(
        write_out,
        out_shape=[jax.ShapeDtypeStruct((rows, width), bf16)] * 2 + [
            like(array) for array in (
                position_kernel, position_bias, early_gain, early_shift, joint_weight, joint_bias,
                small_kernel, small_bias, middle_kernel, middle_bias, large_kernel, large_bias,
                output_weight, output_bias, late_gain, late_shift, expand_weight, expand_bias,
                reduce_weight, reduce_bias,
            )
        ],
        in_specs=[anywhere] * 8 + [inside] * 2,
        out_specs=[
            anywhere if at in (0, 1, 6, 14, 18, 20) else inside for at in range(22)
        ],
        scratch_shapes=[vmem((rows, width))] * 2
        + [vmem((depth,) + shape) for shape in shapes[3:6]] + [vmem(shape) for shape in shapes[:3]]
        + [vmem(array.shape, f32) for array in (joint_weight, output_weight, expand_weight, reduce_weight)]
        + [vmem((shapes[6][0], width), f32), pltpu.SemaphoreType.DMA((8,)), pltpu.SemaphoreType.DMA((8,))],
        compiler_params=pltpu.CompilerParams(vmem_limit_bytes=VMEM_BYTES),
    )(*made)
    image_form = lambda array: array.reshape(tokens, images, width).transpose(1, 0, 2)
    return (image_form(results[0]), image_form(results[1])) + tuple(results[2:])


def solution(mesh):
    images = P(("dp", "tensor"), None, None)
    in_specs = (images,) + (P(),) * 12 + (
        P("tensor", None), P(), P(), P(), P(None, "tensor"), P("tensor"), P("tensor", None), P(), images,
    )
    out_specs = (images, images) + (P(),) * 12 + (
        P("tensor", None), P(), P(), P(), P(None, "tensor"), P("tensor"), P("tensor", None), P(),
    )
    return jax.shard_map(per_device, mesh=mesh, in_specs=in_specs, out_specs=out_specs, check_vma=False)
```

```python
import math
from functools import partial

import jax
import jax.numpy as jnp
from jax import lax
from jax.experimental import pallas as pl
from jax.experimental.pallas import tpu as pltpu
from jax.sharding import PartitionSpec as P

HEADS = 8
HEAD = 64
GRID = 7
CELLS = GRID * GRID
NORM_EPS = 1e-06
SCALE = HEAD**-0.5
LANES = 128
GROUP = 256
PAD_TOK = 64
VMEM_BYTES = 62 * 1024 * 1024

f32 = jnp.float32
bf16 = jnp.bfloat16

ROW_POS_BIAS, ROW_EARLY_GAIN, ROW_EARLY_SHIFT, ROW_BIAS_Q, ROW_BIAS_V = 0, 1, 2, 3, 4
ROW_BIAS_ALL, ROW_OUT_BIAS, ROW_LATE_GAIN, ROW_LATE_SHIFT, ROW_REDUCE_BIAS = 5, 6, 7, 8, 9
ROW_POS_KERNEL, ROW_KERNEL_ALL = 10, 19
PARAM_ROWS = 72

OUT_KERNEL_ALL, OUT_BIAS_Q, OUT_BIAS_V, OUT_BIAS_ALL = 0, 49, 50, 51
OUT_LATE_GAIN, OUT_LATE_SHIFT, OUT_OUT_BIAS, OUT_REDUCE_BIAS, OUT_EXPAND_BIAS = 52, 53, 54, 55, 56
TAIL_POS_KERNEL, TAIL_POS_BIAS, TAIL_EARLY_GAIN, TAIL_EARLY_SHIFT, TAIL_ROWS = 0, 9, 10, 11, 16
MESH = pl.DeviceIdType.MESH

SCHEDULE = {
    "qdot": ("wo1",),
    "conv1": ("g1 1",),
    "image2": ("wo2",),
    "norm2b": ("g1 2",),
    "chunk0b": ("g1 3", "g2 1",),
    "chunk0f": ("g3 1",),
    "chunk1b": ("f1 0",),
    "chunk1e": ("g2 2",),
    "chunk2a": ("f1 1",),
    "chunk2c": ("g2 3",),
    "chunk3a": ("f2 0", "f1 2",),
    "chunk3c": ("f2 1",),
    "finish0": ("f3 0", "f1 3",),
    "finish1": ("f2 2",),
    "datt": ("f3 1",),
    "back0": ("o1",),
    "back1": ("f2 3",),
    "back2": ("f3 2",),
    "gq": ("o2",),
    "values0": ("f3 3",),
    "values1": ("q1",),
    "values2": ("k1",),
    "taps2": ("v1",),
    "small": ("o3",),
    "dh1a": ("q2",),
    "dh1b": ("s1",),
    "normback0": ("f4",),
    "normback1": ("k2",),
    "pos3": ("q3",),
    "tail": ("v2",),
    "end": ("o4", "s2", "t1", "o5", "k3", "f5", "q4", "t2", "v3", "s3", "k4", "f6", "t3", "f7", "v4", "s4", "q5", "q6", "k5", "k6", "v5", "s5", "v6", "s6",),
}


def lane(tile):
    if isinstance(tile, int):
        return slice(tile * LANES, (tile + 1) * LANES)
    return pl.ds(pl.multiple_of(tile * LANES, LANES), LANES)


def taps(extent):
    return range(extent)


def columns(shift):
    return range(max(0, -shift), min(GRID, GRID - shift))


def depthwise_rows(get_row, get_weight, extent, flip, emit):
    margin = extent // 2
    for i in range(GRID):
        total = [None] * GRID
        for a in range(extent):
            r = i + a - margin
            if not 0 <= r < GRID:
                continue
            row = get_row(r)
            for b in range(extent):
                weight = get_weight((extent - 1 - a, extent - 1 - b) if flip else (a, b))
                for j in columns(b - margin):
                    term = row[j + b - margin] * weight
                    total[j] = term if total[j] is None else total[j] + term
        emit(i, total)


def kernel_grads(get_left, get_right, extent, emit):
    margin = extent // 2
    for a in range(extent):
        total = [None] * extent
        for i in range(GRID):
            r = i + a - margin
            if not 0 <= r < GRID:
                continue
            left, right = get_left(i), get_right(r)
            for b in range(extent):
                for j in columns(b - margin):
                    term = left[j] * right[j + b - margin]
                    total[b] = term if total[b] is None else total[b] + term
        for b in range(extent):
            emit(a, b, total[b])


def cell_rows(images, cell, count=1):
    return slice((1 + cell) * images, (1 + cell + count) * images)


def grid_row(ref, tile, images, i):
    block = ref[tile, cell_rows(images, i * GRID, GRID), :]
    return [block[j * images : (j + 1) * images] for j in range(GRID)]


def full_tap(extent, a, b):
    extra = (GRID - extent) // 2
    return ROW_KERNEL_ALL + (a + extra) * GRID + b + extra


def narrow_tiles(body):
    body(0, 3)
    body(1, 5)


def normalise(block):
    centre = jnp.mean(block, axis=-1, keepdims=True)
    centred = block - centre
    spread = jnp.mean(centred * centred, axis=-1, keepdims=True)
    scale = lax.rsqrt(spread + NORM_EPS)
    return centred * scale, scale


def normalise_back(grad, gain, unit, scale):
    scaled = grad * gain
    mean_one = jnp.mean(scaled, axis=-1, keepdims=True)
    mean_two = jnp.mean(scaled * unit, axis=-1, keepdims=True)
    return (scaled - mean_one - unit * mean_two) * scale


def fold_rows(block):
    return jnp.sum(block.reshape(block.shape[0] // 8, 8, block.shape[1]), axis=0)


def dot(left, right, left_dim=1, right_dim=0):
    return lax.dot_general(
        left, right, (((left_dim,), (right_dim,)), ((), ())), preferred_element_type=f32
    )


def padded(count, unit):
    return -(-count // unit) * unit


class Ring:
    def __init__(self, pairs, depth, send_sems, recv_sems):
        self.dp = lax.axis_index("dp")
        self.me = lax.axis_index("tensor")
        self.planes, self.depth = pairs, depth
        group = 2 * pairs
        self.base = lax.div(self.dp, group) * group
        self.core = lax.rem(self.dp, 2)
        self.spot = lax.div(lax.rem(self.dp, group), 2)
        self.send_sems, self.recv_sems, self.used = send_sems, recv_sems, 0
        self.sent = []

    def twin(self):
        return {"dp": self.base + self.spot * 2 + (1 - self.core), "tensor": self.me}

    def plane(self, k):
        return {"dp": self.base + lax.rem(self.spot + k, self.planes) * 2 + self.core, "tensor": self.me}

    def plane_spot(self, k):
        return lax.rem(self.spot + k, self.planes)

    def across(self, k):
        return {"dp": self.base + self.beside(k) * 2 + self.core, "tensor": self.me}

    def beside(self, k):
        low, high = lax.rem(self.spot, 2), lax.div(self.spot, 2)
        return high * 2 + 1 - low if k == 1 else (1 - high) * 2 + low

    def stack(self, k):
        return {"dp": self.dp, "tensor": lax.rem(self.me + k, self.depth)}

    def everyone(self):
        return (
            [self.twin()]
            + [self.plane(k) for k in range(1, self.planes)]
            + [self.stack(k) for k in range(1, self.depth)]
        )

    def piece(self, rows, spot, core=None):
        each = rows // (2 * self.planes)
        core = self.core if core is None else core
        return pl.ds(pl.multiple_of((core * self.planes + spot) * each, each), each)

    def band(self, rows, high):
        each = rows // (2 * self.planes)
        start = (self.core * self.planes + high * 2) * each
        return pl.ds(pl.multiple_of(start, 2 * each), 2 * each)

    def half(self, rows, core):
        return pl.ds(pl.multiple_of(core * (rows // 2), rows // 2), rows // 2)

    def send(self, source, target, device):
        at = self.used
        self.used += 1
        copy = pltpu.make_async_remote_copy(
            src_ref=source, dst_ref=target, send_sem=self.send_sems.at[at], recv_sem=self.recv_sems.at[at],
            device_id=device, device_id_type=MESH,
        )
        copy.start()
        self.sent.append(copy)
        return copy


def arrive(copies):
    for copy in copies:
        copy.wait_recv()


class Reduction:
    def __init__(self, ring, grads, twin_box, plane_box, stack_box, out, whole, relative):
        self.ring, self.grads, self.out, self.whole, self.relative = ring, grads, out, whole, relative
        self.twin_box, self.plane_box, self.stack_box = twin_box, plane_box, stack_box
        self.rows = grads.shape[1]
        self.depth = grads.shape[0]
        self.pairs, self.planes, self.stacks = {}, {}, {}
        self.all = slice(0, self.depth)

    def slot(self, k):
        return k if self.relative else lax.rem(self.ring.me + k, self.depth)

    def pair(self, part):
        ring = self.ring
        away = ring.half(self.rows, 1 - ring.core)
        self.pairs[str(part)] = ring.send(self.grads.at[part, away], self.twin_box.at[part], ring.twin())

    def meet(self, part):
        ring = self.ring
        arrive([self.pairs[str(part)]])
        mine = ring.half(self.rows, ring.core)
        self.grads[part, mine] = (
            self.grads[part, mine].astype(f32) + self.twin_box[part].astype(f32)
        ).astype(bf16)

    def plane(self, part):
        ring = self.ring
        self.meet(part)
        self.planes[str(part)] = [
            ring.send(
                self.grads.at[part, ring.piece(self.rows, ring.plane_spot(k))],
                self.plane_box.at[k - 1, part], ring.plane(k),
            )
            for k in range(1, ring.planes)
        ]

    def gather_plane(self, part):
        ring = self.ring
        arrive(self.planes[str(part)])
        mine = ring.piece(self.rows, ring.spot)
        total = self.grads[part, mine].astype(f32)
        for k in range(1, ring.planes):
            total = total + self.plane_box[k - 1, part].astype(f32)
        self.grads[part, mine] = total.astype(bf16)

    def stack(self, offsets=None):
        ring = self.ring
        mine = ring.piece(self.rows, ring.spot)
        for k in range(1, self.depth) if offsets is None else offsets:
            self.stacks[k] = ring.send(self.grads.at[self.slot(k), mine], self.stack_box.at[k - 1], ring.stack(k))

    def settle(self):
        ring = self.ring
        arrive(self.stacks.values())
        mine = ring.piece(self.rows, ring.spot)
        total = self.grads[self.slot(0), mine].astype(f32)
        for k in self.stacks:
            total = total + self.stack_box[k - 1].astype(f32)
        done = total.astype(bf16)
        if self.whole:
            self.out[ring.me, mine] = done
            place = self.out.at[ring.me, mine]
            self.spread = [ring.send(place, place, ring.stack(k)) for k in range(1, self.depth)]
        else:
            self.out[mine] = done
            self.to_plane()

    def to_plane(self):
        ring = self.ring
        mine = ring.piece(self.rows, ring.spot)
        if self.whole:
            arrive(self.spread)
            place = self.out.at[:, mine]
        else:
            place = self.out.at[mine]
        self.back = [ring.send(place, place, ring.plane(k)) for k in range(1, ring.planes)]

    def to_twin(self):
        ring = self.ring
        arrive(self.back)
        mine = ring.half(self.rows, ring.core)
        place = self.out.at[:, mine] if self.whole else self.out.at[mine]
        self.last = ring.send(place, place, ring.twin())

    def finish(self):
        arrive([self.last])


class TwoPhase(Reduction):
    def __init__(self, ring, grads, twin_box, plane_boxes, stack_box, out, whole, relative):
        super().__init__(ring, grads, twin_box, None, stack_box, out, whole, relative)
        self.first_box, self.band_box, self.low_box, self.high_box = plane_boxes
        self.cut = grads.shape[2] // 2
        self.ones, self.twos = {}, {}

    def add(self, part, at, columns, box):
        self.grads[part, at, columns] = (self.grads[part, at, columns].astype(f32) + box.astype(f32)).astype(bf16)

    def phase_one(self, part):
        ring = self.ring
        self.meet(part)
        left, right = slice(0, self.cut), slice(self.cut, 2 * self.cut)
        low, high = lax.rem(ring.spot, 2), lax.div(ring.spot, 2)
        self.ones[str(part)] = [
            ring.send(
                self.grads.at[part, ring.piece(self.rows, 2 * y + 1 - low), left],
                self.first_box.at[part, y], ring.across(1),
            )
            for y in range(2)
        ] + [
            ring.send(
                self.grads.at[part, ring.band(self.rows, 1 - high), right], self.band_box.at[part], ring.across(2)
            )
        ]

    def phase_two(self, part):
        ring = self.ring
        left, right = slice(0, self.cut), slice(self.cut, 2 * self.cut)
        low, high = lax.rem(ring.spot, 2), lax.div(ring.spot, 2)
        arrive(self.ones[str(part)])
        for y in range(2):
            self.add(part, ring.piece(self.rows, 2 * y + low), left, self.first_box[part, y])
        self.add(part, ring.band(self.rows, high), right, self.band_box[part])
        self.twos[str(part)] = [
            ring.send(
                self.grads.at[part, ring.piece(self.rows, ring.beside(2)), left], self.high_box.at[part], ring.across(2)
            ),
            ring.send(
                self.grads.at[part, ring.piece(self.rows, ring.beside(1)), right], self.low_box.at[part], ring.across(1)
            ),
        ]

    def to_plane(self):
        if self.whole:
            super().to_plane()
            return
        ring = self.ring
        mine = ring.piece(self.rows, ring.spot)
        left, right = self.out.at[mine, 0 : self.cut], self.out.at[mine, self.cut : 2 * self.cut]
        self.ahead = [ring.send(left, left, ring.across(2)), ring.send(right, right, ring.across(1))]

    def to_plane_two(self):
        ring = self.ring
        arrive(self.ahead)
        low, high = lax.rem(ring.spot, 2), lax.div(ring.spot, 2)
        places = [self.out.at[ring.piece(self.rows, 2 * y + low), 0 : self.cut] for y in range(2)]
        band = self.out.at[ring.band(self.rows, high), self.cut : 2 * self.cut]
        self.back = [ring.send(place, place, ring.across(1)) for place in places]
        self.back.append(ring.send(band, band, ring.across(2)))

    def gather_plane(self, part):
        ring = self.ring
        arrive(self.twos[str(part)])
        mine = ring.piece(self.rows, ring.spot)
        self.add(part, mine, slice(0, self.cut), self.high_box[part])
        self.add(part, mine, slice(self.cut, 2 * self.cut), self.low_box[part])


class Gather:
    def __init__(self, ring, shard, box, relative):
        self.ring, self.shard, self.box, self.relative = ring, shard, box, relative
        self.depth, self.rows = box.shape[0], box.shape[1]
        self.first, self.second, self.third = {}, {}, {}

    def slot(self, j):
        return j if self.relative else lax.rem(self.ring.me + j, self.depth)

    def start(self, j):
        ring = self.ring
        mine = ring.piece(self.rows, ring.spot)
        target = self.box.at[j if self.relative else ring.me, mine]
        self.first[j] = ring.send(self.shard.at[mine], target, ring.stack(self.depth - j))

    def plane(self, j):
        ring = self.ring
        arrive([self.first[j]])
        place = self.box.at[self.slot(j), ring.piece(self.rows, ring.spot)]
        self.second[j] = [ring.send(place, place, ring.plane(k)) for k in range(1, ring.planes)]

    def pair(self, j):
        ring = self.ring
        arrive(self.second[j])
        place = self.box.at[self.slot(j), ring.half(self.rows, ring.core)]
        self.third[j] = ring.send(place, place, ring.twin())

    def finish(self, j):
        arrive([self.third[j]])


class Tail:
    def __init__(self, ring, mine, boxes):
        self.ring, self.mine, self.boxes = ring, mine, boxes

    def start(self, stage):
        ring = self.ring
        devices = (
            [ring.twin()],
            [ring.plane(k) for k in range(1, ring.planes)],
            [ring.stack(k) for k in range(1, ring.depth)],
        )[stage]
        self.copies = [
            ring.send(self.mine.at[stage], self.boxes[stage].at[k], device) for k, device in enumerate(devices)
        ]

    def collect(self, stage):
        total = self.mine[stage].astype(f32)
        for k, copy in enumerate(self.copies):
            copy.wait_recv()
            total = total + self.boxes[stage][k].astype(f32)
        if stage < 2:
            self.mine[stage + 1] = total.astype(bf16)
            self.start(stage + 1)
        return total


class Plan:
    def __init__(self, schedule):
        self.schedule, self.steps, self.done = schedule, {}, set()

    def add(self, name, needs, action):
        self.steps[name] = (needs, action)

    def need(self, name):
        if name in self.done:
            return
        needs, action = self.steps[name]
        for other in needs:
            self.need(other)
        self.done.add(name)
        action()

    def at(self, point):
        for name in self.schedule.get(point, ()):
            if name in self.steps:
                self.need(name)

    def rest(self):
        for name in self.steps:
            self.need(name)


def each(parts, step_name, *args):
    for part in parts:
        getattr(part, step_name)(*args)


def wide(ref, at):
    return jnp.concatenate([ref[tile, at, :] for tile in range(4)], axis=1)


def put_wide(ref, at, block):
    for tile in range(4):
        ref[tile, at, :] = block[:, lane(tile)]


def whole_block(
    images, tokens, planes, depth, *refs,
):
    given, refs = refs[:22], refs[22:]
    results, refs = refs[:10], refs[10:]
    held, refs = refs[:19], refs[19:]
    boxes, refs = refs[:10], refs[10:]
    (
        x_ref, cot_ref, wj_ref, pk_ref, pb_ref, eg_ref, es_ref, jb_ref, sk_ref, sb_ref, mk_ref, mb_ref,
        lk_ref, lb_ref, ob_ref, lg_ref, ls_ref, rb_ref, eb_shard,
    ) = held
    wo_shard, we_shard, wr_shard = given[19:]
    y_ref, dx_ref, gwo_ref, gwe_ref, gwr_ref, gwq_ref, gwk_ref, gwv_ref, gsm_ref, gtail_ref = boxes
    (
        prm_ref, x1_ref, x2_ref, q_ref, v_ref, ks_ref, conv_ref, fac_ref, one_ref, two_ref, three_ref,
        h1_ref, att_ref, h2_ref, raw_ref,
        qi_ref, ki_ref, vi_ref, dai_ref, ctx_ref, sums_ref, last_ref,
        wo_ref, we_ref, wr_ref, eb_ref,
        go_ref, ge_ref, gr_ref, gq_ref, gk_ref, gv_ref, gs_ref,
        to_ref, te_ref, tr_ref, tq_ref, tk_ref, tv_ref, ts_ref,
        po_ref, pq_ref, pk2_ref, pv_ref, ps_ref,
        e_first, e_band, e_low, e_high, r_first, r_band, r_low, r_high,
        so_ref, se_ref, sr_ref, sq_ref, sk2_ref, sv_ref, ss_ref,
        tail_ref, tail_pair, tail_plane, tail_stack,
        send_sems, recv_sems, local_sems,
    ) = refs
    ring = Ring(planes, depth, send_sems, recv_sems)
    barrier = pltpu.get_barrier_semaphore()
    for device in ring.everyone():
        pl.semaphore_signal(barrier, inc=1, device_id=device, device_id_type=MESH)

    rows = images * tokens
    width = 4 * LANES
    step = 5 * images
    steps = rows // step
    share = width // depth
    cw = we_ref.shape[2]
    get_out = Gather(ring, wo_shard, wo_ref, False)
    get_expand = Gather(ring, we_shard, we_ref, True)
    get_reduce = Gather(ring, wr_shard, wr_ref, True)
    feed_in = (get_expand, get_reduce)
    slots = range(1, depth)
    used = []

    def local(source, target):
        copy = pltpu.make_async_copy(source, target, local_sems.at[len(used)])
        copy.start()
        used.append(copy)
        return copy

    loads = [local(source, target) for source, target in zip(given, held)]
    pl.semaphore_wait(barrier, planes + depth - 1)
    order = list(slots)
    plan = Plan(SCHEDULE)

    def chain(name, parts, suffix, actions, first=()):
        before = list(first)
        for at, action in enumerate(actions):
            label = name + str(at) + suffix
            plan.add(label, before, action)
            before = [label]

    def calls(parts, step_name, *args):
        return partial(each, parts, step_name, *args)

    def out_all(step_name):
        for j in slots:
            getattr(get_out, step_name)(j)

    chain("wo", None, "", [partial(out_all, name) for name in ("start", "plane", "pair", "finish")])
    for j in slots:
        chain("g", None, " " + str(j), [calls(feed_in, name, j) for name in ("start", "plane", "pair", "finish")])
    plan.need("wo0")
    plan.need("g0 1")
    own = [
        local(source, target)
        for source, target in ((wo_shard, wo_ref.at[ring.me]), (we_shard, we_ref.at[0]), (wr_shard, wr_ref.at[0]))
    ]
    for copy in [loads[0]] + loads[3:]:
        copy.wait()
    eb_ref[0] = jnp.broadcast_to(eb_shard[...].astype(f32).reshape(1, cw), (8, cw))

    get_bias = [ring.send(eb_ref.at[0], eb_ref.at[j], ring.stack(depth - j)) for j in slots]

    for at, ref in (
        (ROW_POS_BIAS, pb_ref), (ROW_EARLY_GAIN, eg_ref), (ROW_EARLY_SHIFT, es_ref), (ROW_OUT_BIAS, ob_ref),
        (ROW_LATE_GAIN, lg_ref), (ROW_LATE_SHIFT, ls_ref), (ROW_REDUCE_BIAS, rb_ref),
    ):
        prm_ref[at : at + 1, :] = ref[...].astype(f32).reshape(1, width)
    prm_ref[ROW_BIAS_Q : ROW_BIAS_Q + 1, :] = jb_ref[0:width].astype(f32).reshape(1, width)
    prm_ref[ROW_BIAS_V : ROW_BIAS_V + 1, :] = jb_ref[width : 2 * width].astype(f32).reshape(1, width)
    prm_ref[ROW_KERNEL_ALL:PARAM_ROWS, :] = jnp.zeros((PARAM_ROWS - ROW_KERNEL_ALL, width), f32)
    first_lane = 0
    for kernel_ref, bias_ref in ((sk_ref, sb_ref), (mk_ref, mb_ref), (lk_ref, lb_ref)):
        extent, count = kernel_ref.shape[0], kernel_ref.shape[2]
        span = slice(first_lane, first_lane + count)
        prm_ref[ROW_BIAS_ALL : ROW_BIAS_ALL + 1, span] = bias_ref[...].astype(f32).reshape(1, count)
        for a in range(extent):
            at = full_tap(extent, a, 0)
            prm_ref[at : at + extent, span] = kernel_ref[a].astype(f32)
        first_lane += count
    for a in range(3):
        prm_ref[ROW_POS_KERNEL + 3 * a : ROW_POS_KERNEL + 3 * a + 3, :] = pk_ref[a].astype(f32)

    prm = lambda row, tile: prm_ref[row : row + 1, lane(tile)]
    row = lambda r: prm_ref[r : r + 1, :]
    block_at = lambda k: pl.ds(pl.multiple_of(k * step, step), step)

    x_row = lambda tile, i: [
        x_ref[cell_rows(images, i * GRID + j), lane(tile)].astype(f32) for j in range(GRID)
    ]

    def position(tile, carry):
        x1_ref[tile, 0:images, :] = x_ref[0:images, lane(tile)].astype(f32)
        bias = prm(ROW_POS_BIAS, tile)

        def emit(i, total):
            here = x_row(tile, i)
            for j in range(GRID):
                x1_ref[tile, cell_rows(images, i * GRID + j), :] = here[j] + total[j] + bias

        depthwise_rows(
            partial(x_row, tile), lambda ab: prm(ROW_POS_KERNEL + ab[0] * 3 + ab[1], tile), 3, False, emit
        )
        return carry

    lax.fori_loop(0, 4, position, 0)
    for j in slots:
        plan.need("g0 " + str(j))
    plan.at("position")

    def norm_of(source, target, gain, shift):
        def norm(k, carry):
            at = block_at(k)
            unit, _ = normalise(wide(source, at))
            target[at, :] = (unit * gain + shift).astype(bf16)
            return carry

        lax.fori_loop(0, steps, norm, 0)

    gain_one, shift_one = row(ROW_EARLY_GAIN), row(ROW_EARLY_SHIFT)
    norm_of(x1_ref, h1_ref, gain_one, shift_one)
    plan.at("norm1b")
    every = slice(0, rows)
    loads[2].wait()
    put_wide(v_ref, every, (dot(h1_ref[...], wj_ref[:, 2 * width :]) + row(ROW_BIAS_V)).astype(bf16).astype(f32))
    plan.at("vdot")
    put_wide(ks_ref, every, dot(h1_ref[...], wj_ref[:, width : 2 * width]).astype(bf16).astype(f32))
    plan.at("kdot")
    put_wide(q_ref, every, (dot(h1_ref[...], wj_ref[:, :width]) + row(ROW_BIAS_Q)).astype(bf16).astype(f32))
    plan.at("qdot")

    token = lambda n: slice(n * images, (n + 1) * images)

    def soften(tile, carry):
        top = ks_ref[tile, token(0), :]
        for n in range(1, tokens):
            top = jnp.maximum(top, ks_ref[tile, token(n), :])
        total = jnp.zeros_like(top)
        for n in range(tokens):
            e = jnp.exp(ks_ref[tile, token(n), :] - top)
            ks_ref[tile, token(n), :] = e
            total = total + e
        scale = 1.0 / total
        for n in range(tokens):
            ks_ref[tile, token(n), :] = ks_ref[tile, token(n), :] * scale
        return carry

    lax.fori_loop(0, 4, soften, 0)
    plan.at("soft3")

    def convolve(tile, extent):
        conv_ref[tile, 0:images, :] = jnp.zeros((images, LANES), f32)
        bias = prm(ROW_BIAS_ALL, tile)

        def emit(i, total):
            for j in range(GRID):
                conv_ref[tile, cell_rows(images, i * GRID + j), :] = total[j] + bias

        depthwise_rows(
            partial(grid_row, v_ref, tile, images), lambda ab: prm(full_tap(extent, *ab), tile),
            extent, False, emit,
        )

    narrow_tiles(convolve)
    plan.at("conv0")
    for tile in (2, 3):
        convolve(tile, 7)
        plan.at("conv" + str(tile - 1))

    some = images // 4
    lanes_of = lax.broadcasted_iota(jnp.int32, (LANES, LANES), 1) // HEAD
    rows_of = lax.broadcasted_iota(jnp.int32, (LANES, LANES), 0) // HEAD
    pair_mask = jnp.where(lanes_of == rows_of, 1.0, 0.0)
    here = lambda b: pl.ds(b, tokens, stride=images)

    def per_image(source, target, b):
        target[b, 48:PAD_TOK, :] = jnp.zeros((PAD_TOK - 48, width), bf16)
        for tile in range(4):
            target[b, 0:tokens, lane(tile)] = source[tile, here(b), :].astype(bf16)

    def image(g, carry):
        batch = [g * some + u for u in range(some)]
        for b in batch:
            for source, target in ((ks_ref, ki_ref), (v_ref, vi_ref), (q_ref, qi_ref)):
                per_image(source, target, b)
        for b in batch:
            for t in range(4):
                full = dot(ki_ref[b, :, lane(t)], vi_ref[b, :, lane(t)], 0, 0)
                ctx_ref[b, t] = (full * pair_mask).astype(bf16)
        for b in batch:
            for t in range(4):
                out = dot(qi_ref[b, :, lane(t)], ctx_ref[b, t]) * SCALE
                fac_ref[t, here(b), :] = out[0:tokens]
        return carry

    for g in range(4):
        lax.fori_loop(g, g + 1, image, 0)
        plan.at("image" + str(g))

    def combine(tile, carry):
        att_ref[:, lane(tile)] = (fac_ref[tile] + q_ref[tile] * conv_ref[tile]).astype(bf16)
        return carry

    lax.fori_loop(0, 4, combine, 0)

    loads[1].wait()
    for copy in own:
        copy.wait()
    plan.at("combine")
    plan.need("wo3")
    whole_out = jnp.concatenate([wo_ref[t, 0:share, :] for t in range(depth)], axis=0)
    branch = dot(att_ref[...], whole_out) + row(ROW_OUT_BIAS)
    for tile in range(4):
        x2_ref[tile] = x1_ref[tile] + branch[:, lane(tile)]
    gain_two, shift_two = row(ROW_LATE_GAIN), row(ROW_LATE_SHIFT)
    plan.at("outproj")
    norm_of(x2_ref, h2_ref, gain_two, shift_two)
    plan.at("norm2b")

    e_boxes, r_boxes = (e_first, e_band, e_low, e_high), (r_first, r_band, r_low, r_high)
    send_expand = TwoPhase(ring, ge_ref, te_ref, e_boxes, se_ref, gwe_ref, False, True)
    send_reduce = TwoPhase(ring, gr_ref, tr_ref, r_boxes, sr_ref, gwr_ref, False, True)
    send_out = Reduction(ring, go_ref, to_ref, po_ref, so_ref, gwo_ref, False, False)
    send_q = Reduction(ring, gq_ref, tq_ref, pq_ref, sq_ref, gwq_ref, True, False)
    send_k = Reduction(ring, gk_ref, tk_ref, pk2_ref, sk2_ref, gwk_ref, True, False)
    send_v = Reduction(ring, gv_ref, tv_ref, pv_ref, sv_ref, gwv_ref, True, False)
    send_small = Reduction(ring, gs_ref, ts_ref, ps_ref, ss_ref, gsm_ref, True, False)
    feed = (send_expand, send_reduce)

    chunks = [0] + order
    written = []

    def feed_stack(c):
        for part in feed:
            part.gather_plane(c)
            if c >= 1:
                part.stack([c])

    def store(items):
        for part, at in items:
            part.finish()
            written.append(local(boxes[at], results[at]))

    for c in chunks:
        chain("f", None, " " + str(c), [
            calls(feed, "pair", c), calls(feed, "phase_one", c), calls(feed, "phase_two", c), partial(feed_stack, c),
        ])
    plan.add("f4", ["f3 " + str(c) for c in chunks], calls(feed, "settle"))
    plan.add("f5", ["f4"], calls(feed, "to_plane_two"))
    plan.add("f6", ["f5"], calls(feed, "to_twin"))
    plan.add("f7", ["f6"], partial(store, ((send_expand, 3), (send_reduce, 4))))

    def climb(part):
        part.gather_plane(part.all)
        part.stack()

    for name, part, at in (("q", send_q, 5), ("k", send_k, 6), ("v", send_v, 7), ("s", send_small, 8)):
        chain(name, None, "", [
            partial(part.pair, part.all), partial(part.plane, part.all), partial(climb, part), part.settle,
            part.to_plane, part.to_twin, partial(store, ((part, at),)),
        ])
    chain("o", None, "", [
        partial(send_out.pair, send_out.all), partial(send_out.plane, send_out.all), partial(climb, send_out),
        send_out.settle, send_out.to_twin, partial(store, ((send_out, 2),)),
    ])
    closing = Tail(ring, tail_ref, (tail_pair, tail_plane, tail_stack))

    def tail_last():
        gtail_ref[...] = closing.collect(2)
        written.append(local(gtail_ref, results[9]))

    chain("t", None, "", [
        partial(closing.start, 0), partial(closing.collect, 0), partial(closing.collect, 1), tail_last,
    ])

    acc_ref, dh2_ref = one_ref, two_ref
    hid_ref, dpre_ref = raw_ref.at[:, 0:cw], raw_ref.at[:, width : width + cw]
    datt_ref = raw_ref.at[:, 2 * width : 3 * width]
    half = rows // 2
    sums_ref[...] = jnp.zeros_like(sums_ref)
    arrive(get_bias)
    for at_chunk, c in enumerate(chunks):
        point = "chunk" + str(at_chunk)
        if at_chunk >= 1:
            plan.need("g3 " + str(c))
        bias = eb_ref[c, 0:1, :]
        folded = jnp.zeros((8, cw), f32)
        we, wr = we_ref[c], wr_ref[c, 0:cw, :]
        for k in range(2):
            at = slice(k * half, (k + 1) * half)
            pre = dot(h2_ref[at, :], we) + bias
            dh = dot(cot_ref[at, :], wr, 1, 1)
            gauss = jnp.exp(pre * pre * -0.5)
            t = 1.0 / (1.0 + (0.3275911 * 0.7071067811865476) * jnp.abs(pre))
            poly = t * (0.127414796 + t * (-0.142248368 + t * (0.7107068705 + t * (-0.7265760135 + t * 0.5307027145))))
            tail = poly * gauss
            cdf = jnp.where(pre >= 0, 1.0 - tail, tail)
            hid_ref[at, :] = (pre * cdf).astype(bf16)
            dpre = ((cdf + pre * gauss * 0.3989422804014327) * dh).astype(bf16)
            dpre_ref[at, :] = dpre
            folded = folded + fold_rows(dpre.astype(f32))
            plan.at(point + "ab"[k])
        sums_ref[OUT_EXPAND_BIAS + lax.rem(ring.me + c, depth), :, 0:cw] = folded
        ge_ref[c] = dot(h2_ref[...], dpre_ref[...], 0, 0).astype(bf16)
        plan.at(point + "c")
        gr_ref[c, 0:cw] = dot(hid_ref[...], cot_ref[...], 0, 0).astype(bf16)
        if gr_ref.shape[1] > cw:
            gr_ref[c, cw:] = jnp.zeros((gr_ref.shape[1] - cw, width), bf16)
        plan.need("f0 " + str(c))
        plan.at(point + "e")
        out = dot(hid_ref[...], wr)
        back = dot(dpre_ref[...], we, 1, 1)
        for tile in range(4):
            if at_chunk == 0:
                acc_ref[tile] = out[:, lane(tile)]
                dh2_ref[tile] = back[:, lane(tile)]
            else:
                acc_ref[tile] += out[:, lane(tile)]
                dh2_ref[tile] += back[:, lane(tile)]
        plan.at(point + "f")

    def finish(k, carry):
        at = block_at(k)
        x2 = wide(x2_ref, at)
        y_ref[at, :] = (x2 + wide(acc_ref, at) + row(ROW_REDUCE_BIAS)).astype(bf16)
        unit, scale = normalise(x2)
        grad = wide(dh2_ref, at)
        dy = cot_ref[at, :].astype(f32)
        dx2 = dy + normalise_back(grad, gain_two, unit, scale)
        put_wide(x2_ref, at, dx2)
        low = dx2.astype(bf16)
        datt_ref[at, :] = low
        return (
            carry[0] + fold_rows(grad * unit), carry[1] + fold_rows(grad),
            carry[2] + fold_rows(low.astype(f32)), carry[3] + fold_rows(dy),
        )

    zero = jnp.zeros((8, width), f32)
    sums = lax.fori_loop(0, steps // 2, finish, (zero,) * 4)
    plan.at("finish0")
    sums = lax.fori_loop(steps // 2, steps, finish, sums)
    plan.at("finish1")
    written.append(local(y_ref, results[0]))
    for r, total in zip((OUT_LATE_GAIN, OUT_LATE_SHIFT, OUT_OUT_BIAS, OUT_REDUCE_BIAS), sums):
        sums_ref[r] = total
    grad_out = dot(att_ref[...], datt_ref[...], 0, 0).astype(bf16)
    for t in range(depth):
        go_ref[t, 0:share, :] = grad_out[t * share : (t + 1) * share, :]
        if go_ref.shape[1] > share:
            go_ref[t, share:, :] = jnp.zeros((go_ref.shape[1] - share, width), bf16)
    plan.need("o0")
    plan.at("gwo")
    grad_att = dot(datt_ref[...], whole_out, 1, 1).astype(bf16).astype(f32)
    da_ref, dq_ref, dk_ref, dv_ref = fac_ref, one_ref, two_ref, three_ref
    put_wide(da_ref, every, grad_att)
    plan.at("datt")

    def image_back(g, carry):
        batch = [g * some + u for u in range(some)]
        scaled = pair_mask * SCALE
        for b in batch:
            per_image(da_ref, dai_ref, b)
        for b in batch:
            for t in range(4):
                dq = dot(dai_ref[b, :, lane(t)], ctx_ref[b, t], 1, 1) * SCALE
                dq_ref[t, here(b), :] = dq[0:tokens]
        for b in batch:
            for t in range(4):
                full = dot(qi_ref[b, :, lane(t)], dai_ref[b, :, lane(t)], 0, 0)
                ctx_ref[b, t] = (full * scaled).astype(bf16)
        for b in batch:
            for t in range(4):
                dk = dot(vi_ref[b, :, lane(t)], ctx_ref[b, t], 1, 1)
                dk_ref[t, here(b), :] = dk[0:tokens]
                dv = dot(ki_ref[b, :, lane(t)], ctx_ref[b, t])
                dv_ref[t, here(b), :] = dv[0:tokens]
        return carry

    for g in range(4):
        lax.fori_loop(g, g + 1, image_back, 0)
        plan.at("back" + str(g))

    def split(tile, carry):
        bias_q = jnp.zeros((images, LANES), f32)
        bias_all = jnp.zeros((images, LANES), f32)
        dot_sum = jnp.zeros((images, LANES), f32)
        for n in range(tokens):
            grad = da_ref[tile, token(n), :]
            dq = (dq_ref[tile, token(n), :] + grad * conv_ref[tile, token(n), :]).astype(bf16)
            raw_ref[token(n), lane(tile)] = dq
            bias_q = bias_q + dq.astype(f32)
            dc = grad * q_ref[tile, token(n), :]
            da_ref[tile, token(n), :] = dc
            if n > 0:
                bias_all = bias_all + dc
            dot_sum = dot_sum + dk_ref[tile, token(n), :] * ks_ref[tile, token(n), :]
        for n in range(tokens):
            soft = ks_ref[tile, token(n), :]
            raw_ref[token(n), lane(tile + 4)] = (soft * (dk_ref[tile, token(n), :] - dot_sum)).astype(bf16)
        sums_ref[OUT_BIAS_Q, :, lane(tile)] = fold_rows(bias_q)
        sums_ref[OUT_BIAS_ALL, :, lane(tile)] = fold_rows(bias_all)
        return carry

    lax.fori_loop(0, 4, split, 0)
    plan.at("split")

    def grad_joint(target, part):
        grad = dot(h1_ref[...], raw_ref[:, part * width : (part + 1) * width], 0, 0).astype(bf16)
        for t in range(depth):
            target[t, 0:share, :] = grad[t * share : (t + 1) * share, :]
            if target.shape[1] > share:
                target[t, share:, :] = jnp.zeros((target.shape[1] - share, width), bf16)

    grad_joint(gq_ref, 0)
    plan.need("q0")
    plan.at("gq")
    grad_joint(gk_ref, 1)
    plan.need("k0")
    plan.at("gk")
    def values_back(tile, extent):
        first = dv_ref[tile, token(0), :].astype(bf16)
        raw_ref[token(0), lane(tile + 8)] = first
        bias_v = [first.astype(f32)]

        def emit(i, total):
            for j in range(GRID):
                here = cell_rows(images, i * GRID + j)
                dv = (dv_ref[tile, here, :] + total[j]).astype(bf16)
                raw_ref[here, lane(tile + 8)] = dv
                bias_v[0] = bias_v[0] + dv.astype(f32)

        depthwise_rows(
            partial(grid_row, da_ref, tile, images), lambda ab: prm(full_tap(extent, *ab), tile),
            extent, True, emit,
        )
        sums_ref[OUT_BIAS_V, :, lane(tile)] = fold_rows(bias_v[0])

    narrow_tiles(values_back)
    plan.at("values0")
    for tile in (2, 3):
        values_back(tile, 7)
        plan.at("values" + str(tile - 1))
    grad_joint(gv_ref, 2)
    plan.need("v0")
    plan.at("gv")

    def tap_grads(tile, extent):
        extra = (GRID - extent) // 2

        def emit_tap(a, b, total):
            sums_ref[OUT_KERNEL_ALL + (a + extra) * GRID + b + extra, :, lane(tile)] = fold_rows(total)

        kernel_grads(
            partial(grid_row, da_ref, tile, images), partial(grid_row, v_ref, tile, images), extent, emit_tap
        )

    narrow_tiles(tap_grads)
    plan.at("taps0")
    for tile in (2, 3):
        tap_grads(tile, 7)
        plan.at("taps" + str(tile - 1))
    small = jnp.sum(sums_ref[...], axis=1).astype(bf16)
    for t in range(depth):
        gs_ref[t] = jnp.zeros(gs_ref.shape[1:], bf16)
        gs_ref[t, 0 : small.shape[0], :] = small[:, t * share : (t + 1) * share]
    plan.need("s0")
    plan.at("small")

    dh1_ref = one_ref
    for k in range(2):
        at = slice(k * half, (k + 1) * half)
        put_wide(dh1_ref, at, dot(raw_ref[at, :], wj_ref[...], 1, 1))
        plan.at("dh1" + "ab"[k])

    def back(k, carry):
        at = block_at(k)
        grad = wide(dh1_ref, at)
        unit, scale = normalise(wide(x1_ref, at))
        put_wide(da_ref, at, wide(x2_ref, at) + normalise_back(grad, gain_one, unit, scale))
        return carry[0] + fold_rows(grad * unit), carry[1] + fold_rows(grad)

    sums = lax.fori_loop(0, steps // 2, back, (zero, zero))
    plan.at("normback0")
    sums = lax.fori_loop(steps // 2, steps, back, sums)
    plan.at("normback1")
    last_ref[...] = jnp.zeros_like(last_ref)
    last_ref[TAIL_EARLY_GAIN] = sums[0]
    last_ref[TAIL_EARLY_SHIFT] = sums[1]

    def position_back(tile, carry):
        bias = [jnp.zeros((images, LANES), f32)]
        dx_ref[0:images, lane(tile)] = da_ref[tile, 0:images, :].astype(bf16)

        def emit(i, total):
            here = grid_row(da_ref, tile, images, i)
            for j in range(GRID):
                dx_ref[cell_rows(images, i * GRID + j), lane(tile)] = (here[j] + total[j]).astype(bf16)
                bias[0] = bias[0] + here[j]

        depthwise_rows(
            partial(grid_row, da_ref, tile, images),
            lambda ab: prm(ROW_POS_KERNEL + ab[0] * 3 + ab[1], tile),
            3, True, emit,
        )
        last_ref[TAIL_POS_BIAS, :, lane(tile)] = fold_rows(bias[0])

        def emit_tap(a, b, total):
            last_ref[TAIL_POS_KERNEL + a * 3 + b, :, lane(tile)] = fold_rows(total)

        kernel_grads(partial(grid_row, da_ref, tile, images), partial(x_row, tile), 3, emit_tap)
        return carry

    lax.fori_loop(0, 2, position_back, 0)
    plan.at("pos1")
    lax.fori_loop(2, 4, position_back, 0)
    plan.at("pos3")
    written.append(local(dx_ref, results[1]))
    tail_ref[0] = jnp.sum(last_ref[...], axis=1).astype(bf16)
    plan.need("t0")
    plan.at("tail")
    plan.at("end")
    plan.rest()
    for copy in written:
        copy.wait()
    for copy in ring.sent:
        copy.wait_send()


def write_out(
    y_ref, dx_ref, gwo_ref, gwe_ref, gwr_ref, gwq_ref, gwk_ref, gwv_ref, gsm_ref, gtail_ref,
    y_out, dx_out, pk_out, pb_out, eg_out, es_out, jw_out, jb_out, sk_out, sb_out, mk_out, mb_out, lk_out, lb_out,
    ow_out, ob_out, lg_out, ls_out, ew_out, eb_out, rw_out, rb_out,
    y_box, dx_box, q_box, k_box, v_box, o_box, e_box, r_box, jw_box, ow_box, ew_box, rw_box,
    small_ref, in_sems, out_sems,
):
    depth, share = gsm_ref.shape[0], gsm_ref.shape[2]
    width = y_ref.shape[1]
    joint = [
        (ref, box, jw_box.at[:, part * width : (part + 1) * width], jw_out.at[:, part * width : (part + 1) * width])
        for part, (ref, box) in enumerate(((gwq_ref, q_box), (gwk_ref, k_box), (gwv_ref, v_box)))
    ]
    flat = [
        (gwe_ref, e_box, ew_box, ew_out), (gwr_ref, r_box, rw_box, rw_out), (gwo_ref, o_box, ow_box, ow_out),
    ]
    plain = [(y_ref, y_box, y_out), (dx_ref, dx_box, dx_out)]
    sources = [(ref, box) for ref, box, _, _ in flat + joint] + [(ref, box) for ref, box, _ in plain]
    loads = [pltpu.make_async_copy(ref, box, in_sems.at[at]) for at, (ref, box) in enumerate(sources)]
    for load in loads:
        load.start()
    stores = []

    def store(box, out):
        stores.append(pltpu.make_async_copy(box, out, out_sems.at[len(stores)]))
        stores[-1].start()

    for at, (_, box, wide_box, out) in enumerate(flat):
        loads[at].wait()
        wide_box[...] = box[0 : wide_box.shape[0], :].astype(f32)
        store(wide_box, out)
    for at, (_, box, wide_box, out) in enumerate(joint):
        loads[3 + at].wait()
        for t in range(depth):
            wide_box[t * share : (t + 1) * share, :] = box[t, 0:share, :].astype(f32)
        store(wide_box, out)
    for at, (_, box, out) in enumerate(plain):
        loads[6 + at].wait()
        store(box, out)
    for t in range(depth):
        small_ref[:, t * share : (t + 1) * share] = gsm_ref[t].astype(f32)
    for at, out in (
        (OUT_OUT_BIAS, ob_out), (OUT_LATE_GAIN, lg_out), (OUT_LATE_SHIFT, ls_out), (OUT_REDUCE_BIAS, rb_out),
    ):
        out[...] = small_ref[at, :]
    jb_out[0:width] = small_ref[OUT_BIAS_Q, :]
    jb_out[width:] = small_ref[OUT_BIAS_V, :]
    cw = eb_out.shape[0]
    mine = small_ref[pl.ds(OUT_EXPAND_BIAS + lax.axis_index("tensor"), 1), 0:cw]
    eb_out[...] = mine.reshape(cw)
    first_lane = 0
    for kernel_out, bias_out in ((sk_out, sb_out), (mk_out, mb_out), (lk_out, lb_out)):
        extent, count = kernel_out.shape[0], kernel_out.shape[2]
        span = slice(first_lane, first_lane + count)
        bias_out[...] = small_ref[OUT_BIAS_ALL, span]
        for a in range(extent):
            at = full_tap(extent, a, 0) - ROW_KERNEL_ALL + OUT_KERNEL_ALL
            kernel_out[a] = small_ref[at : at + extent, span]
        first_lane += count
    for a in range(3):
        at = TAIL_POS_KERNEL + 3 * a
        pk_out[a] = gtail_ref[at : at + 3, :]
    for at, out in ((TAIL_POS_BIAS, pb_out), (TAIL_EARLY_GAIN, eg_out), (TAIL_EARLY_SHIFT, es_out)):
        out[...] = gtail_ref[at, :]
    for copy in stores:
        copy.wait()


def per_device(
    block_input, position_kernel, position_bias, early_gain, early_shift, joint_weight, joint_bias,
    small_kernel, small_bias, middle_kernel, middle_bias, large_kernel, large_bias,
    output_weight, output_bias, late_gain, late_shift, expand_weight, expand_bias,
    reduce_weight, reduce_bias, cotangent,
):
    images, tokens, width = block_input.shape
    rows = images * tokens
    depth, copies_of = lax.axis_size("tensor"), lax.axis_size("dp")
    planes = math.gcd(copies_of // 2, 4)
    pieces = 2 * planes
    share, cw = width // depth, expand_weight.shape[1]
    unit = 16 * pieces
    sum_rows = padded(OUT_EXPAND_BIAS + depth, 16)
    shapes = [
        (padded(share, unit), width), (padded(width, unit), cw), (padded(cw, unit), width),
        (padded(share, unit), width), (padded(share, unit), width), (padded(share, unit), width),
        (padded(sum_rows, unit), share),
    ]
    near, far = planes - 1, depth - 1
    copies = far + 3 * far * (2 + near) + 2 * depth * 6 + 5 * (1 + near) + 7 * far + 4 * far + 5 * near + 2 * 5 + 7
    copies += 1 + near + far
    fill = lambda array, count: jnp.pad(array, ((0, count - array.shape[0]), (0, 0)))
    vmem = lambda shape, dtype=bf16: pltpu.VMEM(shape, dtype)
    tail = (TAIL_ROWS, width)
    flat = lambda array: array.transpose(1, 0, 2).reshape(rows, width)
    given = (
        flat(block_input), flat(cotangent), joint_weight, position_kernel, position_bias, early_gain, early_shift,
        joint_bias, small_kernel, small_bias, middle_kernel, middle_bias, large_kernel, large_bias, output_bias,
        late_gain, late_shift, reduce_bias, expand_bias,
        fill(output_weight, shapes[0][0]), fill(expand_weight, shapes[1][0]), fill(reduce_weight, shapes[2][0]),
    )
    outs = [
        ((rows, width), bf16), ((rows, width), bf16),
        (shapes[0], bf16), (shapes[1], bf16), (shapes[2], bf16),
        ((depth,) + shapes[3], bf16), ((depth,) + shapes[4], bf16), ((depth,) + shapes[5], bf16),
        ((depth,) + shapes[6], bf16), (tail, f32),
    ]
    scratch = (
        [vmem(array.shape) for array in given[:19]] + [vmem(shape, dtype) for shape, dtype in outs] +
        [vmem((PARAM_ROWS, width), f32)]
        + [vmem((4, rows, LANES), f32)] * 10
        + [vmem((rows, width))] * 3 + [vmem((rows, 3 * width))]
        + [vmem((images, PAD_TOK, width))] * 4 + [vmem((images, 4, LANES, LANES))]
        + [vmem((sum_rows, 8, width), f32), vmem((TAIL_ROWS, 8, width), f32)]
        + [vmem((depth,) + shape) for shape in shapes[:3]] + [vmem((depth, 8, cw), f32)]
        + [vmem((depth,) + shape) for shape in shapes]
        + [vmem((depth, r // 2, w)) for r, w in shapes]
        + [vmem((near, depth, r // pieces, w)) for r, w in shapes[:1] + shapes[3:]]
        + [
            vmem(shape)
            for r, w in shapes[1:3]
            for shape in (
                (depth, 2, r // pieces, w // 2), (depth, 2 * r // pieces, w // 2),
                (depth, r // pieces, w // 2), (depth, r // pieces, w // 2),
            )
        ]
        + [vmem((far, r // pieces, w)) for r, w in shapes]
        + [vmem((3,) + tail), vmem((1,) + tail), vmem((near,) + tail), vmem((far,) + tail)]
        + [pltpu.SemaphoreType.DMA((copies,))] * 2 + [pltpu.SemaphoreType.DMA((32,))]
    )
    anywhere = pl.BlockSpec(memory_space=pl.ANY)
    inside = pl.BlockSpec(memory_space=pltpu.VMEM)
    made = pl.pallas_call(
        partial(whole_block, images, tokens, planes, depth),
        out_shape=[jax.ShapeDtypeStruct(shape, dtype) for shape, dtype in outs],
        in_specs=[anywhere] * 22,
        out_specs=[anywhere] * len(outs),
        scratch_shapes=scratch,
        compiler_params=pltpu.CompilerParams(
            vmem_limit_bytes=VMEM_BYTES, collective_id=1, has_side_effects=True
        ),
    )(*given)
    if copies_of > pieces:
        groups = [list(range(first, copies_of, pieces)) for first in range(pieces)]
        made = list(made[:2]) + list(lax.psum(tuple(made[2:]), "dp", axis_index_groups=groups))
    like = lambda array: jax.ShapeDtypeStruct(array.shape, f32)
    results = pl.pallas_call(
        write_out,
        out_shape=[jax.ShapeDtypeStruct((rows, width), bf16)] * 2 + [
            like(array) for array in (
                position_kernel, position_bias, early_gain, early_shift, joint_weight, joint_bias,
                small_kernel, small_bias, middle_kernel, middle_bias, large_kernel, large_bias,
                output_weight, output_bias, late_gain, late_shift, expand_weight, expand_bias,
                reduce_weight, reduce_bias,
            )
        ],
        in_specs=[anywhere] * 8 + [inside] * 2,
        out_specs=[
            anywhere if at in (0, 1, 6, 14, 18, 20) else inside for at in range(22)
        ],
        scratch_shapes=[vmem((rows, width))] * 2
        + [vmem((depth,) + shape) for shape in shapes[3:6]] + [vmem(shape) for shape in shapes[:3]]
        + [vmem(array.shape, f32) for array in (joint_weight, output_weight, expand_weight, reduce_weight)]
        + [vmem((shapes[6][0], width), f32), pltpu.SemaphoreType.DMA((8,)), pltpu.SemaphoreType.DMA((8,))],
        compiler_params=pltpu.CompilerParams(vmem_limit_bytes=VMEM_BYTES),
    )(*made)
    image_form = lambda array: array.reshape(tokens, images, width).transpose(1, 0, 2)
    return (image_form(results[0]), image_form(results[1])) + tuple(results[2:])


def solution(mesh):
    images = P(("dp", "tensor"), None, None)
    in_specs = (images,) + (P(),) * 12 + (
        P("tensor", None), P(), P(), P(), P(None, "tensor"), P("tensor"), P("tensor", None), P(), images,
    )
    out_specs = (images, images) + (P(),) * 12 + (
        P("tensor", None), P(), P(), P(), P(None, "tensor"), P("tensor"), P("tensor", None), P(),
    )
    return jax.shard_map(per_device, mesh=mesh, in_specs=in_specs, out_specs=out_specs, check_vma=False)
```

```python
import math
from functools import partial

import jax
import jax.numpy as jnp
from jax import lax
from jax.experimental import pallas as pl
from jax.experimental.pallas import tpu as pltpu
from jax.sharding import PartitionSpec as P

HEADS = 8
HEAD = 64
GRID = 7
CELLS = GRID * GRID
NORM_EPS = 1e-06
SCALE = HEAD**-0.5
LANES = 128
GROUP = 256
PAD_TOK = 64
VMEM_BYTES = 62 * 1024 * 1024

f32 = jnp.float32
bf16 = jnp.bfloat16

ROW_POS_BIAS, ROW_EARLY_GAIN, ROW_EARLY_SHIFT, ROW_BIAS_Q, ROW_BIAS_V = 0, 1, 2, 3, 4
ROW_BIAS_ALL, ROW_OUT_BIAS, ROW_LATE_GAIN, ROW_LATE_SHIFT, ROW_REDUCE_BIAS = 5, 6, 7, 8, 9
ROW_POS_KERNEL, ROW_KERNEL_ALL = 10, 19
PARAM_ROWS = 72

OUT_KERNEL_ALL, OUT_BIAS_Q, OUT_BIAS_V, OUT_BIAS_ALL = 0, 49, 50, 51
OUT_LATE_GAIN, OUT_LATE_SHIFT, OUT_OUT_BIAS, OUT_REDUCE_BIAS, OUT_EXPAND_BIAS = 52, 53, 54, 55, 56
TAIL_POS_KERNEL, TAIL_POS_BIAS, TAIL_EARLY_GAIN, TAIL_EARLY_SHIFT, TAIL_ROWS = 0, 9, 10, 11, 16
MESH = pl.DeviceIdType.MESH

SCHEDULE = {
    "qdot": ("wo1",),
    "conv1": ("g1 1",),
    "image2": ("wo2",),
    "outproj": ("g1 2",),
    "chunk0a": ("g1 3",),
    "chunk0b": ("g2 1",),
    "chunk0f": ("g3 1",),
    "chunk1b": ("f1 0", "g2 2",),
    "chunk1f": ("g3 2",),
    "chunk2b": ("f1 1",),
    "chunk2c": ("g2 3",),
    "chunk3a": ("f2 0", "f1 2",),
    "chunk3c": ("f2 1",),
    "finish0": ("f3 0", "f1 3",),
    "finish1": ("f2 2",),
    "gwo": ("f3 1",),
    "back0": ("o1",),
    "back1": ("f2 3",),
    "back2": ("f3 2",),
    "gq": ("o2",),
    "values0": ("f3 3",),
    "values1": ("q1",),
    "values2": ("k1",),
    "taps2": ("o3", "v1",),
    "dh1a": ("q2",),
    "dh1b": ("f4", "s1",),
    "normback0": ("k2",),
    "normback1": ("o4",),
    "pos3": ("q3", "o5",),
    "tail": ("v2",),
    "end": ("k3", "f5", "s2", "t1", "q4", "v3", "k4", "f6", "s3", "t2", "f7", "v4", "q5", "s4", "t3", "q6", "k5", "k6", "v5", "s5", "v6", "s6",),
}


def lane(tile):
    if isinstance(tile, int):
        return slice(tile * LANES, (tile + 1) * LANES)
    return pl.ds(pl.multiple_of(tile * LANES, LANES), LANES)


def taps(extent):
    return range(extent)


def columns(shift):
    return range(max(0, -shift), min(GRID, GRID - shift))


def depthwise_rows(get_row, get_weight, extent, flip, emit):
    margin = extent // 2
    for i in range(GRID):
        total = [None] * GRID
        for a in range(extent):
            r = i + a - margin
            if not 0 <= r < GRID:
                continue
            row = get_row(r)
            for b in range(extent):
                weight = get_weight((extent - 1 - a, extent - 1 - b) if flip else (a, b))
                for j in columns(b - margin):
                    term = row[j + b - margin] * weight
                    total[j] = term if total[j] is None else total[j] + term
        emit(i, total)


def kernel_grads(get_left, get_right, extent, emit):
    margin = extent // 2
    for a in range(extent):
        total = [None] * extent
        for i in range(GRID):
            r = i + a - margin
            if not 0 <= r < GRID:
                continue
            left, right = get_left(i), get_right(r)
            for b in range(extent):
                for j in columns(b - margin):
                    term = left[j] * right[j + b - margin]
                    total[b] = term if total[b] is None else total[b] + term
        for b in range(extent):
            emit(a, b, total[b])


def cell_rows(images, cell, count=1):
    return slice((1 + cell) * images, (1 + cell + count) * images)


def grid_row(ref, tile, images, i):
    block = ref[tile, cell_rows(images, i * GRID, GRID), :]
    return [block[j * images : (j + 1) * images] for j in range(GRID)]


def full_tap(extent, a, b):
    extra = (GRID - extent) // 2
    return ROW_KERNEL_ALL + (a + extra) * GRID + b + extra


def narrow_tiles(body):
    body(0, 3)
    body(1, 5)


def normalise(block):
    centre = jnp.mean(block, axis=-1, keepdims=True)
    centred = block - centre
    spread = jnp.mean(centred * centred, axis=-1, keepdims=True)
    scale = lax.rsqrt(spread + NORM_EPS)
    return centred * scale, scale


def normalise_back(grad, gain, unit, scale):
    scaled = grad * gain
    mean_one = jnp.mean(scaled, axis=-1, keepdims=True)
    mean_two = jnp.mean(scaled * unit, axis=-1, keepdims=True)
    return (scaled - mean_one - unit * mean_two) * scale


def fold_rows(block):
    return jnp.sum(block.reshape(block.shape[0] // 8, 8, block.shape[1]), axis=0)


def dot(left, right, left_dim=1, right_dim=0):
    return lax.dot_general(
        left, right, (((left_dim,), (right_dim,)), ((), ())), preferred_element_type=f32
    )


def padded(count, unit):
    return -(-count // unit) * unit


class Ring:
    def __init__(self, pairs, depth, send_sems, recv_sems):
        self.dp = lax.axis_index("dp")
        self.me = lax.axis_index("tensor")
        self.planes, self.depth = pairs, depth
        group = 2 * pairs
        self.base = lax.div(self.dp, group) * group
        self.core = lax.rem(self.dp, 2)
        self.spot = lax.div(lax.rem(self.dp, group), 2)
        self.send_sems, self.recv_sems, self.used = send_sems, recv_sems, 0
        self.sent = []

    def twin(self):
        return {"dp": self.base + self.spot * 2 + (1 - self.core), "tensor": self.me}

    def plane(self, k):
        return {"dp": self.base + lax.rem(self.spot + k, self.planes) * 2 + self.core, "tensor": self.me}

    def plane_spot(self, k):
        return lax.rem(self.spot + k, self.planes)

    def across(self, k):
        return {"dp": self.base + self.beside(k) * 2 + self.core, "tensor": self.me}

    def beside(self, k):
        low, high = lax.rem(self.spot, 2), lax.div(self.spot, 2)
        return high * 2 + 1 - low if k == 1 else (1 - high) * 2 + low

    def stack(self, k):
        return {"dp": self.dp, "tensor": lax.rem(self.me + k, self.depth)}

    def everyone(self):
        return (
            [self.twin()]
            + [self.plane(k) for k in range(1, self.planes)]
            + [self.stack(k) for k in range(1, self.depth)]
        )

    def piece(self, rows, spot, core=None):
        each = rows // (2 * self.planes)
        core = self.core if core is None else core
        return pl.ds(pl.multiple_of((core * self.planes + spot) * each, each), each)

    def band(self, rows, high):
        each = rows // (2 * self.planes)
        start = (self.core * self.planes + high * 2) * each
        return pl.ds(pl.multiple_of(start, 2 * each), 2 * each)

    def half(self, rows, core):
        return pl.ds(pl.multiple_of(core * (rows // 2), rows // 2), rows // 2)

    def send(self, source, target, device):
        at = self.used
        self.used += 1
        copy = pltpu.make_async_remote_copy(
            src_ref=source, dst_ref=target, send_sem=self.send_sems.at[at], recv_sem=self.recv_sems.at[at],
            device_id=device, device_id_type=MESH,
        )
        copy.start()
        self.sent.append(copy)
        return copy


def arrive(copies):
    for copy in copies:
        copy.wait_recv()


class Reduction:
    def __init__(self, ring, grads, twin_box, plane_box, stack_box, out, whole, relative):
        self.ring, self.grads, self.out, self.whole, self.relative = ring, grads, out, whole, relative
        self.twin_box, self.plane_box, self.stack_box = twin_box, plane_box, stack_box
        self.rows = grads.shape[1]
        self.depth = grads.shape[0]
        self.pairs, self.planes, self.stacks = {}, {}, {}
        self.all = slice(0, self.depth)

    def slot(self, k):
        return k if self.relative else lax.rem(self.ring.me + k, self.depth)

    def pair(self, part):
        ring = self.ring
        away = ring.half(self.rows, 1 - ring.core)
        self.pairs[str(part)] = ring.send(self.grads.at[part, away], self.twin_box.at[part], ring.twin())

    def meet(self, part):
        ring = self.ring
        arrive([self.pairs[str(part)]])
        mine = ring.half(self.rows, ring.core)
        self.grads[part, mine] = (
            self.grads[part, mine].astype(f32) + self.twin_box[part].astype(f32)
        ).astype(bf16)

    def plane(self, part):
        ring = self.ring
        self.meet(part)
        self.planes[str(part)] = [
            ring.send(
                self.grads.at[part, ring.piece(self.rows, ring.plane_spot(k))],
                self.plane_box.at[k - 1, part], ring.plane(k),
            )
            for k in range(1, ring.planes)
        ]

    def gather_plane(self, part):
        ring = self.ring
        arrive(self.planes[str(part)])
        mine = ring.piece(self.rows, ring.spot)
        total = self.grads[part, mine].astype(f32)
        for k in range(1, ring.planes):
            total = total + self.plane_box[k - 1, part].astype(f32)
        self.grads[part, mine] = total.astype(bf16)

    def stack(self, offsets=None):
        ring = self.ring
        mine = ring.piece(self.rows, ring.spot)
        for k in range(1, self.depth) if offsets is None else offsets:
            self.stacks[k] = ring.send(self.grads.at[self.slot(k), mine], self.stack_box.at[k - 1], ring.stack(k))

    def settle(self):
        ring = self.ring
        arrive(self.stacks.values())
        mine = ring.piece(self.rows, ring.spot)
        total = self.grads[self.slot(0), mine].astype(f32)
        for k in self.stacks:
            total = total + self.stack_box[k - 1].astype(f32)
        done = total.astype(bf16)
        if self.whole:
            self.out[ring.me, mine] = done
            place = self.out.at[ring.me, mine]
            self.spread = [ring.send(place, place, ring.stack(k)) for k in range(1, self.depth)]
        else:
            self.out[mine] = done
            self.to_plane()

    def to_plane(self):
        ring = self.ring
        mine = ring.piece(self.rows, ring.spot)
        if self.whole:
            arrive(self.spread)
            place = self.out.at[:, mine]
        else:
            place = self.out.at[mine]
        self.back = [ring.send(place, place, ring.plane(k)) for k in range(1, ring.planes)]

    def to_twin(self):
        ring = self.ring
        arrive(self.back)
        mine = ring.half(self.rows, ring.core)
        place = self.out.at[:, mine] if self.whole else self.out.at[mine]
        self.last = ring.send(place, place, ring.twin())

    def finish(self):
        arrive([self.last])


class TwoPhase(Reduction):
    def __init__(self, ring, grads, twin_box, plane_boxes, stack_box, out, whole, relative):
        super().__init__(ring, grads, twin_box, None, stack_box, out, whole, relative)
        self.first_box, self.band_box, self.low_box, self.high_box = plane_boxes
        self.cut = grads.shape[2] // 2
        self.ones, self.twos = {}, {}

    def add(self, part, at, columns, box):
        self.grads[part, at, columns] = (self.grads[part, at, columns].astype(f32) + box.astype(f32)).astype(bf16)

    def phase_one(self, part):
        ring = self.ring
        self.meet(part)
        left, right = slice(0, self.cut), slice(self.cut, 2 * self.cut)
        low, high = lax.rem(ring.spot, 2), lax.div(ring.spot, 2)
        self.ones[str(part)] = [
            ring.send(
                self.grads.at[part, ring.piece(self.rows, 2 * y + 1 - low), left],
                self.first_box.at[part, y], ring.across(1),
            )
            for y in range(2)
        ] + [
            ring.send(
                self.grads.at[part, ring.band(self.rows, 1 - high), right], self.band_box.at[part], ring.across(2)
            )
        ]

    def phase_two(self, part):
        ring = self.ring
        left, right = slice(0, self.cut), slice(self.cut, 2 * self.cut)
        low, high = lax.rem(ring.spot, 2), lax.div(ring.spot, 2)
        arrive(self.ones[str(part)])
        for y in range(2):
            self.add(part, ring.piece(self.rows, 2 * y + low), left, self.first_box[part, y])
        self.add(part, ring.band(self.rows, high), right, self.band_box[part])
        self.twos[str(part)] = [
            ring.send(
                self.grads.at[part, ring.piece(self.rows, ring.beside(2)), left], self.high_box.at[part], ring.across(2)
            ),
            ring.send(
                self.grads.at[part, ring.piece(self.rows, ring.beside(1)), right], self.low_box.at[part], ring.across(1)
            ),
        ]

    def to_plane(self):
        if self.whole:
            super().to_plane()
            return
        ring = self.ring
        mine = ring.piece(self.rows, ring.spot)
        left, right = self.out.at[mine, 0 : self.cut], self.out.at[mine, self.cut : 2 * self.cut]
        self.ahead = [ring.send(left, left, ring.across(2)), ring.send(right, right, ring.across(1))]

    def to_plane_two(self):
        ring = self.ring
        arrive(self.ahead)
        low, high = lax.rem(ring.spot, 2), lax.div(ring.spot, 2)
        places = [self.out.at[ring.piece(self.rows, 2 * y + low), 0 : self.cut] for y in range(2)]
        band = self.out.at[ring.band(self.rows, high), self.cut : 2 * self.cut]
        self.back = [ring.send(place, place, ring.across(1)) for place in places]
        self.back.append(ring.send(band, band, ring.across(2)))

    def gather_plane(self, part):
        ring = self.ring
        arrive(self.twos[str(part)])
        mine = ring.piece(self.rows, ring.spot)
        self.add(part, mine, slice(0, self.cut), self.high_box[part])
        self.add(part, mine, slice(self.cut, 2 * self.cut), self.low_box[part])


class Gather:
    def __init__(self, ring, shard, box, relative):
        self.ring, self.shard, self.box, self.relative = ring, shard, box, relative
        self.depth, self.rows = box.shape[0], box.shape[1]
        self.first, self.second, self.third = {}, {}, {}

    def slot(self, j):
        return j if self.relative else lax.rem(self.ring.me + j, self.depth)

    def start(self, j):
        ring = self.ring
        mine = ring.piece(self.rows, ring.spot)
        target = self.box.at[j if self.relative else ring.me, mine]
        self.first[j] = ring.send(self.shard.at[mine], target, ring.stack(self.depth - j))

    def plane(self, j):
        ring = self.ring
        arrive([self.first[j]])
        place = self.box.at[self.slot(j), ring.piece(self.rows, ring.spot)]
        self.second[j] = [ring.send(place, place, ring.plane(k)) for k in range(1, ring.planes)]

    def pair(self, j):
        ring = self.ring
        arrive(self.second[j])
        place = self.box.at[self.slot(j), ring.half(self.rows, ring.core)]
        self.third[j] = ring.send(place, place, ring.twin())

    def finish(self, j):
        arrive([self.third[j]])


class Tail:
    def __init__(self, ring, mine, boxes):
        self.ring, self.mine, self.boxes = ring, mine, boxes

    def start(self, stage):
        ring = self.ring
        devices = (
            [ring.twin()],
            [ring.plane(k) for k in range(1, ring.planes)],
            [ring.stack(k) for k in range(1, ring.depth)],
        )[stage]
        self.copies = [
            ring.send(self.mine.at[stage], self.boxes[stage].at[k], device) for k, device in enumerate(devices)
        ]

    def collect(self, stage):
        total = self.mine[stage].astype(f32)
        for k, copy in enumerate(self.copies):
            copy.wait_recv()
            total = total + self.boxes[stage][k].astype(f32)
        if stage < 2:
            self.mine[stage + 1] = total.astype(bf16)
            self.start(stage + 1)
        return total


class Plan:
    def __init__(self, schedule):
        self.schedule, self.steps, self.done = schedule, {}, set()

    def add(self, name, needs, action):
        self.steps[name] = (needs, action)

    def need(self, name):
        if name in self.done:
            return
        needs, action = self.steps[name]
        for other in needs:
            self.need(other)
        self.done.add(name)
        action()

    def at(self, point):
        for name in self.schedule.get(point, ()):
            if name in self.steps:
                self.need(name)

    def rest(self):
        for name in self.steps:
            self.need(name)


def each(parts, step_name, *args):
    for part in parts:
        getattr(part, step_name)(*args)


def wide(ref, at):
    return jnp.concatenate([ref[tile, at, :] for tile in range(4)], axis=1)


def put_wide(ref, at, block):
    for tile in range(4):
        ref[tile, at, :] = block[:, lane(tile)]


def whole_block(
    images, tokens, planes, depth, *refs,
):
    given, refs = refs[:22], refs[22:]
    results, refs = refs[:10], refs[10:]
    held, refs = refs[:19], refs[19:]
    boxes, refs = refs[:10], refs[10:]
    (
        x_ref, cot_ref, wj_ref, pk_ref, pb_ref, eg_ref, es_ref, jb_ref, sk_ref, sb_ref, mk_ref, mb_ref,
        lk_ref, lb_ref, ob_ref, lg_ref, ls_ref, rb_ref, eb_shard,
    ) = held
    wo_shard, we_shard, wr_shard = given[19:]
    y_ref, dx_ref, gwo_ref, gwe_ref, gwr_ref, gwq_ref, gwk_ref, gwv_ref, gsm_ref, gtail_ref = boxes
    (
        prm_ref, x1_ref, x2_ref, q_ref, v_ref, ks_ref, conv_ref, fac_ref, one_ref, two_ref, three_ref,
        h1_ref, att_ref, h2_ref, raw_ref,
        qi_ref, ki_ref, vi_ref, dai_ref, ctx_ref, sums_ref, last_ref,
        wo_ref, we_ref, wr_ref, eb_ref,
        go_ref, ge_ref, gr_ref, gq_ref, gk_ref, gv_ref, gs_ref,
        to_ref, te_ref, tr_ref, tq_ref, tk_ref, tv_ref, ts_ref,
        po_ref, pq_ref, pk2_ref, pv_ref, ps_ref,
        e_first, e_band, e_low, e_high, r_first, r_band, r_low, r_high,
        so_ref, se_ref, sr_ref, sq_ref, sk2_ref, sv_ref, ss_ref,
        tail_ref, tail_pair, tail_plane, tail_stack,
        send_sems, recv_sems, local_sems,
    ) = refs
    ring = Ring(planes, depth, send_sems, recv_sems)
    barrier = pltpu.get_barrier_semaphore()
    for device in ring.everyone():
        pl.semaphore_signal(barrier, inc=1, device_id=device, device_id_type=MESH)

    rows = images * tokens
    width = 4 * LANES
    step = 5 * images
    steps = rows // step
    share = width // depth
    cw = we_ref.shape[2]
    get_out = Gather(ring, wo_shard, wo_ref, False)
    get_expand = Gather(ring, we_shard, we_ref, True)
    get_reduce = Gather(ring, wr_shard, wr_ref, True)
    feed_in = (get_expand, get_reduce)
    slots = range(1, depth)
    used = []

    def local(source, target):
        copy = pltpu.make_async_copy(source, target, local_sems.at[len(used)])
        copy.start()
        used.append(copy)
        return copy

    loads = [local(source, target) for source, target in zip(given, held)]
    pl.semaphore_wait(barrier, planes + depth - 1)
    order = list(slots)
    plan = Plan(SCHEDULE)

    def chain(name, parts, suffix, actions, first=()):
        before = list(first)
        for at, action in enumerate(actions):
            label = name + str(at) + suffix
            plan.add(label, before, action)
            before = [label]

    def calls(parts, step_name, *args):
        return partial(each, parts, step_name, *args)

    def out_all(step_name):
        for j in slots:
            getattr(get_out, step_name)(j)

    chain("wo", None, "", [partial(out_all, name) for name in ("start", "plane", "pair", "finish")])
    for j in slots:
        chain("g", None, " " + str(j), [calls(feed_in, name, j) for name in ("start", "plane", "pair", "finish")])
    plan.need("wo0")
    plan.need("g0 1")
    own = [
        local(source, target)
        for source, target in ((wo_shard, wo_ref.at[ring.me]), (we_shard, we_ref.at[0]), (wr_shard, wr_ref.at[0]))
    ]
    for copy in [loads[0]] + loads[3:]:
        copy.wait()
    eb_ref[0] = jnp.broadcast_to(eb_shard[...].astype(f32).reshape(1, cw), (8, cw))

    get_bias = [ring.send(eb_ref.at[0], eb_ref.at[j], ring.stack(depth - j)) for j in slots]

    for at, ref in (
        (ROW_POS_BIAS, pb_ref), (ROW_EARLY_GAIN, eg_ref), (ROW_EARLY_SHIFT, es_ref), (ROW_OUT_BIAS, ob_ref),
        (ROW_LATE_GAIN, lg_ref), (ROW_LATE_SHIFT, ls_ref), (ROW_REDUCE_BIAS, rb_ref),
    ):
        prm_ref[at : at + 1, :] = ref[...].astype(f32).reshape(1, width)
    prm_ref[ROW_BIAS_Q : ROW_BIAS_Q + 1, :] = jb_ref[0:width].astype(f32).reshape(1, width)
    prm_ref[ROW_BIAS_V : ROW_BIAS_V + 1, :] = jb_ref[width : 2 * width].astype(f32).reshape(1, width)
    prm_ref[ROW_KERNEL_ALL:PARAM_ROWS, :] = jnp.zeros((PARAM_ROWS - ROW_KERNEL_ALL, width), f32)
    first_lane = 0
    for kernel_ref, bias_ref in ((sk_ref, sb_ref), (mk_ref, mb_ref), (lk_ref, lb_ref)):
        extent, count = kernel_ref.shape[0], kernel_ref.shape[2]
        span = slice(first_lane, first_lane + count)
        prm_ref[ROW_BIAS_ALL : ROW_BIAS_ALL + 1, span] = bias_ref[...].astype(f32).reshape(1, count)
        for a in range(extent):
            at = full_tap(extent, a, 0)
            prm_ref[at : at + extent, span] = kernel_ref[a].astype(f32)
        first_lane += count
    for a in range(3):
        prm_ref[ROW_POS_KERNEL + 3 * a : ROW_POS_KERNEL + 3 * a + 3, :] = pk_ref[a].astype(f32)

    prm = lambda row, tile: prm_ref[row : row + 1, lane(tile)]
    row = lambda r: prm_ref[r : r + 1, :]
    block_at = lambda k: pl.ds(pl.multiple_of(k * step, step), step)

    x_row = lambda tile, i: [
        x_ref[cell_rows(images, i * GRID + j), lane(tile)].astype(f32) for j in range(GRID)
    ]

    def position(tile, carry):
        x1_ref[tile, 0:images, :] = x_ref[0:images, lane(tile)].astype(f32)
        bias = prm(ROW_POS_BIAS, tile)

        def emit(i, total):
            here = x_row(tile, i)
            for j in range(GRID):
                x1_ref[tile, cell_rows(images, i * GRID + j), :] = here[j] + total[j] + bias

        depthwise_rows(
            partial(x_row, tile), lambda ab: prm(ROW_POS_KERNEL + ab[0] * 3 + ab[1], tile), 3, False, emit
        )
        return carry

    lax.fori_loop(0, 4, position, 0)
    for j in slots:
        plan.need("g0 " + str(j))
    plan.at("position")

    def norm_of(source, target, gain, shift):
        def norm(k, carry):
            at = block_at(k)
            unit, _ = normalise(wide(source, at))
            target[at, :] = (unit * gain + shift).astype(bf16)
            return carry

        lax.fori_loop(0, steps, norm, 0)

    gain_one, shift_one = row(ROW_EARLY_GAIN), row(ROW_EARLY_SHIFT)
    norm_of(x1_ref, h1_ref, gain_one, shift_one)
    plan.at("norm1b")
    every = slice(0, rows)
    loads[2].wait()
    put_wide(v_ref, every, (dot(h1_ref[...], wj_ref[:, 2 * width :]) + row(ROW_BIAS_V)).astype(bf16).astype(f32))
    plan.at("vdot")
    put_wide(ks_ref, every, dot(h1_ref[...], wj_ref[:, width : 2 * width]).astype(bf16).astype(f32))
    plan.at("kdot")
    put_wide(q_ref, every, (dot(h1_ref[...], wj_ref[:, :width]) + row(ROW_BIAS_Q)).astype(bf16).astype(f32))
    plan.at("qdot")

    token = lambda n: slice(n * images, (n + 1) * images)

    def soften(tile, carry):
        top = ks_ref[tile, token(0), :]
        for n in range(1, tokens):
            top = jnp.maximum(top, ks_ref[tile, token(n), :])
        total = jnp.zeros_like(top)
        for n in range(tokens):
            e = jnp.exp(ks_ref[tile, token(n), :] - top)
            ks_ref[tile, token(n), :] = e
            total = total + e
        scale = 1.0 / total
        for n in range(tokens):
            ks_ref[tile, token(n), :] = ks_ref[tile, token(n), :] * scale
        return carry

    lax.fori_loop(0, 4, soften, 0)
    plan.at("soft3")

    def convolve(tile, extent):
        conv_ref[tile, 0:images, :] = jnp.zeros((images, LANES), f32)
        bias = prm(ROW_BIAS_ALL, tile)

        def emit(i, total):
            for j in range(GRID):
                conv_ref[tile, cell_rows(images, i * GRID + j), :] = total[j] + bias

        depthwise_rows(
            partial(grid_row, v_ref, tile, images), lambda ab: prm(full_tap(extent, *ab), tile),
            extent, False, emit,
        )

    narrow_tiles(convolve)
    plan.at("conv0")
    for tile in (2, 3):
        convolve(tile, 7)
        plan.at("conv" + str(tile - 1))

    some = images // 4
    lanes_of = lax.broadcasted_iota(jnp.int32, (LANES, LANES), 1) // HEAD
    rows_of = lax.broadcasted_iota(jnp.int32, (LANES, LANES), 0) // HEAD
    pair_mask = jnp.where(lanes_of == rows_of, 1.0, 0.0)
    here = lambda b: pl.ds(b, tokens, stride=images)

    def per_image(source, target, b):
        target[b, 48:PAD_TOK, :] = jnp.zeros((PAD_TOK - 48, width), bf16)
        for tile in range(4):
            target[b, 0:tokens, lane(tile)] = source[tile, here(b), :].astype(bf16)

    def image(g, carry):
        batch = [g * some + u for u in range(some)]
        for b in batch:
            for source, target in ((ks_ref, ki_ref), (v_ref, vi_ref), (q_ref, qi_ref)):
                per_image(source, target, b)
        for b in batch:
            for t in range(4):
                full = dot(ki_ref[b, :, lane(t)], vi_ref[b, :, lane(t)], 0, 0)
                ctx_ref[b, t] = (full * pair_mask).astype(bf16)
        for b in batch:
            for t in range(4):
                out = dot(qi_ref[b, :, lane(t)], ctx_ref[b, t]) * SCALE
                fac_ref[t, here(b), :] = out[0:tokens]
        return carry

    for g in range(4):
        lax.fori_loop(g, g + 1, image, 0)
        plan.at("image" + str(g))

    def combine(tile, carry):
        att_ref[:, lane(tile)] = (fac_ref[tile] + q_ref[tile] * conv_ref[tile]).astype(bf16)
        return carry

    lax.fori_loop(0, 4, combine, 0)

    loads[1].wait()
    for copy in own:
        copy.wait()
    plan.at("combine")
    plan.need("wo3")
    whole_out = jnp.concatenate([wo_ref[t, 0:share, :] for t in range(depth)], axis=0)
    branch = dot(att_ref[...], whole_out) + row(ROW_OUT_BIAS)
    for tile in range(4):
        x2_ref[tile] = x1_ref[tile] + branch[:, lane(tile)]
    gain_two, shift_two = row(ROW_LATE_GAIN), row(ROW_LATE_SHIFT)
    plan.at("outproj")
    norm_of(x2_ref, h2_ref, gain_two, shift_two)
    plan.at("norm2b")

    e_boxes, r_boxes = (e_first, e_band, e_low, e_high), (r_first, r_band, r_low, r_high)
    send_expand = TwoPhase(ring, ge_ref, te_ref, e_boxes, se_ref, gwe_ref, False, True)
    send_reduce = TwoPhase(ring, gr_ref, tr_ref, r_boxes, sr_ref, gwr_ref, False, True)
    send_out = Reduction(ring, go_ref, to_ref, po_ref, so_ref, gwo_ref, False, False)
    send_q = Reduction(ring, gq_ref, tq_ref, pq_ref, sq_ref, gwq_ref, True, False)
    send_k = Reduction(ring, gk_ref, tk_ref, pk2_ref, sk2_ref, gwk_ref, True, False)
    send_v = Reduction(ring, gv_ref, tv_ref, pv_ref, sv_ref, gwv_ref, True, False)
    send_small = Reduction(ring, gs_ref, ts_ref, ps_ref, ss_ref, gsm_ref, True, False)
    feed = (send_expand, send_reduce)

    chunks = [0] + order
    written = []

    def feed_stack(c):
        for part in feed:
            part.gather_plane(c)
            if c >= 1:
                part.stack([c])

    def store(items):
        for part, at in items:
            part.finish()
            written.append(local(boxes[at], results[at]))

    for c in chunks:
        chain("f", None, " " + str(c), [
            calls(feed, "pair", c), calls(feed, "phase_one", c), calls(feed, "phase_two", c), partial(feed_stack, c),
        ])
    plan.add("f4", ["f3 " + str(c) for c in chunks], calls(feed, "settle"))
    plan.add("f5", ["f4"], calls(feed, "to_plane_two"))
    plan.add("f6", ["f5"], calls(feed, "to_twin"))
    plan.add("f7", ["f6"], partial(store, ((send_expand, 3), (send_reduce, 4))))

    def climb(part):
        part.gather_plane(part.all)
        part.stack()

    for name, part, at in (("q", send_q, 5), ("k", send_k, 6), ("v", send_v, 7), ("s", send_small, 8)):
        chain(name, None, "", [
            partial(part.pair, part.all), partial(part.plane, part.all), partial(climb, part), part.settle,
            part.to_plane, part.to_twin, partial(store, ((part, at),)),
        ])
    chain("o", None, "", [
        partial(send_out.pair, send_out.all), partial(send_out.plane, send_out.all), partial(climb, send_out),
        send_out.settle, send_out.to_twin, partial(store, ((send_out, 2),)),
    ])
    closing = Tail(ring, tail_ref, (tail_pair, tail_plane, tail_stack))

    def tail_last():
        gtail_ref[...] = closing.collect(2)
        written.append(local(gtail_ref, results[9]))

    chain("t", None, "", [
        partial(closing.start, 0), partial(closing.collect, 0), partial(closing.collect, 1), tail_last,
    ])

    acc_ref, dh2_ref = one_ref, two_ref
    hid_ref, dpre_ref = raw_ref.at[:, 0:cw], raw_ref.at[:, width : width + cw]
    datt_ref = raw_ref.at[:, 2 * width : 3 * width]
    half = rows // 2
    sums_ref[...] = jnp.zeros_like(sums_ref)
    arrive(get_bias)
    for at_chunk, c in enumerate(chunks):
        point = "chunk" + str(at_chunk)
        if at_chunk >= 1:
            plan.need("g3 " + str(c))
        bias = eb_ref[c, 0:1, :]
        folded = jnp.zeros((8, cw), f32)
        we, wr = we_ref[c], wr_ref[c, 0:cw, :]
        for k in range(2):
            at = slice(k * half, (k + 1) * half)
            pre = dot(h2_ref[at, :], we) + bias
            dh = dot(cot_ref[at, :], wr, 1, 1)
            gauss = jnp.exp(pre * pre * -0.5)
            t = 1.0 / (1.0 + (0.3275911 * 0.7071067811865476) * jnp.abs(pre))
            poly = t * (0.127414796 + t * (-0.142248368 + t * (0.7107068705 + t * (-0.7265760135 + t * 0.5307027145))))
            tail = poly * gauss
            cdf = jnp.where(pre >= 0, 1.0 - tail, tail)
            hid_ref[at, :] = (pre * cdf).astype(bf16)
            dpre = ((cdf + pre * gauss * 0.3989422804014327) * dh).astype(bf16)
            dpre_ref[at, :] = dpre
            folded = folded + fold_rows(dpre.astype(f32))
            plan.at(point + "ab"[k])
        sums_ref[OUT_EXPAND_BIAS + lax.rem(ring.me + c, depth), :, 0:cw] = folded
        ge_ref[c] = dot(h2_ref[...], dpre_ref[...], 0, 0).astype(bf16)
        plan.at(point + "c")
        gr_ref[c, 0:cw] = dot(hid_ref[...], cot_ref[...], 0, 0).astype(bf16)
        if gr_ref.shape[1] > cw:
            gr_ref[c, cw:] = jnp.zeros((gr_ref.shape[1] - cw, width), bf16)
        plan.need("f0 " + str(c))
        plan.at(point + "e")
        out = dot(hid_ref[...], wr)
        back = dot(dpre_ref[...], we, 1, 1)
        for tile in range(4):
            if at_chunk == 0:
                acc_ref[tile] = out[:, lane(tile)]
                dh2_ref[tile] = back[:, lane(tile)]
            else:
                acc_ref[tile] += out[:, lane(tile)]
                dh2_ref[tile] += back[:, lane(tile)]
        plan.at(point + "f")

    def finish(k, carry):
        at = block_at(k)
        x2 = wide(x2_ref, at)
        y_ref[at, :] = (x2 + wide(acc_ref, at) + row(ROW_REDUCE_BIAS)).astype(bf16)
        unit, scale = normalise(x2)
        grad = wide(dh2_ref, at)
        dy = cot_ref[at, :].astype(f32)
        dx2 = dy + normalise_back(grad, gain_two, unit, scale)
        put_wide(x2_ref, at, dx2)
        low = dx2.astype(bf16)
        datt_ref[at, :] = low
        return (
            carry[0] + fold_rows(grad * unit), carry[1] + fold_rows(grad),
            carry[2] + fold_rows(low.astype(f32)), carry[3] + fold_rows(dy),
        )

    zero = jnp.zeros((8, width), f32)
    sums = lax.fori_loop(0, steps // 2, finish, (zero,) * 4)
    plan.at("finish0")
    sums = lax.fori_loop(steps // 2, steps, finish, sums)
    plan.at("finish1")
    written.append(local(y_ref, results[0]))
    for r, total in zip((OUT_LATE_GAIN, OUT_LATE_SHIFT, OUT_OUT_BIAS, OUT_REDUCE_BIAS), sums):
        sums_ref[r] = total
    grad_out = dot(att_ref[...], datt_ref[...], 0, 0).astype(bf16)
    for t in range(depth):
        go_ref[t, 0:share, :] = grad_out[t * share : (t + 1) * share, :]
        if go_ref.shape[1] > share:
            go_ref[t, share:, :] = jnp.zeros((go_ref.shape[1] - share, width), bf16)
    plan.need("o0")
    plan.at("gwo")
    grad_att = dot(datt_ref[...], whole_out, 1, 1).astype(bf16).astype(f32)
    da_ref, dq_ref, dk_ref, dv_ref = fac_ref, one_ref, two_ref, three_ref
    put_wide(da_ref, every, grad_att)
    plan.at("datt")

    def image_back(g, carry):
        batch = [g * some + u for u in range(some)]
        scaled = pair_mask * SCALE
        for b in batch:
            per_image(da_ref, dai_ref, b)
        for b in batch:
            for t in range(4):
                dq = dot(dai_ref[b, :, lane(t)], ctx_ref[b, t], 1, 1) * SCALE
                dq_ref[t, here(b), :] = dq[0:tokens]
        for b in batch:
            for t in range(4):
                full = dot(qi_ref[b, :, lane(t)], dai_ref[b, :, lane(t)], 0, 0)
                ctx_ref[b, t] = (full * scaled).astype(bf16)
        for b in batch:
            for t in range(4):
                dk = dot(vi_ref[b, :, lane(t)], ctx_ref[b, t], 1, 1)
                dk_ref[t, here(b), :] = dk[0:tokens]
                dv = dot(ki_ref[b, :, lane(t)], ctx_ref[b, t])
                dv_ref[t, here(b), :] = dv[0:tokens]
        return carry

    for g in range(4):
        lax.fori_loop(g, g + 1, image_back, 0)
        plan.at("back" + str(g))

    def split(tile, carry):
        bias_q = jnp.zeros((images, LANES), f32)
        bias_all = jnp.zeros((images, LANES), f32)
        dot_sum = jnp.zeros((images, LANES), f32)
        for n in range(tokens):
            grad = da_ref[tile, token(n), :]
            dq = (dq_ref[tile, token(n), :] + grad * conv_ref[tile, token(n), :]).astype(bf16)
            raw_ref[token(n), lane(tile)] = dq
            bias_q = bias_q + dq.astype(f32)
            dc = grad * q_ref[tile, token(n), :]
            da_ref[tile, token(n), :] = dc
            if n > 0:
                bias_all = bias_all + dc
            dot_sum = dot_sum + dk_ref[tile, token(n), :] * ks_ref[tile, token(n), :]
        for n in range(tokens):
            soft = ks_ref[tile, token(n), :]
            raw_ref[token(n), lane(tile + 4)] = (soft * (dk_ref[tile, token(n), :] - dot_sum)).astype(bf16)
        sums_ref[OUT_BIAS_Q, :, lane(tile)] = fold_rows(bias_q)
        sums_ref[OUT_BIAS_ALL, :, lane(tile)] = fold_rows(bias_all)
        return carry

    lax.fori_loop(0, 4, split, 0)
    plan.at("split")

    def grad_joint(target, part):
        grad = dot(h1_ref[...], raw_ref[:, part * width : (part + 1) * width], 0, 0).astype(bf16)
        for t in range(depth):
            target[t, 0:share, :] = grad[t * share : (t + 1) * share, :]
            if target.shape[1] > share:
                target[t, share:, :] = jnp.zeros((target.shape[1] - share, width), bf16)

    grad_joint(gq_ref, 0)
    plan.need("q0")
    plan.at("gq")
    grad_joint(gk_ref, 1)
    plan.need("k0")
    plan.at("gk")
    def values_back(tile, extent):
        first = dv_ref[tile, token(0), :].astype(bf16)
        raw_ref[token(0), lane(tile + 8)] = first
        bias_v = [first.astype(f32)]

        def emit(i, total):
            for j in range(GRID):
                here = cell_rows(images, i * GRID + j)
                dv = (dv_ref[tile, here, :] + total[j]).astype(bf16)
                raw_ref[here, lane(tile + 8)] = dv
                bias_v[0] = bias_v[0] + dv.astype(f32)

        depthwise_rows(
            partial(grid_row, da_ref, tile, images), lambda ab: prm(full_tap(extent, *ab), tile),
            extent, True, emit,
        )
        sums_ref[OUT_BIAS_V, :, lane(tile)] = fold_rows(bias_v[0])

    narrow_tiles(values_back)
    plan.at("values0")
    for tile in (2, 3):
        values_back(tile, 7)
        plan.at("values" + str(tile - 1))
    grad_joint(gv_ref, 2)
    plan.need("v0")
    plan.at("gv")

    def tap_grads(tile, extent):
        extra = (GRID - extent) // 2

        def emit_tap(a, b, total):
            sums_ref[OUT_KERNEL_ALL + (a + extra) * GRID + b + extra, :, lane(tile)] = fold_rows(total)

        kernel_grads(
            partial(grid_row, da_ref, tile, images), partial(grid_row, v_ref, tile, images), extent, emit_tap
        )

    narrow_tiles(tap_grads)
    plan.at("taps0")
    for tile in (2, 3):
        tap_grads(tile, 7)
        plan.at("taps" + str(tile - 1))
    small = jnp.sum(sums_ref[...], axis=1).astype(bf16)
    for t in range(depth):
        gs_ref[t] = jnp.zeros(gs_ref.shape[1:], bf16)
        gs_ref[t, 0 : small.shape[0], :] = small[:, t * share : (t + 1) * share]
    plan.need("s0")
    plan.at("small")

    dh1_ref = one_ref
    for k in range(2):
        at = slice(k * half, (k + 1) * half)
        put_wide(dh1_ref, at, dot(raw_ref[at, :], wj_ref[...], 1, 1))
        plan.at("dh1" + "ab"[k])

    def back(k, carry):
        at = block_at(k)
        grad = wide(dh1_ref, at)
        unit, scale = normalise(wide(x1_ref, at))
        put_wide(da_ref, at, wide(x2_ref, at) + normalise_back(grad, gain_one, unit, scale))
        return carry[0] + fold_rows(grad * unit), carry[1] + fold_rows(grad)

    sums = lax.fori_loop(0, steps // 2, back, (zero, zero))
    plan.at("normback0")
    sums = lax.fori_loop(steps // 2, steps, back, sums)
    plan.at("normback1")
    last_ref[...] = jnp.zeros_like(last_ref)
    last_ref[TAIL_EARLY_GAIN] = sums[0]
    last_ref[TAIL_EARLY_SHIFT] = sums[1]

    def position_back(tile, carry):
        bias = [jnp.zeros((images, LANES), f32)]
        dx_ref[0:images, lane(tile)] = da_ref[tile, 0:images, :].astype(bf16)

        def emit(i, total):
            here = grid_row(da_ref, tile, images, i)
            for j in range(GRID):
                dx_ref[cell_rows(images, i * GRID + j), lane(tile)] = (here[j] + total[j]).astype(bf16)
                bias[0] = bias[0] + here[j]

        depthwise_rows(
            partial(grid_row, da_ref, tile, images),
            lambda ab: prm(ROW_POS_KERNEL + ab[0] * 3 + ab[1], tile),
            3, True, emit,
        )
        last_ref[TAIL_POS_BIAS, :, lane(tile)] = fold_rows(bias[0])

        def emit_tap(a, b, total):
            last_ref[TAIL_POS_KERNEL + a * 3 + b, :, lane(tile)] = fold_rows(total)

        kernel_grads(partial(grid_row, da_ref, tile, images), partial(x_row, tile), 3, emit_tap)
        return carry

    lax.fori_loop(0, 2, position_back, 0)
    plan.at("pos1")
    lax.fori_loop(2, 4, position_back, 0)
    plan.at("pos3")
    written.append(local(dx_ref, results[1]))
    tail_ref[0] = jnp.sum(last_ref[...], axis=1).astype(bf16)
    plan.need("t0")
    plan.at("tail")
    plan.at("end")
    plan.rest()
    for copy in written:
        copy.wait()
    for copy in ring.sent:
        copy.wait_send()


def write_out(
    y_ref, dx_ref, gwo_ref, gwe_ref, gwr_ref, gwq_ref, gwk_ref, gwv_ref, gsm_ref, gtail_ref,
    y_out, dx_out, pk_out, pb_out, eg_out, es_out, jw_out, jb_out, sk_out, sb_out, mk_out, mb_out, lk_out, lb_out,
    ow_out, ob_out, lg_out, ls_out, ew_out, eb_out, rw_out, rb_out,
    y_box, dx_box, q_box, k_box, v_box, o_box, e_box, r_box, jw_box, ow_box, ew_box, rw_box,
    small_ref, in_sems, out_sems,
):
    depth, share = gsm_ref.shape[0], gsm_ref.shape[2]
    width = y_ref.shape[1]
    joint = [
        (ref, box, jw_box.at[:, part * width : (part + 1) * width], jw_out.at[:, part * width : (part + 1) * width])
        for part, (ref, box) in enumerate(((gwq_ref, q_box), (gwk_ref, k_box), (gwv_ref, v_box)))
    ]
    flat = [
        (gwe_ref, e_box, ew_box, ew_out), (gwr_ref, r_box, rw_box, rw_out), (gwo_ref, o_box, ow_box, ow_out),
    ]
    plain = [(y_ref, y_box, y_out), (dx_ref, dx_box, dx_out)]
    sources = [(ref, box) for ref, box, _, _ in flat + joint] + [(ref, box) for ref, box, _ in plain]
    loads = [pltpu.make_async_copy(ref, box, in_sems.at[at]) for at, (ref, box) in enumerate(sources)]
    for load in loads:
        load.start()
    stores = []

    def store(box, out):
        stores.append(pltpu.make_async_copy(box, out, out_sems.at[len(stores)]))
        stores[-1].start()

    for at, (_, box, wide_box, out) in enumerate(flat):
        loads[at].wait()
        wide_box[...] = box[0 : wide_box.shape[0], :].astype(f32)
        store(wide_box, out)
    for at, (_, box, wide_box, out) in enumerate(joint):
        loads[3 + at].wait()
        for t in range(depth):
            wide_box[t * share : (t + 1) * share, :] = box[t, 0:share, :].astype(f32)
        store(wide_box, out)
    for at, (_, box, out) in enumerate(plain):
        loads[6 + at].wait()
        store(box, out)
    for t in range(depth):
        small_ref[:, t * share : (t + 1) * share] = gsm_ref[t].astype(f32)
    for at, out in (
        (OUT_OUT_BIAS, ob_out), (OUT_LATE_GAIN, lg_out), (OUT_LATE_SHIFT, ls_out), (OUT_REDUCE_BIAS, rb_out),
    ):
        out[...] = small_ref[at, :]
    jb_out[0:width] = small_ref[OUT_BIAS_Q, :]
    jb_out[width:] = small_ref[OUT_BIAS_V, :]
    cw = eb_out.shape[0]
    mine = small_ref[pl.ds(OUT_EXPAND_BIAS + lax.axis_index("tensor"), 1), 0:cw]
    eb_out[...] = mine.reshape(cw)
    first_lane = 0
    for kernel_out, bias_out in ((sk_out, sb_out), (mk_out, mb_out), (lk_out, lb_out)):
        extent, count = kernel_out.shape[0], kernel_out.shape[2]
        span = slice(first_lane, first_lane + count)
        bias_out[...] = small_ref[OUT_BIAS_ALL, span]
        for a in range(extent):
            at = full_tap(extent, a, 0) - ROW_KERNEL_ALL + OUT_KERNEL_ALL
            kernel_out[a] = small_ref[at : at + extent, span]
        first_lane += count
    for a in range(3):
        at = TAIL_POS_KERNEL + 3 * a
        pk_out[a] = gtail_ref[at : at + 3, :]
    for at, out in ((TAIL_POS_BIAS, pb_out), (TAIL_EARLY_GAIN, eg_out), (TAIL_EARLY_SHIFT, es_out)):
        out[...] = gtail_ref[at, :]
    for copy in stores:
        copy.wait()


def per_device(
    block_input, position_kernel, position_bias, early_gain, early_shift, joint_weight, joint_bias,
    small_kernel, small_bias, middle_kernel, middle_bias, large_kernel, large_bias,
    output_weight, output_bias, late_gain, late_shift, expand_weight, expand_bias,
    reduce_weight, reduce_bias, cotangent,
):
    images, tokens, width = block_input.shape
    rows = images * tokens
    depth, copies_of = lax.axis_size("tensor"), lax.axis_size("dp")
    planes = math.gcd(copies_of // 2, 4)
    pieces = 2 * planes
    share, cw = width // depth, expand_weight.shape[1]
    unit = 16 * pieces
    sum_rows = padded(OUT_EXPAND_BIAS + depth, 16)
    shapes = [
        (padded(share, unit), width), (padded(width, unit), cw), (padded(cw, unit), width),
        (padded(share, unit), width), (padded(share, unit), width), (padded(share, unit), width),
        (padded(sum_rows, unit), share),
    ]
    near, far = planes - 1, depth - 1
    copies = far + 3 * far * (2 + near) + 2 * depth * 6 + 5 * (1 + near) + 7 * far + 4 * far + 5 * near + 2 * 5 + 7
    copies += 1 + near + far
    fill = lambda array, count: jnp.pad(array, ((0, count - array.shape[0]), (0, 0)))
    vmem = lambda shape, dtype=bf16: pltpu.VMEM(shape, dtype)
    tail = (TAIL_ROWS, width)
    flat = lambda array: array.transpose(1, 0, 2).reshape(rows, width)
    given = (
        flat(block_input), flat(cotangent), joint_weight, position_kernel, position_bias, early_gain, early_shift,
        joint_bias, small_kernel, small_bias, middle_kernel, middle_bias, large_kernel, large_bias, output_bias,
        late_gain, late_shift, reduce_bias, expand_bias,
        fill(output_weight, shapes[0][0]), fill(expand_weight, shapes[1][0]), fill(reduce_weight, shapes[2][0]),
    )
    outs = [
        ((rows, width), bf16), ((rows, width), bf16),
        (shapes[0], bf16), (shapes[1], bf16), (shapes[2], bf16),
        ((depth,) + shapes[3], bf16), ((depth,) + shapes[4], bf16), ((depth,) + shapes[5], bf16),
        ((depth,) + shapes[6], bf16), (tail, f32),
    ]
    scratch = (
        [vmem(array.shape) for array in given[:19]] + [vmem(shape, dtype) for shape, dtype in outs] +
        [vmem((PARAM_ROWS, width), f32)]
        + [vmem((4, rows, LANES), f32)] * 10
        + [vmem((rows, width))] * 3 + [vmem((rows, 3 * width))]
        + [vmem((images, PAD_TOK, width))] * 4 + [vmem((images, 4, LANES, LANES))]
        + [vmem((sum_rows, 8, width), f32), vmem((TAIL_ROWS, 8, width), f32)]
        + [vmem((depth,) + shape) for shape in shapes[:3]] + [vmem((depth, 8, cw), f32)]
        + [vmem((depth,) + shape) for shape in shapes]
        + [vmem((depth, r // 2, w)) for r, w in shapes]
        + [vmem((near, depth, r // pieces, w)) for r, w in shapes[:1] + shapes[3:]]
        + [
            vmem(shape)
            for r, w in shapes[1:3]
            for shape in (
                (depth, 2, r // pieces, w // 2), (depth, 2 * r // pieces, w // 2),
                (depth, r // pieces, w // 2), (depth, r // pieces, w // 2),
            )
        ]
        + [vmem((far, r // pieces, w)) for r, w in shapes]
        + [vmem((3,) + tail), vmem((1,) + tail), vmem((near,) + tail), vmem((far,) + tail)]
        + [pltpu.SemaphoreType.DMA((copies,))] * 2 + [pltpu.SemaphoreType.DMA((32,))]
    )
    anywhere = pl.BlockSpec(memory_space=pl.ANY)
    inside = pl.BlockSpec(memory_space=pltpu.VMEM)
    made = pl.pallas_call(
        partial(whole_block, images, tokens, planes, depth),
        out_shape=[jax.ShapeDtypeStruct(shape, dtype) for shape, dtype in outs],
        in_specs=[anywhere] * 22,
        out_specs=[anywhere] * len(outs),
        scratch_shapes=scratch,
        compiler_params=pltpu.CompilerParams(
            vmem_limit_bytes=VMEM_BYTES, collective_id=1, has_side_effects=True
        ),
    )(*given)
    if copies_of > pieces:
        groups = [list(range(first, copies_of, pieces)) for first in range(pieces)]
        made = list(made[:2]) + list(lax.psum(tuple(made[2:]), "dp", axis_index_groups=groups))
    like = lambda array: jax.ShapeDtypeStruct(array.shape, f32)
    results = pl.pallas_call(
        write_out,
        out_shape=[jax.ShapeDtypeStruct((rows, width), bf16)] * 2 + [
            like(array) for array in (
                position_kernel, position_bias, early_gain, early_shift, joint_weight, joint_bias,
                small_kernel, small_bias, middle_kernel, middle_bias, large_kernel, large_bias,
                output_weight, output_bias, late_gain, late_shift, expand_weight, expand_bias,
                reduce_weight, reduce_bias,
            )
        ],
        in_specs=[anywhere] * 8 + [inside] * 2,
        out_specs=[
            anywhere if at in (0, 1, 6, 14, 18, 20) else inside for at in range(22)
        ],
        scratch_shapes=[vmem((rows, width))] * 2
        + [vmem((depth,) + shape) for shape in shapes[3:6]] + [vmem(shape) for shape in shapes[:3]]
        + [vmem(array.shape, f32) for array in (joint_weight, output_weight, expand_weight, reduce_weight)]
        + [vmem((shapes[6][0], width), f32), pltpu.SemaphoreType.DMA((8,)), pltpu.SemaphoreType.DMA((8,))],
        compiler_params=pltpu.CompilerParams(vmem_limit_bytes=VMEM_BYTES),
    )(*made)
    image_form = lambda array: array.reshape(tokens, images, width).transpose(1, 0, 2)
    return (image_form(results[0]), image_form(results[1])) + tuple(results[2:])


def solution(mesh):
    images = P(("dp", "tensor"), None, None)
    in_specs = (images,) + (P(),) * 12 + (
        P("tensor", None), P(), P(), P(), P(None, "tensor"), P("tensor"), P("tensor", None), P(), images,
    )
    out_specs = (images, images) + (P(),) * 12 + (
        P("tensor", None), P(), P(), P(), P(None, "tensor"), P("tensor"), P("tensor", None), P(),
    )
    return jax.shard_map(per_device, mesh=mesh, in_specs=in_specs, out_specs=out_specs, check_vma=False)
```
